32 devices in a mesh: section: 2 (over y), dp: 16 (over z, x, core).
Axes of the slice: x: 2, y: 2, z: 4, core: 2. Of those that a mesh axis runs over, the one named last changes fastest.
Arguments:
- tokens: bfloat16 [8192, 768], P('dp'), may hold values from -6 to 6
- cotangent: bfloat16 [8192, 768], P('dp'), may hold values from -6 to 6
- segments: int32 [32, 256], P('dp'), may hold values from 0 to 3, never falling along the last dimension, each value on 1 to 128 neighbouring positions
- chosen: int32 [32, 32], P('dp'), may hold values from 0 to 255, as said below
- router: float32 [768], replicated, may hold values from -0.21875 to 0.21875
- norm_gains: float32 [2, 2, 768], P('section'), may hold values from 0.1 to 1.9
- attn_in: bfloat16 [2, 3, 768, 768], P('section', None, 'dp'), may hold values from -0.21875 to 0.21875
- attn_out: bfloat16 [2, 768, 768], P('section', 'dp'), may hold values from -0.875 to 0.875
- ff_up: bfloat16 [2, 768, 3072], P('section', 'dp'), may hold values from -0.21875 to 0.21875
- ff_down: bfloat16 [2, 3072, 768], P('section', 'dp'), may hold values from -0.109375 to 0.109375
Outputs:
- ends: bfloat16 [2, 8192, 768], P('section', 'dp')
- router_grad: float32 [768], replicated
- gain_grad: float32 [2, 2, 768], P('section', None, 'dp')
- attn_in_grad: float32 [2, 3, 768, 768], P('section', None, 'dp')
- attn_out_grad: float32 [2, 768, 768], P('section', 'dp')
- up_grad: float32 [2, 768, 3072], P('section', 'dp')
- down_grad: float32 [2, 3072, 768], P('section', 'dp')
The draws below stay inside these ranges and needn't reach their ends.
Inputs may be any that keep to these rules, and one draw needn't show every extreme that they name: `chosen`: each row holds 32 distinct positions of its sequence in increasing order.
All inputs are finite; a program needn't handle non-finite values.
Results may differ from the reference program's by a relative error of at most 0.014.
Values may be sent and summed in bfloat16 or wider, within the bound.
No kernel may reach another device: no remote copies, remote signals or barrier semaphores. Data moves between devices by JAX's collectives and lax.ppermute only.
A program may use at most 384 MiB of HBM per device.

```python
import math
import jax
import jax.numpy as jnp
import numpy as np
from jax import lax

D = 768
HEAD_DIM = 64
FF = 3072
SEQ_LEN = 256
KEEP = 32
SEQS = 32
TOKENS = 8192


def draw_chosen(key, part):
    key = jax.random.fold_in(key, 11)
    keys = jax.random.split(key, SEQS)

    def one_row(row_key):
        order = jax.random.permutation(row_key, SEQ_LEN)
        marked = (order < KEEP).astype(jnp.int32)
        return jnp.argsort(1 - marked, stable=True)[:KEEP].astype(jnp.int32)
    return jax.vmap(one_row)(keys)


def level_of(rng, extent, pieces, least, top_value):
    level = 1.0
    for dim, shards_of in pieces:
        draws = jax.random.uniform(jax.random.fold_in(jax.random.fold_in(rng, 6), dim), (shards_of,), jnp.float32, least / len(pieces), top_value / len(pieces))
        level = level * jnp.repeat(jnp.exp(draws), extent[dim] // shards_of).reshape((-1,) + (1,) * (len(extent) - 1 - dim))
    return level


def profile(number_of, total, most, slope):
    loads = [(1 << 20) // math.isqrt(rank ** slope) + 1 for rank in range(2, number_of + 1)]
    rest, given = total - most - (number_of - 1), [1] * (number_of - 1)
    while rest > 0:
        free = [i for i in range(number_of - 1) if given[i] < most]
        whole, left = sum([loads[i] for i in free]), rest
        for i in free:
            more = min(most - given[i], max(1, left * loads[i] // whole), rest)
            given[i] = given[i] + more
            rest = rest - more
    return np.array([most] + given)


def ragged(rng, amount, total, bound, slope):
    if amount == 2:
        one = jax.random.randint(rng, (), max(1, total - bound), min(bound, total - 1) + 1)
        return jnp.stack([one, total - one])
    sizes = jnp.asarray(profile(amount, total, bound, slope), jnp.int32)
    couples = (amount - 1) // 2
    donor, receiver = sizes[1:1 + 2 * couples:2], sizes[2:2 + 2 * couples:2]
    margin = jnp.minimum(donor - 1, bound - receiver)
    moved = jax.random.randint(jax.random.fold_in(rng, 1), (couples,), 0, 1 << 20) % (margin + 1)
    sizes = sizes.at[1:1 + 2 * couples:2].set(donor - moved).at[2:2 + 2 * couples:2].set(receiver + moved)
    return sizes[jax.random.permutation(jax.random.fold_in(rng, 2), amount)]


def normal_values(key, dims, scale, bound, cuts=(), held_as=jnp.bfloat16):
    entries = jax.random.normal(key, dims, jnp.float32) * scale
    if len(cuts) > 0:
        entries = level_of(key, dims, cuts, -0.22, 0.18) * entries
    return jnp.clip(entries, min=-bound, max=bound).astype(held_as)


def setup_inputs(seed: int = 0) -> dict:
    seeds = jax.random.split(jax.random.key(seed), 11)
    return {
        "tokens": normal_values(seeds[0], (TOKENS, D), 1.0, 6.0, ((0, 16),)),
        "cotangent": normal_values(seeds[1], (TOKENS, D), 1.0, 6.0, ((0, 16),)),
        "segments": jax.vmap(lambda own: jnp.searchsorted(jnp.cumsum(ragged(own, max(SEQ_LEN // 64, 4), SEQ_LEN, SEQ_LEN // 2, 2)), jnp.arange(SEQ_LEN), side="right"))(jax.random.split(seeds[2], SEQS)).reshape((SEQS, SEQ_LEN)).astype(jnp.int32),
        "chosen": draw_chosen(jax.random.fold_in(seeds[10], 71), 0),
        "router": normal_values(seeds[4], (D,), D ** -0.5, 0.21875, (), jnp.float32),
        "norm_gains": jnp.clip(1.0 + 0.18 * jax.random.normal(seeds[5], (2, 2, D), jnp.float32), 0.1, 1.9),
        "attn_in": normal_values(seeds[6], (2, 3, D, D), D ** -0.5, 0.21875, ((0, 2), (2, 16))),
        "attn_out": normal_values(seeds[7], (2, D, D), (D // 16) ** -0.5, 0.875, ((0, 2), (1, 16))),
        "ff_up": normal_values(seeds[8], (2, D, FF), D ** -0.5, 0.21875, ((0, 2), (1, 16))),
        "ff_down": normal_values(seeds[9], (2, FF, D), FF ** -0.5, 0.109375, ((0, 2), (1, 16))),
    }


EXACT_GELU_FLAG = lax.Precision.HIGHEST
EPSILON = 1e-05
MASKED = -1e+30

@jax.custom_vjp
def low(v):
    return lax.optimization_barrier(v.astype(jnp.bfloat16)).astype(jnp.float32)

@jax.custom_vjp
def reduced_backward_pass(v):
    return v

def low_keep(v):
    return (low(v), None)

def low_pass(kept, grad):
    return (grad,)

def back_keep(v):
    return (v, None)

def back_low(kept, grad):
    return (low(grad),)
low.defvjp(low_keep, low_pass)
reduced_backward_pass.defvjp(back_keep, back_low)

def both_ways(value):
    return low(reduced_backward_pass(value))

def normalize(rows, gain):
    return rows * lax.rsqrt(lax.optimization_barrier(jnp.mean(rows * rows, axis=-1, keepdims=True)) + EPSILON) * gain

def segment_mask(segment):
    order = jnp.arange(segment.shape[1], dtype=jnp.int32)
    return (order[None, :, None] >= order[None, None, :]) & (segment[:, :, None] == segment[:, None, :])

def block(rows, mask, gains, w_in, w_out, w_up, w_down):
    batch, count, width = rows.shape
    heads = width // HEAD_DIM
    pre_one = low(normalize(rows, gains[0]))
    projected = jnp.einsum('srd,cde->csre', pre_one, w_in, precision=EXACT_GELU_FLAG)
    query = both_ways(projected[0]).reshape(batch, count, heads, HEAD_DIM)
    keyed = both_ways(projected[1]).reshape(batch, count, heads, HEAD_DIM)
    valued = both_ways(projected[2]).reshape(batch, count, heads, HEAD_DIM)
    scores = reduced_backward_pass(jnp.einsum('sqhd,skhd->shqk', query, keyed, precision=EXACT_GELU_FLAG) * HEAD_DIM ** (-0.5))
    scores = jnp.where(mask[:, None], scores, MASKED)
    powers = jnp.exp(scores - lax.optimization_barrier(jnp.max(scores, axis=-1, keepdims=True)))
    chances = low(powers / lax.optimization_barrier(jnp.sum(powers, axis=-1, keepdims=True)))
    mixed = both_ways(jnp.einsum('shqk,skhd->sqhd', chances, valued, precision=EXACT_GELU_FLAG).reshape(batch, count, width))
    attended = reduced_backward_pass(jnp.einsum('srd,de->sre', mixed, w_out, precision=EXACT_GELU_FLAG))
    intermediate_hidden = rows + attended
    pre_two = low(normalize(intermediate_hidden, gains[1]))
    upped = reduced_backward_pass(jnp.einsum('srd,df->srf', pre_two, w_up, precision=EXACT_GELU_FLAG))
    hidden = low(jax.nn.gelu(upped, approximate=False))
    return attended + reduced_backward_pass(jnp.einsum('srf,fd->srd', hidden, w_down, precision=EXACT_GELU_FLAG))

def layer_pair(value_rows, segment, picked_at, router, gains, w_in, w_out, w_up, w_down):
    count = value_rows.shape[1]
    one_hot_selection = (picked_at[:, :, None] == jnp.arange(count, dtype=jnp.int32)[None, None, :]).astype(jnp.float32)
    routed_token_rows = jnp.einsum('wgo,woq->wgq', one_hot_selection, value_rows, precision=EXACT_GELU_FLAG)
    gate = jax.nn.sigmoid(jnp.einsum('skd,d->sk', routed_token_rows, router, precision=EXACT_GELU_FLAG))
    chosen_seg = jnp.take_along_axis(segment, picked_at, axis=1)
    branch = block(routed_token_rows, segment_mask(chosen_seg), gains[0], w_in[0], w_out[0], w_up[0], w_down[0])
    residual_update = low(gate[..., None] * branch)
    intermediate_hidden = reduced_backward_pass(value_rows + jnp.einsum('eub,euz->ebz', one_hot_selection, residual_update, precision=EXACT_GELU_FLAG))
    return intermediate_hidden + block(intermediate_hidden, segment_mask(segment), gains[1], w_in[1], w_out[1], w_up[1], w_down[1])

def reference(tokens, cotangent, segments, chosen, router, norm_gains, attn_in, attn_out, ff_up, ff_down):
    batch = segments.shape[0]
    count = segments.shape[1]
    width = tokens.shape[1]
    group = 8 if batch % 8 == 0 else 1
    inputs = tokens.astype(jnp.float32).reshape(batch // group, group, count, width)
    seg_groups = segments.reshape(batch // group, group, count)
    pick_groups = chosen.reshape(batch // group, group, -1)

    def forward(value_rows, router_w, gains, w_in, w_out, w_up, w_down):

        def one_group(packed):
            rows, segment, picked_at = packed
            return layer_pair(rows, segment, picked_at, router_w, gains, w_in, w_out, w_up, w_down)
        return lax.map(jax.checkpoint(one_group), (value_rows, seg_groups, pick_groups))
    result, pullback = jax.vjp(forward, inputs, router, norm_gains, attn_in.astype(jnp.float32), attn_out.astype(jnp.float32), ff_up.astype(jnp.float32), ff_down.astype(jnp.float32))
    grads = pullback(cotangent.astype(jnp.float32).reshape(result.shape))
    ends = jnp.stack([grads[0].reshape(-1, width), result.reshape(-1, width)]).astype(jnp.bfloat16)
    return (ends, grads[1], grads[2], grads[3], grads[4], grads[5], grads[6])
```

```python
import jax
import jax.numpy as jnp
from jax import lax
from jax.sharding import PartitionSpec as P

HEAD_DIM = 64
EXACT = lax.Precision.HIGHEST
EPSILON = 1e-05
MASKED = -1e30
BF = jnp.bfloat16
F32 = jnp.float32


def move(value, pairs):
    return lax.ppermute(value, "dp", pairs)


def routes(n):
    depth = n // 4
    across = [(i, i ^ 2) for i in range(n)]
    beside = [(i, i ^ 1) for i in range(n)]
    shifts = [[(i, ((i // 4 + k) % depth) * 4 + i % 4) for i in range(n)] for k in range(depth)]
    return depth, across, beside, shifts


def after(value, token):
    return lax.optimization_barrier((value, token))[0]


def gather_parts(parts):
    n = lax.axis_size("dp")
    if n != 16:
        return [lax.all_gather(part, "dp", axis=0) for part in parts]
    depth, across, beside, shifts = routes(n)
    me = lax.axis_index("dp")
    own_across = [move(part, across) for part in parts]
    wholes, last = [], None
    for part, crossed in zip(parts, own_across):
        column = [part]
        for k in range(1, depth):
            source = part if last is None else after(part, last[k - 1][:1, :1])
            column.append(move(source, shifts[k]))
        last = column[1:]
        plane = [column, [crossed] + [move(held, across) for held in last]]
        whole = jnp.zeros((n,) + part.shape, part.dtype)
        for j in range(2):
            for k in range(depth):
                held = plane[j][k]
                for c, piece in ((0, held), (1, move(held, beside))):
                    origin = ((me // 4 - k) % depth) * 4 + ((me % 4) ^ (2 * j + c))
                    whole = lax.dynamic_update_index_in_dim(whole, piece, origin, 0)
        wholes.append(whole)
    return wholes


def scatter_sum(whole):
    n = lax.axis_size("dp")
    if n != 16:
        return lax.psum_scatter(whole.astype(F32), "dp", scatter_dimension=0, tiled=False)
    depth, across, beside, shifts = routes(n)
    me = lax.axis_index("dp")

    def piece(k, j, c):
        target = ((me // 4 + k) % depth) * 4 + ((me % 4) ^ (2 * j + c))
        return lax.dynamic_index_in_dim(whole, target, 0, keepdims=False)

    order = list(range(1, depth)) + [0]
    came = {}
    for j in (1, 0):
        got = move(jnp.stack([piece(k, j, 1) for k in order]), beside)
        for slot, k in enumerate(order):
            came[k, j] = got[slot].astype(F32) + piece(k, j, 0).astype(F32)
    crossed = {k: move(came[k, 1].astype(BF), across) for k in order}
    here = {k: came[k, 0] + crossed[k].astype(F32) for k in order}
    total = here[0]
    arrived = [move(here[k].astype(BF), shifts[k]) for k in range(1, depth)]
    for value in arrived:
        total = total + value.astype(F32)
    return total


def normalize(rows, gain):
    inverse = lax.rsqrt(jnp.mean(rows * rows, axis=-1, keepdims=True) + EPSILON)
    normed = rows * inverse
    return (normed, inverse, normed * gain)


def norm_back(upstream, normed, inverse, gain):
    scaled = upstream * gain
    d_gain = jnp.sum(upstream * normed, axis=(0, 1))
    d_rows = inverse * (scaled - normed * jnp.mean(scaled * normed, axis=-1, keepdims=True))
    return (d_rows, d_gain)


def gelu_exact(value):
    return jax.nn.gelu(value, approximate=False)


def segment_mask(segment):
    order = lax.iota(jnp.int32, segment.shape[1])
    return (order[None, :, None] >= order[None, None, :]) & (
        segment[:, :, None] == segment[:, None, :]
    )


def masked_scores(query, keyed, mask):
    scores = jnp.einsum(
        "sqhd,skhd->shqk", query, keyed, preferred_element_type=F32
    ) * HEAD_DIM ** (-0.5)
    return jnp.where(mask[:, None], scores, MASKED)


def block_forward(rows, mask, gains, w_in, w_out, w_up, w_down):
    batch, count, width = rows.shape
    normed_one, inverse_one, pre_one = normalize(rows, gains[0])
    act_one = pre_one.astype(BF)
    projected = jnp.einsum("srd,cde->csre", act_one, w_in, preferred_element_type=F32).astype(BF)
    heads = projected.reshape(3, batch, count, width // HEAD_DIM, HEAD_DIM)
    scores = masked_scores(heads[0], heads[1], mask)
    top = jnp.max(scores, axis=-1, keepdims=True)
    powers = jnp.exp(scores - top)
    total = jnp.sum(powers, axis=-1, keepdims=True)
    chances = (powers / total).astype(BF)
    mixed = jnp.einsum("shqk,skhd->sqhd", chances, heads[2], preferred_element_type=F32)
    mixed = mixed.reshape(batch, count, width).astype(BF)
    attended = jnp.einsum("srd,de->sre", mixed, w_out, preferred_element_type=F32)
    middle = rows + attended
    normed_two, inverse_two, pre_two = normalize(middle, gains[1])
    act_two = pre_two.astype(BF)
    upped = jnp.einsum("srd,df->srf", act_two, w_up, preferred_element_type=F32)
    hidden = gelu_exact(upped).astype(BF)
    branch = attended + jnp.einsum("srf,fd->srd", hidden, w_down, preferred_element_type=F32)
    log_total = top + jnp.log(total)
    first = (normed_one, inverse_one, act_one, heads, log_total, mixed)
    second = (normed_two, inverse_two, act_two, upped, hidden)
    return branch, first, second


def feed_back(grad_branch, second, gain, w_up, w_down):
    normed_two, inverse_two, act_two, upped, hidden = second
    d_out = grad_branch.astype(BF)
    d_hidden = jnp.einsum("srd,fd->srf", d_out, w_down, preferred_element_type=F32)
    d_upped = jax.vjp(gelu_exact, upped)[1](d_hidden)[0].astype(BF)
    d_act_two = jnp.einsum("srf,df->srd", d_upped, w_up, preferred_element_type=F32)
    d_middle, g_gain = norm_back(d_act_two, normed_two, inverse_two, gain)
    return d_middle, g_gain, (hidden, d_out, act_two, d_upped)


def attend_back(grad_branch, d_middle, mask, first, gain, w_in, w_out):
    normed_one, inverse_one, act_one, heads, log_total, mixed = first
    batch, count, width = grad_branch.shape
    d_attended = (grad_branch + d_middle).astype(BF)
    d_mixed = jnp.einsum("sre,de->srd", d_attended, w_out, preferred_element_type=F32).astype(BF)
    d_mixed = d_mixed.reshape(batch, count, width // HEAD_DIM, HEAD_DIM)
    chances = jnp.exp(masked_scores(heads[0], heads[1], mask) - log_total)
    d_chances = jnp.einsum("sqhd,skhd->shqk", d_mixed, heads[2], preferred_element_type=F32)
    d_value = jnp.einsum("shqk,sqhd->skhd", chances.astype(BF), d_mixed, preferred_element_type=F32)
    d_scores = chances * (d_chances - jnp.sum(chances * d_chances, axis=-1, keepdims=True))
    d_scores = d_scores.astype(BF)
    factor = HEAD_DIM ** (-0.5)
    d_query = jnp.einsum("shqk,skhd->sqhd", d_scores, heads[1], preferred_element_type=F32) * factor
    d_key = jnp.einsum("shqk,sqhd->skhd", d_scores, heads[0], preferred_element_type=F32) * factor
    d_projected = jnp.stack([d_query, d_key, d_value]).reshape(3, batch, count, width).astype(BF)
    d_act_one = jnp.einsum("csre,cde->srd", d_projected, w_in, preferred_element_type=F32)
    d_rows, g_gain = norm_back(d_act_one, normed_one, inverse_one, gain)
    return d_rows + d_middle, g_gain, (mixed, d_attended, act_one, d_projected)


def feed_grads(kept):
    hidden, d_out, act_two, d_upped = kept
    g_down = jnp.einsum("srf,srd->fd", hidden, d_out, preferred_element_type=F32)
    g_up = jnp.einsum("srd,srf->df", act_two, d_upped, preferred_element_type=F32)
    return g_up.astype(BF), g_down.astype(BF)


def attend_grads(kept):
    mixed, d_attended, act_one, d_projected = kept
    g_out = jnp.einsum("srd,sre->de", mixed, d_attended, preferred_element_type=F32)
    g_in = jnp.einsum("srd,csre->cde", act_one, d_projected, preferred_element_type=F32)
    return g_in.astype(BF), g_out.astype(BF)


def zeros_of(work, *operands):
    return jax.tree.map(lambda leaf: jnp.zeros(leaf.shape, leaf.dtype), jax.eval_shape(work, *operands))


def on_section(active, work, *operands):
    return lax.cond(active, work, lambda *inner: zeros_of(work, *inner), *operands)


def body(
    tokens, cotangent, segments, chosen, router, norm_gains, attn_in, attn_out, ff_up, ff_down
):
    n = lax.axis_size("dp")
    routed = lax.axis_index("section") == 0
    batch, length = segments.shape
    width = tokens.shape[1]
    kept = chosen.shape[1]
    rows_in, rows_down, ff = attn_in.shape[2], ff_down.shape[1], ff_up.shape[2]
    blocks = ff // width
    gains = norm_gains[0]

    first_part = jnp.concatenate([attn_in[0].reshape(-1, width), attn_out[0]])
    second_part = jnp.concatenate([ff_up[0][:, b * width:(b + 1) * width] for b in range(blocks)])
    whole_first, whole_second, whole_down = gather_parts([first_part, second_part, ff_down[0]])
    whole_first = whole_first.reshape(n, 4, rows_in, width).transpose(1, 0, 2, 3).reshape(4, -1, width)
    w_in, w_out = whole_first[:3], whole_first[3]
    w_up = whole_second.reshape(n, blocks, rows_in, width).transpose(0, 2, 1, 3).reshape(-1, ff)
    w_down = whole_down.reshape(-1, width)

    inputs = tokens.reshape(batch, length, width)
    upstream = cotangent.reshape(batch, length, width)
    picks = (chosen[:, :, None] == lax.iota(jnp.int32, length)[None, None, :]).astype(BF)

    def pick(rows):
        return jnp.einsum("wgo,woq->wgq", picks, rows, preferred_element_type=F32)

    def put(rows):
        return jnp.einsum("wgo,wgq->woq", picks, rows, preferred_element_type=F32)

    pick_mask = segment_mask(jnp.take_along_axis(segments, chosen, axis=1))

    def routed_forward():
        rows = pick(inputs)
        gate = jax.nn.sigmoid(jnp.einsum("skd,d->sk", rows, router, precision=EXACT))
        branch, first, second = block_forward(rows, pick_mask, gains, w_in, w_out, w_up, w_down)
        return (gate[..., None] * branch).astype(BF), (rows, gate, branch, first, second)

    delta, stash = on_section(routed, routed_forward)
    arrived = lax.ppermute(delta, "section", [(0, 1)])

    def dense_work():
        base = inputs.astype(F32) + put(arrived)
        mask = segment_mask(segments)
        branch, first, second = block_forward(base, mask, gains, w_in, w_out, w_up, w_down)
        grad = upstream.astype(F32)
        d_middle, g_two, kept_feed = feed_back(grad, second, gains[1], w_up, w_down)
        d_rows, g_one, kept_attend = attend_back(grad, d_middle, mask, first, gains[0], w_in, w_out)
        back = (grad + d_rows).astype(BF)
        result = (base + branch).astype(BF)
        return result, back, pick(back).astype(BF), jnp.stack([g_one, g_two]), kept_feed, kept_attend

    result, back, back_rows, g_gains, kept_feed, kept_attend = on_section(
        jnp.logical_not(routed), dense_work
    )
    d_delta = lax.ppermute(back_rows, "section", [(1, 0)])
    returned = lax.ppermute(back, "section", [(1, 0)])

    def routed_feed():
        rows, gate, branch, first, second = stash
        grad = gate[..., None] * d_delta.astype(F32)
        d_middle, g_two, kept_here = feed_back(grad, second, gains[1], w_up, w_down)
        return feed_grads(kept_here) + (d_middle, g_two)

    def dense_feed():
        return feed_grads(kept_feed) + (jnp.zeros((batch, kept, width), F32), g_gains[1])

    g_up, g_down, d_middle, g_two = lax.cond(routed, routed_feed, dense_feed)

    def routed_attend():
        rows, gate, branch, first, second = stash
        d_rows_out = d_delta.astype(F32)
        d_logit = jnp.sum(d_rows_out * branch, axis=-1) * gate * (1.0 - gate)
        d_picked, g_one, kept_here = attend_back(
            gate[..., None] * d_rows_out, d_middle, pick_mask, first, gains[0], w_in, w_out
        )
        d_picked = d_picked + d_logit[..., None] * router
        g_router = jnp.einsum("sk,skd->d", d_logit, rows, precision=EXACT)
        return attend_grads(kept_here) + (g_one, g_router, d_picked)

    def dense_attend():
        return attend_grads(kept_attend) + (
            g_gains[0], jnp.zeros_like(router), jnp.zeros((batch, kept, width), F32)
        )

    g_in, g_out, g_one, g_router, d_picked = lax.cond(routed, routed_attend, dense_attend)

    down_grad = scatter_sum(g_down.reshape(n, rows_down, width))
    up_grad = scatter_sum(
        g_up.reshape(n, rows_in, blocks, width).transpose(0, 2, 1, 3).reshape(n, -1, width)
    )
    attend_sum = scatter_sum(
        jnp.concatenate([g_in, g_out[None]])
        .reshape(4, n, rows_in, width).transpose(1, 0, 2, 3).reshape(n, -1, width)
    )
    gain_grad = lax.psum_scatter(jnp.stack([g_one, g_two]), "dp", scatter_dimension=1, tiled=True)
    router_grad = lax.psum(g_router, ("section", "dp"))

    spread = jnp.einsum("wgo,wgq->woq", picks.astype(F32), d_picked, precision=EXACT)
    first_rows = (returned.astype(F32) + spread).astype(BF)
    ends = jnp.where(routed, first_rows, result).reshape(1, -1, width)
    attend_sum = attend_sum.reshape(4, rows_in, width)
    up_grad = up_grad.reshape(blocks, rows_in, width).transpose(1, 0, 2).reshape(rows_in, ff)
    return (
        ends, router_grad, gain_grad[None], attend_sum[:3][None], attend_sum[3][None],
        up_grad[None], down_grad[None],
    )


def solution(mesh):
    return jax.shard_map(
        body,
        mesh=mesh,
        in_specs=(
            P("dp", None),
            P("dp", None),
            P("dp", None),
            P("dp", None),
            P(),
            P("section", None, None),
            P("section", None, "dp", None),
            P("section", "dp", None),
            P("section", "dp", None),
            P("section", "dp", None),
        ),
        out_specs=(
            P("section", "dp", None),
            P(),
            P("section", None, "dp"),
            P("section", None, "dp", None),
            P("section", "dp", None),
            P("section", "dp", None),
            P("section", "dp", None),
        ),
        check_vma=False,
    )
```

```python
import functools

import jax
import jax.numpy as jnp
from jax import lax
from jax.experimental import pallas as pl
from jax.experimental.pallas import tpu as pltpu
from jax.sharding import PartitionSpec as P

HEAD_DIM = 64
LANES = 2 * HEAD_DIM
EPSILON = 1e-05
MASKED = -1e30
BF = jnp.bfloat16
F32 = jnp.float32
VMEM_BYTES = 60 * 1024 * 1024
STRIP = 16
CODES = 16


def move(value, pairs):
    return lax.ppermute(value, "dp", pairs)


def device_at(spot, core, depth):
    return 4 * spot + core if spot < depth else 4 * (2 * depth - 1 - spot) + 2 + core


def routes(n):
    depth = n // 4
    ring = 2 * depth

    def turned(by):
        return [
            (device_at(r, c, depth), device_at((r + by) % ring, c, depth))
            for r in range(ring) for c in range(2)
        ]

    return turned(1), turned(-1), [(i, i ^ 1) for i in range(n)]


def hops(depth, far):
    return (depth, depth - 1) if far == 0 else (depth - 1, depth)


def slots(depth, far):
    ahead, behind = hops(depth, far)
    distances = [0] + list(range(1, ahead + 1)) + [-d for d in range(1, behind + 1)]
    return [(d, c) for d in distances for c in range(2)]


def ways(depth, far):
    sign = 1 if far == 0 else -1
    found = []
    for d in range(depth, 0, -1):
        found += [sign * d, -sign * (d - 1)]
    return found


def after(value, token):
    return lax.optimization_barrier((value, token))[0]


def sliced(n):
    return n == 16


FAR = (0, 1, 0)
ORDER = sorted(((s, p) for s in range(1, 5) for p in range(3)), key=lambda sp: sp[0] + (0, 0.1, 0.2)[sp[1]])


class Gather:
    def __init__(self, parts, n):
        self.n = n
        self.forward, self.backward, self.beside = routes(n)
        self.held = [{(0, 0): part, (0, 1): move(part, self.beside)} for part in parts]

    def step(self, p, s, token=None):
        ahead, behind = hops(self.n // 4, FAR[p])
        held = self.held[p]
        for sign, limit, way in ((1, ahead, self.forward), (-1, behind, self.backward)):
            if s <= limit:
                source = held[sign * (s - 1), 0]
                if token is not None:
                    source = after(source, token)
                came = move(source, way)
                held[sign * s, 0] = came
                held[sign * s, 1] = move(came, self.beside)

    def shards(self, p):
        return [self.held[p][slot] for slot in slots(self.n // 4, FAR[p])]


class Sum:
    def __init__(self, pieces, n, far):
        self.depth = n // 4
        forward, backward, self.beside = routes(n)
        self.main, self.minor = (forward, backward) if far == 0 else (backward, forward)
        self.own = pieces[0], pieces[2]
        self.got = move(pieces[1], self.beside), move(pieces[3], self.beside)
        self.came = [None, None]
        self.left = None

    def term(self, e, came):
        half, at = divmod(e, self.depth)
        found = self.own[half][at].astype(F32) + self.got[half][at].astype(F32)
        return found if came is None else found + came.astype(F32)

    def step(self, s):
        sent = []
        for i, way in enumerate((self.main, self.minor)):
            if s + i < self.depth:
                value = self.term(2 * s + i, self.came[i]).astype(BF)
                sent.append(value)
                self.came[i] = move(value, way)
        return sent

    def total(self):
        return self.term(2 * self.depth - 1, self.came[0]) + self.came[1].astype(F32)


def scatter_plain(whole):
    return lax.psum_scatter(whole.astype(F32), "dp", scatter_dimension=0, tiled=False)


def sum_small(value, n):
    way = 1
    while way < n:
        value = value + move(value, [(i, i ^ way) for i in range(n)])
        way = 2 * way
    return value


def dot(a, b):
    return jnp.dot(a, b, preferred_element_type=F32)


def dot_t(a, b):
    return lax.dot_general(a, b, (((1,), (1,)), ((), ())), preferred_element_type=F32)


def t_dot(a, b):
    return lax.dot_general(a, b, (((0,), (0,)), ((), ())), preferred_element_type=F32)


def spot_of(me, depth):
    return jnp.where((me // 2) % 2 == 0, me // 4, 2 * depth - 1 - me // 4)


def device_on(me, distance, core, depth):
    spot = lax.rem(spot_of(me, depth) + (2 * depth + distance), 2 * depth)
    base = jnp.where(spot < depth, 4 * spot, 4 * (2 * depth - 1 - spot) + 2)
    return base + ((me % 2) ^ core)


def fetch(refs, hold, sem, me, far):
    if len(refs) == 1:
        pltpu.make_async_copy(refs[0], hold, sem).start()
        return
    depth = len(refs) // 4
    count = hold.shape[1] // len(refs)
    for (distance, core), ref in zip(slots(depth, far), refs):
        origin = device_on(me, -distance, core, depth)
        spot = pl.ds(pl.multiple_of(origin * count, 16), count)
        for q in range(hold.shape[0]):
            pltpu.make_async_copy(ref.at[pl.ds(q * count, count)], hold.at[q, spot], sem).start()


def ready(hold, sem):
    pltpu.make_async_copy(hold, hold, sem).wait()


def emit(value_ref, outs, me, q, far):
    if len(outs) == 1:
        outs[0][q] = value_ref[...].astype(BF)
        return
    depth = outs[0].shape[0]
    count = value_ref.shape[0] // (4 * depth)
    for e, distance in enumerate(ways(depth, far)):
        half, at = divmod(e, depth)
        for core in range(2):
            target = device_on(me, distance, core, depth)
            rows = value_ref[pl.ds(pl.multiple_of(target * count, 16), count), :]
            outs[2 * half + core][at, q * count:(q + 1) * count, :] = rows.astype(BF)


def inverse_of(rows):
    return lax.rsqrt(jnp.mean(rows * rows, axis=-1, keepdims=True) + EPSILON)


def norm_back(upstream, normed, inverse, gain):
    scaled = upstream * gain
    d_gain = jnp.sum(upstream * normed, axis=0, keepdims=True)
    d_rows = inverse * (scaled - normed * jnp.mean(scaled * normed, axis=-1, keepdims=True))
    return d_rows, d_gain


def normal_parts(value):
    size = jnp.abs(value)
    fall = jnp.exp(value * value * -0.5)
    t = 1.0 / (1.0 + size * (0.3275911 * 0.7071067811865476))
    poly = t * (
        0.127414796
        + t * (-0.142248368 + t * (0.7107068705 + t * (-0.7265760135 + t * 0.5307027145)))
    )
    tail = poly * fall
    whole = jnp.where(value < 0.0, tail, 1.0 - tail)
    return whole, value * fall * 0.3989422804014327


def left_lanes(rows):
    return lax.broadcasted_iota(jnp.int32, (rows, LANES), 1) < HEAD_DIM


def two_heads(value):
    left = left_lanes(value.shape[0])
    zero = jnp.zeros_like(value)
    return jnp.concatenate([jnp.where(left, value, zero), jnp.where(left, zero, value)], axis=0)


def one_row(value):
    half = value.shape[0] // 2
    return jnp.where(left_lanes(half), value[:half], value[half:])


def bias_of(same):
    shape = same.shape
    order = lax.broadcasted_iota(jnp.int32, shape, 0) >= lax.broadcasted_iota(jnp.int32, shape, 1)
    return jnp.where(order & (same > 0.5), 0.0, MASKED).astype(F32)


def hot_rows(line, count):
    return (lax.broadcasted_iota(jnp.int32, (count, line.shape[1]), 0) == line).astype(BF)


def attend(query, keyed, valued, bias):
    size = query.shape[0]
    scores = dot_t(two_heads(query) * jnp.asarray(HEAD_DIM ** -0.5, BF), keyed)
    scores = (scores.reshape(2, size, size) + bias[None]).reshape(2 * size, size)
    powers = jnp.exp(scores - jnp.max(scores, axis=-1, keepdims=True))
    chances = (powers * (1.0 / jnp.sum(powers, axis=-1, keepdims=True))).astype(BF)
    return one_row(dot(chances, valued)).astype(BF), chances


def attend_back(query, keyed, valued, mixed, chances, d_mixed):
    both = two_heads(d_mixed)
    d_chances = dot_t(both, valued)
    overlap = jnp.sum(two_heads(d_mixed.astype(F32) * mixed.astype(F32)), axis=-1, keepdims=True)
    d_scores = (chances.astype(F32) * (d_chances - overlap)).astype(BF)
    factor = HEAD_DIM ** -0.5
    d_query = one_row(dot(d_scores, keyed)) * factor
    d_key = t_dot(d_scores, two_heads(query)) * factor
    d_value = t_dot(chances, both)
    return d_query.astype(BF), d_key.astype(BF), d_value.astype(BF)


def lanes_of(p):
    return pl.ds(pl.multiple_of(p * LANES, LANES), LANES)


def routed_attend_kernel(slot_count, batch, place, *refs):
    first = refs[:slot_count]
    (tokens, spots, codes, router, gains,
     rows_o, gate_o, z_o, act_one_o, heads_o, chances_o, mixed_o, act_two_o,
     w_first, sems) = refs[slot_count:]
    me = place[0]
    fetch(first, w_first, sems.at[0], me, FAR[0])
    hot = hot_rows(spots[...], tokens.shape[0])
    rows = t_dot(hot, tokens[...])
    rows_o[...] = rows
    gate_o[...] = jax.nn.sigmoid(jnp.sum(rows * router[...], axis=-1, keepdims=True))
    act = (rows * inverse_of(rows) * gains[0:1]).astype(BF)
    act_one_o[...] = act
    member = dot(hot_rows(codes[...], CODES * batch), hot).astype(BF)
    bias = bias_of(t_dot(member, member))
    ready(w_first, sems.at[0])
    heads = [dot(act, w_first[c]).astype(BF) for c in range(3)]
    for c in range(3):
        heads_o[c] = heads[c]
    found = []
    for p in range(rows.shape[1] // LANES):
        lanes = slice(p * LANES, (p + 1) * LANES)
        mixed, chances = attend(heads[0][:, lanes], heads[1][:, lanes], heads[2][:, lanes], bias)
        found.append(mixed)
        chances_o[p] = chances.astype(F32)
    mixed = jnp.concatenate(found, axis=1)
    mixed_o[...] = mixed
    z = dot(mixed, w_first[3])
    z_o[...] = z
    middle = rows + z
    act_two_o[...] = (middle * inverse_of(middle) * gains[1:2]).astype(BF)


def routed_up_kernel(slot_count, place, *refs):
    up = refs[:slot_count]
    act_two, hidden_o, slope_o, w_up, sems = refs[slot_count:]
    fetch(up, w_up, sems.at[0], place[0], FAR[1])
    ready(w_up, sems.at[0])
    width = act_two.shape[1]
    for b in range(w_up.shape[0]):
        lanes = slice(b * width, (b + 1) * width)
        upped = dot(act_two[...], w_up[b])
        whole, dense = normal_parts(upped)
        hidden_o[:, lanes] = (upped * whole).astype(BF)
        slope_o[:, lanes] = whole + dense


def routed_down_kernel(slot_count, place, *refs):
    down = refs[:slot_count]
    hidden, z, gate, branch_o, delta_o, w_down, sems = refs[slot_count:]
    fetch(down, w_down, sems.at[0], place[0], FAR[2])
    ready(w_down, sems.at[0])
    branch = z[...] + dot(hidden[...], w_down[0])
    branch_o[...] = branch
    delta_o[...] = (gate[...] * branch).astype(BF)


def routed_outer_kernel(out_count, place, d_delta, gate, hidden, *refs):
    downs_o, g_down = refs[:out_count], refs[out_count]
    width = d_delta.shape[1]
    d_out = (gate[...] * d_delta[...].astype(F32)).astype(BF)
    for b in range(hidden.shape[1] // width):
        lanes = slice(b * width, (b + 1) * width)
        g_down[lanes] = t_dot(hidden[:, lanes], d_out)
    emit(g_down, downs_o, place[0], 0, FAR[2])


def routed_feed_kernel(slot_count, out_count, place, *refs):
    up, down = refs[:slot_count], refs[slot_count:2 * slot_count]
    (d_delta, gate, rows, z, act_two, slope, gains) = refs[2 * slot_count:2 * slot_count + 7]
    refs = refs[2 * slot_count + 7:]
    ups_o = refs[:out_count]
    d_middle_o, gain_o, w_up, w_down, g_up, sems = refs[out_count:]
    me = place[0]
    fetch(down, w_down, sems.at[0], me, FAR[2])
    fetch(up, w_up, sems.at[1], me, FAR[1])
    width = rows.shape[1]
    d_out = (gate[...] * d_delta[...].astype(F32)).astype(BF)
    ready(w_down, sems.at[0])
    ready(w_up, sems.at[1])
    d_act = jnp.zeros(rows.shape, F32)
    for b in range(w_up.shape[0]):
        lanes = slice(b * width, (b + 1) * width)
        d_hidden = dot_t(d_out, w_down[0, lanes])
        d_upped = (d_hidden * slope[:, lanes]).astype(BF)
        d_act = d_act + dot_t(d_upped, w_up[b])
        g_up[...] = t_dot(act_two[...], d_upped)
        emit(g_up, ups_o, me, b, FAR[1])
    middle = rows[...] + z[...]
    inverse = inverse_of(middle)
    d_middle_o[...], gain_o[...] = norm_back(d_act, middle * inverse, inverse, gains[1:2])


def routed_attend_back_kernel(slot_count, out_count, place, *refs):
    first = refs[:slot_count]
    (d_delta, gate, d_middle, branch, rows, act_one, heads, chances, mixed, router, gains) = refs[
        slot_count:slot_count + 11]
    refs = refs[slot_count + 11:]
    outs = refs[:out_count]
    gain_o, router_o, d_picked_o, w_first, grad, sems = refs[out_count:]
    me = place[0]
    fetch(first, w_first, sems.at[0], me, FAR[0])
    gated = gate[...]
    upstream = d_delta[...].astype(F32)
    d_logit = jnp.sum(upstream * branch[...], axis=-1, keepdims=True) * gated * (1.0 - gated)
    router_o[...] = jnp.sum(d_logit * rows[...], axis=0, keepdims=True)
    d_z = (gated * upstream + d_middle[...]).astype(BF)
    grad[...] = t_dot(mixed[...], d_z)
    emit(grad, outs, me, 3, FAR[0])
    ready(w_first, sems.at[0])
    d_mixed = dot_t(d_z, w_first[3]).astype(BF)
    held = [heads[c] for c in range(3)]
    blend = mixed[...]
    found = []
    for p in range(rows.shape[1] // LANES):
        lanes = slice(p * LANES, (p + 1) * LANES)
        found.append(attend_back(
            held[0][:, lanes], held[1][:, lanes], held[2][:, lanes], blend[:, lanes],
            chances[p].astype(BF), d_mixed[:, lanes],
        ))
    d_heads = [jnp.concatenate([one[c] for one in found], axis=1) for c in range(3)]
    d_act = jnp.zeros(rows.shape, F32)
    for c in range(3):
        d_act = d_act + dot_t(d_heads[c], w_first[c])
        grad[...] = t_dot(act_one[...], d_heads[c])
        emit(grad, outs, me, c, FAR[0])
    held = rows[...]
    inverse = inverse_of(held)
    d_rows, gain_o[...] = norm_back(d_act, held * inverse, inverse, gains[0:1])
    d_picked_o[...] = d_rows + d_middle[...] + d_logit * router[...]


def dense_kernel(slot_count, place, *refs):
    first = refs[:slot_count]
    up = refs[slot_count:2 * slot_count]
    down = refs[2 * slot_count:3 * slot_count]
    (tokens, cotangent, delta, spots, segments, gains,
     result_o, back_o, picked_o, gain_o,
     act_one_o, d_heads_o, mixed_o, d_z_o, act_two_o, hidden_o, d_upped_o,
     w_first, w_up, w_down, rows, z, heads, chances, bias, fed, d_act, upped, d_hidden, d_mixed,
     act_one, d_heads, mixed, d_z, act_two, hidden, d_upped, sems, out_sems) = refs[3 * slot_count:]
    me = place[0]
    fetch(first, w_first, sems.at[0], me, FAR[0])
    fetch(up, w_up, sems.at[1], me, FAR[1])
    fetch(down, w_down, sems.at[2], me, FAR[2])
    batch, length, _ = bias.shape
    width = tokens.shape[1]
    pairs = width // LANES
    blocks = w_up.shape[0]
    parts = [slice(s * length, (s + 1) * length) for s in range(batch)]
    copies = [
        pltpu.make_async_copy(held, out, out_sems.at[i])
        for i, (held, out) in enumerate((
            (act_one, act_one_o), (d_heads, d_heads_o), (mixed, mixed_o), (d_z, d_z_o),
            (act_two, act_two_o), (hidden, hidden_o), (d_upped, d_upped_o),
        ))
    ]

    hot = hot_rows(spots[...], tokens.shape[0])
    for s, part in enumerate(parts):
        held = tokens[part].astype(F32) + dot(hot[part], delta[...])
        rows[part] = held
        act_one[part] = (held * inverse_of(held) * gains[0:1]).astype(BF)
        member = hot_rows(segments[:, part], CODES)
        bias[s] = bias_of(t_dot(member, member))
    copies[0].start()
    ready(w_first, sems.at[0])
    for c in range(3):
        for part in parts:
            heads[c, part] = dot(act_one[part], w_first[c]).astype(BF)

    def forward(p, carry):
        lanes = lanes_of(p)
        for s, part in enumerate(parts):
            mixed[part, lanes], chances[s, p] = attend(
                heads[0, part, lanes], heads[1, part, lanes], heads[2, part, lanes], bias[s]
            )
        return carry

    lax.fori_loop(0, pairs, forward, 0)
    copies[2].start()
    for part in parts:
        attended = dot(mixed[part], w_first[3])
        z[part] = attended
        middle = rows[part] + attended
        act_two[part] = (middle * inverse_of(middle) * gains[1:2]).astype(BF)
    copies[4].start()
    ready(w_up, sems.at[1])
    ready(w_down, sems.at[2])
    fed[...] = jnp.zeros(fed.shape, F32)
    d_act[...] = jnp.zeros(d_act.shape, F32)

    def feed(b, carry):
        lanes = pl.ds(pl.multiple_of(b * width, width), width)
        for s, part in enumerate(parts):
            upped[...] = dot(act_two[part], w_up[b])
            d_hidden[...] = dot_t(cotangent[part], w_down[0, lanes])

            def strip(r, inner):
                spot = pl.ds(pl.multiple_of(r * STRIP, STRIP), STRIP)
                there = pl.ds(pl.multiple_of(s * length + r * STRIP, STRIP), STRIP)
                for half in range(2):
                    cut = slice(half * width // 2, (half + 1) * width // 2)
                    out = pl.ds(pl.multiple_of(b * width + half * width // 2, LANES), width // 2)
                    value = upped[spot, cut]
                    whole, dense = normal_parts(value)
                    hidden[there, out] = (value * whole).astype(BF)
                    d_upped[there, out] = (d_hidden[spot, cut] * (whole + dense)).astype(BF)
                return inner

            lax.fori_loop(0, length // STRIP, strip, 0)
            fed[part] += dot(hidden[part, lanes], w_down[0, lanes])
            d_act[part] += dot_t(d_upped[part, lanes], w_up[b])
        return carry

    lax.fori_loop(0, blocks, feed, 0)
    copies[5].start()
    copies[6].start()
    gain = jnp.zeros((1, width), F32)
    for part in parts:
        result_o[part] = (rows[part] + z[part] + fed[part]).astype(BF)
        middle = rows[part] + z[part]
        inverse = inverse_of(middle)
        d_middle, more = norm_back(d_act[part], middle * inverse, inverse, gains[1:2])
        gain = gain + more
        held = cotangent[part].astype(F32) + d_middle
        d_act[part] = held
        d_z[part] = held.astype(BF)
        d_mixed[part] = dot_t(held.astype(BF), w_first[3]).astype(BF)
    gain_o[1:2] = gain
    copies[3].start()

    def backward(p, carry):
        lanes = lanes_of(p)
        for s, part in enumerate(parts):
            d_heads[0, part, lanes], d_heads[1, part, lanes], d_heads[2, part, lanes] = attend_back(
                heads[0, part, lanes], heads[1, part, lanes], heads[2, part, lanes],
                mixed[part, lanes], chances[s, p], d_mixed[part, lanes],
            )
        return carry

    lax.fori_loop(0, pairs, backward, 0)
    copies[1].start()
    gain = jnp.zeros((1, width), F32)
    for s, part in enumerate(parts):
        d_first = dot_t(d_heads[0, part], w_first[0])
        d_first = d_first + dot_t(d_heads[1, part], w_first[1])
        d_first = d_first + dot_t(d_heads[2, part], w_first[2])
        held = rows[part]
        inverse = inverse_of(held)
        d_rows, more = norm_back(d_first, held * inverse, inverse, gains[0:1])
        gain = gain + more
        back_o[part] = (d_act[part] + d_rows).astype(BF)
    picked_o[...] = t_dot(hot, back_o[...]).astype(BF)
    gain_o[0:1] = gain
    for copy in copies:
        copy.wait()


def dense_outer_kernel(out_count, place, hidden, d_out, *refs):
    downs_o, g_down = refs[:out_count], refs[out_count]
    width = d_out.shape[1]
    for b in range(hidden.shape[1] // width):
        lanes = slice(b * width, (b + 1) * width)
        g_down[lanes] = t_dot(hidden[:, lanes], d_out[...])
    emit(g_down, downs_o, place[0], 0, FAR[2])


def dense_feed_kernel(out_count, place, act_two, d_upped, *refs):
    ups_o, g_up = refs[:out_count], refs[out_count]
    width = act_two.shape[1]
    for b in range(d_upped.shape[1] // width):
        lanes = slice(b * width, (b + 1) * width)
        g_up[...] = t_dot(act_two[...], d_upped[:, lanes])
        emit(g_up, ups_o, place[0], b, FAR[1])


def dense_attend_kernel(out_count, place, mixed, d_z, act_one, d_heads, *refs):
    outs, grad = refs[:out_count], refs[out_count]
    me = place[0]
    grad[...] = t_dot(mixed[...], d_z[...])
    emit(grad, outs, me, 3, FAR[0])
    for c in range(3):
        grad[...] = t_dot(act_one[...], d_heads[c])
        emit(grad, outs, me, c, FAR[0])


def call(kernel, inputs, anywhere, outs, scratch, flops, anywhere_outs=0):
    vmem = pl.BlockSpec(memory_space=pltpu.VMEM)
    hbm = pl.BlockSpec(memory_space=pltpu.HBM)
    specs = [pl.BlockSpec(memory_space=pltpu.SMEM)] + [hbm] * anywhere
    specs = specs + [vmem] * (len(inputs) - len(specs))
    moved = sum(v.size * v.dtype.itemsize for v in inputs) + sum(
        o.size * jnp.dtype(o.dtype).itemsize for o in outs)
    return tuple(pl.pallas_call(
        kernel,
        out_shape=outs,
        in_specs=specs,
        out_specs=[vmem] * (len(outs) - anywhere_outs) + [hbm] * anywhere_outs,
        scratch_shapes=scratch,
        compiler_params=pltpu.CompilerParams(vmem_limit_bytes=VMEM_BYTES),
        cost_estimate=pl.CostEstimate(flops=flops, bytes_accessed=moved, transcendentals=0),
    )(*inputs))


def body(
    tokens, cotangent, segments, chosen, router, norm_gains, attn_in, attn_out, ff_up, ff_down
):
    n = lax.axis_size("dp")
    routed = lax.axis_index("section") == 0
    place = lax.axis_index("dp").astype(jnp.int32).reshape(1)
    batch, length = segments.shape
    width = tokens.shape[1]
    kept = chosen.shape[1]
    rows_in, rows_down, ff = attn_in.shape[2], ff_down.shape[1], ff_up.shape[2]
    blocks, pairs = ff // width, width // LANES
    picked, count = batch * kept, batch * length
    gains = norm_gains[0]
    router_row = router[None]

    def shape(*dims, dtype=F32):
        return jax.ShapeDtypeStruct(dims, dtype)

    def hold(*dims, dtype=F32):
        return pltpu.VMEM(dims, dtype)

    first_part = jnp.concatenate([attn_in[0].reshape(-1, width), attn_out[0]])
    up_part = jnp.concatenate([ff_up[0][:, b * width:(b + 1) * width] for b in range(blocks)])
    parts = [first_part, up_part, ff_down[0]]
    order = lax.iota(jnp.int32, batch)[:, None]
    spots = (chosen + order * length).reshape(1, picked)
    lines = segments.reshape(1, count)
    codes = (segments + order * CODES).reshape(1, count)
    if sliced(n):
        gather = Gather(parts, n)
        for s, p in ORDER:
            gather.step(p, s, (spots, lines, codes) if s == 2 else None)
        first, up, down = (gather.shards(p) for p in range(3))
    else:
        first, up, down = (lax.all_gather(part, "dp", axis=0) for part in parts)
    if sliced(n):
        block = shape(n // 4, 4 * rows_in, width, dtype=BF)
        first_outs, up_outs, down_outs = [block] * 4, [block] * 4, [block] * 4
    else:
        first = [first.reshape(n, 4, rows_in, width).transpose(1, 0, 2, 3).reshape(4, width, width)]
        up = [up.reshape(n, blocks, rows_in, width).transpose(1, 0, 2, 3).reshape(blocks, width, width)]
        down = [down.reshape(1, ff, width)]
        first_outs = [shape(4, width, width, dtype=BF)]
        up_outs = [shape(blocks, width, width, dtype=BF)]
        down_outs = [shape(1, ff, width, dtype=BF)]
    number, out_number = len(first), len(first_outs)
    w_first, w_up, w_down = (
        hold(4, width, width, dtype=BF), hold(blocks, width, width, dtype=BF), hold(1, ff, width, dtype=BF))

    (rows, gate, z, act_one, heads, chances, mixed, act_two) = call(
        functools.partial(routed_attend_kernel, number, batch),
        [place, *first, tokens, spots, codes, router_row, gains],
        number,
        [shape(picked, width), shape(picked, 1), shape(picked, width), shape(picked, width, dtype=BF),
         shape(3, picked, width, dtype=BF), shape(pairs, 2 * picked, picked),
         shape(picked, width, dtype=BF), shape(picked, width, dtype=BF)],
        [w_first, pltpu.SemaphoreType.DMA((1,))],
        8 * picked * width * width,
    )
    hidden, slope = call(
        functools.partial(routed_up_kernel, number),
        [place, *up, act_two],
        number,
        [shape(picked, ff, dtype=BF), shape(picked, ff)],
        [w_up, pltpu.SemaphoreType.DMA((1,))],
        2 * picked * width * ff,
    )
    branch, delta = call(
        functools.partial(routed_down_kernel, number),
        [place, *down, hidden, z, gate],
        number,
        [shape(picked, width), shape(picked, width, dtype=BF)],
        [w_down, pltpu.SemaphoreType.DMA((1,))],
        2 * picked * width * ff,
    )
    arrived = lax.ppermute(delta, "section", [(0, 1)])

    (result, back, back_rows, dense_gains, *dense_kept) = call(
        functools.partial(dense_kernel, number),
        [place, *first, *up, *down, tokens, cotangent, arrived, spots, lines, gains],
        3 * number,
        [shape(count, width, dtype=BF), shape(count, width, dtype=BF), shape(picked, width, dtype=BF),
         shape(2, width),
         shape(count, width, dtype=BF), shape(3, count, width, dtype=BF), shape(count, width, dtype=BF),
         shape(count, width, dtype=BF), shape(count, width, dtype=BF), shape(count, ff, dtype=BF),
         shape(count, ff, dtype=BF)],
        [w_first, w_up, w_down, hold(count, width), hold(count, width), hold(3, count, width, dtype=BF),
         hold(batch, pairs, 2 * length, length, dtype=BF), hold(batch, length, length),
         hold(count, width), hold(count, width), hold(length, width), hold(length, width),
         hold(count, width, dtype=BF),
         hold(count, width, dtype=BF), hold(3, count, width, dtype=BF), hold(count, width, dtype=BF),
         hold(count, width, dtype=BF), hold(count, width, dtype=BF), hold(count, ff, dtype=BF),
         hold(count, ff, dtype=BF),
         pltpu.SemaphoreType.DMA((3,)), pltpu.SemaphoreType.DMA((7,))],
        4 * count * width * (4 * width + 2 * ff),
        anywhere_outs=7,
    )
    dense_act_one, dense_d_heads, dense_mixed, dense_d_z, dense_act_two, dense_hidden, dense_d_upped = dense_kept
    d_delta = lax.ppermute(back_rows, "section", [(1, 0)])
    returned = lax.ppermute(back, "section", [(1, 0)])

    def routed_outer():
        return call(
            functools.partial(routed_outer_kernel, out_number),
            [place, d_delta, gate, hidden],
            0,
            down_outs,
            [hold(ff, width)],
            2 * picked * width * ff,
        )

    def dense_outer():
        return call(
            functools.partial(dense_outer_kernel, out_number),
            [place, dense_hidden, cotangent],
            0,
            down_outs,
            [hold(ff, width)],
            2 * count * width * ff,
        )

    down_pieces = lax.cond(routed, routed_outer, dense_outer)

    def routed_feed():
        return call(
            functools.partial(routed_feed_kernel, number, out_number),
            [place, *up, *down, d_delta, gate, rows, z, act_two, slope, gains],
            2 * number,
            [*up_outs, shape(picked, width), shape(1, width)],
            [w_up, w_down, hold(width, width), pltpu.SemaphoreType.DMA((2,))],
            6 * picked * width * ff,
        )

    def dense_feed():
        found = call(
            functools.partial(dense_feed_kernel, out_number),
            [place, dense_act_two, dense_d_upped],
            0,
            up_outs,
            [hold(width, width)],
            2 * count * width * ff,
        )
        return (*found, jnp.zeros((picked, width), F32), dense_gains[1:2])

    (*up_pieces, d_middle, g_two) = lax.cond(routed, routed_feed, dense_feed)
    if sliced(n):
        down_sum = Sum(down_pieces, n, FAR[2])
        up_sum = Sum(up_pieces, n, FAR[1])
        set_out = down_sum.step(0) + up_sum.step(0)
        d_middle = after(d_middle, set_out)

    def routed_attend():
        return call(
            functools.partial(routed_attend_back_kernel, number, out_number),
            [place, *first, d_delta, gate, d_middle, branch, rows, act_one, heads, chances, mixed,
             router_row, gains],
            number,
            [*first_outs, shape(1, width), shape(1, width), shape(picked, width)],
            [w_first, hold(width, width), pltpu.SemaphoreType.DMA((1,))],
            16 * picked * width * width,
        )

    def dense_attend():
        found = call(
            functools.partial(dense_attend_kernel, out_number),
            [place, dense_mixed, dense_d_z, dense_act_one, dense_d_heads],
            0,
            [*first_outs],
            [hold(width, width)],
            8 * count * width * width,
        )
        return (*found, dense_gains[0:1], jnp.zeros((1, width), F32), jnp.zeros((picked, width), F32))

    (*first_pieces, g_one, g_router, d_picked) = lax.cond(routed, routed_attend, dense_attend)

    small = jnp.concatenate([g_one, g_two, g_router, jnp.zeros((5, width), F32)])
    if sliced(n):
        first_sum = Sum(first_pieces, n, FAR[0])
        first_sum.step(0)
        for s in range(1, n // 4):
            for one in (down_sum, up_sum, first_sum):
                one.step(s)
        down_grad, up_grad, first_grad = (one.total() for one in (down_sum, up_sum, first_sum))
        small = sum_small(small, n)
    else:
        def plain(pieces):
            whole = pieces[0]
            whole = whole.reshape(whole.shape[0], n, -1, width).transpose(1, 0, 2, 3)
            return scatter_plain(whole.reshape(n, -1, width))

        down_grad, up_grad, first_grad = plain(down_pieces), plain(up_pieces), plain(first_pieces)
        small = lax.psum(small, "dp")
    first_grad = first_grad.reshape(4, rows_in, width)
    up_grad = up_grad.reshape(blocks, rows_in, width).transpose(1, 0, 2).reshape(rows_in, ff)
    gain_grad = lax.dynamic_slice_in_dim(small[:2], place[0] * (width // n), width // n, 1)
    other_small = lax.ppermute(small, "section", [(0, 1), (1, 0)])
    router_grad = small[2] + other_small[2]

    picks = (chosen[:, :, None] == lax.iota(jnp.int32, length)[None, None, :]).astype(F32)
    spread = jnp.einsum(
        "wgo,wgq->woq", picks, d_picked.reshape(batch, kept, width), precision=lax.Precision.HIGHEST)
    first_rows = (returned.astype(F32) + spread.reshape(count, width)).astype(BF)
    ends = jnp.where(routed, first_rows, result)[None]
    return (
        ends, router_grad, gain_grad[None], first_grad[:3][None], first_grad[3][None],
        up_grad[None], down_grad[None],
    )


def solution(mesh):
    return jax.shard_map(
        body,
        mesh=mesh,
        in_specs=(
            P("dp", None),
            P("dp", None),
            P("dp", None),
            P("dp", None),
            P(),
            P("section", None, None),
            P("section", None, "dp", None),
            P("section", "dp", None),
            P("section", "dp", None),
            P("section", "dp", None),
        ),
        out_specs=(
            P("section", "dp", None),
            P(),
            P("section", None, "dp"),
            P("section", None, "dp", None),
            P("section", "dp", None),
            P("section", "dp", None),
            P("section", "dp", None),
        ),
        check_vma=False,
    )
```

```python
import functools

import jax
import jax.numpy as jnp
from jax import lax
from jax.experimental import pallas as pl
from jax.experimental.pallas import tpu as pltpu
from jax.sharding import PartitionSpec as P

HEAD_DIM = 64
LANES = 2 * HEAD_DIM
EPSILON = 1e-05
MASKED = -1e30
BF = jnp.bfloat16
F32 = jnp.float32
VMEM_BYTES = 60 * 1024 * 1024
STRIP = 16
CODES = 16
SHARDS = 16


def move(value, pairs):
    return lax.ppermute(value, "dp", pairs)


def device_at(spot, core, depth):
    return 4 * spot + core if spot < depth else 4 * (2 * depth - 1 - spot) + 2 + core


def routes(n):
    depth = n // 4
    ring = 2 * depth

    def turned(by):
        return [
            (device_at(r, c, depth), device_at((r + by) % ring, c, depth))
            for r in range(ring) for c in range(2)
        ]

    return turned(1), turned(-1), [(i, i ^ 1) for i in range(n)]


def hops(depth, far):
    return (depth, depth - 1) if far == 0 else (depth - 1, depth)


def slots(depth, far):
    ahead, behind = hops(depth, far)
    distances = [0] + list(range(1, ahead + 1)) + [-d for d in range(1, behind + 1)]
    return [(d, c) for d in distances for c in range(2)]


def after(value, token):
    return lax.optimization_barrier((value, token))[0]


def sliced(n):
    return n == 16


FAR = (0, 1, 0)


def gather_halves(halves, n, token):
    depth = n // 4
    forward, backward, beside = routes(n)
    held = [{(0, 0): half, (0, 1): move(half, beside)} for half in halves]
    for s in range(1, depth + 1):
        for far, mine in enumerate(held):
            ahead, behind = hops(depth, far)
            for sign, limit, way in ((1, ahead, forward), (-1, behind, backward)):
                if s <= limit:
                    source = mine[sign * (s - 1), 0]
                    came = move(after(source, token) if s == 2 else source, way)
                    mine[sign * s, 0] = came
                    mine[sign * s, 1] = move(came, beside)
    return [[mine[slot] for slot in slots(depth, far)] for far, mine in enumerate(held)]


EXTRA = 16


class Sum:
    def __init__(self, own, other, n, far, spot):
        self.depth = n // 4
        forward, backward, beside = routes(n)
        self.ways = (forward, backward) if far == 0 else (backward, forward)
        self.sign = 1 if far == 0 else -1
        self.own, self.got = own, move(other, beside)
        self.spot = spot
        self.came = [None, None]

    def block(self, held, distance):
        at = lax.rem(self.spot + (2 * self.depth + distance), 2 * self.depth)
        return lax.dynamic_index_in_dim(held, at, 0, keepdims=False).astype(F32)

    def term(self, distance, came):
        found = self.block(self.own, distance) + self.block(self.got, distance)
        for value in came:
            if value is not None:
                found = found + value.astype(F32)
        return found

    def step(self, s):
        for i in range(2):
            if s + i < self.depth:
                distance = self.sign * (self.depth - s) if i == 0 else -self.sign * (self.depth - s - 1)
                self.send(i, self.term(distance, [self.came[i]]).astype(BF))

    def send(self, i, value):
        self.came[i] = move(value, self.ways[i])

    def total(self):
        return self.term(0, self.came)


class SumAndLines(Sum):
    def __init__(self, own, other, n, far, spot, core):
        super().__init__(own, other, n, far, spot)
        rows = own.shape[1] - EXTRA
        mine, beside = own[0, rows:rows + 3], self.got[0, rows:rows + 3]
        both = jnp.concatenate([jnp.where(core == 0, mine, beside), jnp.where(core == 0, beside, mine)])
        self.lines = {0: jnp.concatenate([both, jnp.zeros((EXTRA - 6, own.shape[2]), BF)])}

    def send(self, i, value):
        rows = value.shape[0] - EXTRA
        came = self.lines[0] if self.came[i] is None else self.came[i][rows:]
        super().send(i, jnp.concatenate([value[:rows], came]))
        sign = self.sign if i == 0 else -self.sign
        self.lines[-sign * (1 + max(sign * -d for d in self.lines))] = self.came[i][rows:]

    def all_lines(self):
        ring = 2 * self.depth
        found = jnp.stack([self.lines[d if d in self.lines else d - ring] for d in range(ring)])
        found = lax.dynamic_slice_in_dim(jnp.concatenate([found, found]), ring - self.spot, ring, 0)
        parts = found[:, :6].astype(F32).reshape(ring, 2, 3, -1)
        return jnp.sum((parts[:, :, 0] + parts[:, :, 1]) + parts[:, :, 2], axis=(0, 1))


def scatter_plain(whole):
    return lax.psum_scatter(whole.astype(F32), "dp", scatter_dimension=0, tiled=False)


def dot(a, b):
    return jnp.dot(a, b, preferred_element_type=F32)


def dot_t(a, b):
    return lax.dot_general(a, b, (((1,), (1,)), ((), ())), preferred_element_type=F32)


def t_dot(a, b):
    return lax.dot_general(a, b, (((0,), (0,)), ((), ())), preferred_element_type=F32)


def spot_of(me, depth):
    return jnp.where((me // 2) % 2 == 0, me // 4, 2 * depth - 1 - me // 4)


def device_on(me, distance, core, depth):
    spot = lax.rem(spot_of(me, depth) + (2 * depth + distance), 2 * depth)
    base = jnp.where(spot < depth, 4 * spot, 4 * (2 * depth - 1 - spot) + 2)
    return base + ((me % 2) ^ core)


def fetch_start(refs, holds, sems, me, names):
    if len(refs) == 3:
        for i in names:
            pltpu.make_async_copy(refs[i], holds[i], sems.at[i]).start()
        return
    count = len(refs) // 2
    depth = count // 4
    rows = holds[0].shape[1]
    cuts = ((0, 0, 0, 0, rows), (0, 1, rows, 0, rows // 2), (1, 1, 0, rows // 2, rows // 2), (1, 2, rows // 2, 0, rows))
    for i in names:
        for far, name, source, target, size in cuts:
            if name == i:
                for (distance, core), ref in zip(slots(depth, far), refs[far * count:(far + 1) * count]):
                    origin = device_on(me, -distance, core, depth)
                    pltpu.make_async_copy(
                        ref.at[pl.ds(source, size)], holds[i].at[origin, pl.ds(target, size)], sems.at[i]
                    ).start()


def ready(hold, sem):
    pltpu.make_async_copy(hold, hold, sem).wait()


def matrix(hold, q):
    shards, _, width = hold.shape
    count = width // shards
    return hold[:, q * count:(q + 1) * count, :].reshape(width, width)


def band(hold, b):
    shards, count, width = hold.shape
    some = width // count
    return hold[b * some:(b + 1) * some].reshape(width, width)


def deal(value, outs, core, first, q):
    piece = slice(q[0], q[1])
    rows = q[1] - q[0]
    number = value.shape[0] // rows
    if len(outs) == 1:
        outs[0][first:first + number, piece, :] = value.reshape(number, rows, value.shape[1]).astype(BF)
        return
    own, other = outs
    ring = own.shape[0]
    for t in range(number // 2):
        even, odd = value[2 * t * rows:(2 * t + 1) * rows], value[(2 * t + 1) * rows:(2 * t + 2) * rows]
        z, x = divmod(first // 2 + t, 2)
        spot = z if x == 0 else ring - 1 - z
        own[spot, piece, :] = jnp.where(core == 0, even, odd).astype(BF)
        other[spot, piece, :] = jnp.where(core == 0, odd, even).astype(BF)


def split(line):
    high = line.astype(BF).astype(F32)
    middle = (line - high).astype(BF).astype(F32)
    return [high, middle, line - high - middle]


def deal_lines(lines, outs, small):
    value = jnp.concatenate(lines + [jnp.zeros((EXTRA - len(lines), lines[0].shape[1]), F32)], axis=0)
    small[...] = value
    if len(outs) == 2:
        for out in outs:
            for spot in range(out.shape[0]):
                out[spot, out.shape[1] - EXTRA:, :] = value.astype(BF)


def deal_matrix(value, outs, core, q):
    count = value.shape[0] // SHARDS
    deal(value, outs, core, 0, (q * count, (q + 1) * count))


def deal_band(value, outs, core, b):
    count = outs[0].shape[1] - (EXTRA if len(outs) == 2 else 0)
    deal(value, outs, core, b * (value.shape[0] // count), (0, count))


def inverse_of(rows):
    return lax.rsqrt(jnp.mean(rows * rows, axis=-1, keepdims=True) + EPSILON)


def norm_back(upstream, normed, inverse, gain):
    scaled = upstream * gain
    d_gain = jnp.sum(upstream * normed, axis=0, keepdims=True)
    d_rows = inverse * (scaled - normed * jnp.mean(scaled * normed, axis=-1, keepdims=True))
    return d_rows, d_gain


def normal_parts(value):
    whole = 0.5 + 0.5 * lax.erf(value * 0.7071067811865476)
    return whole, value * jnp.exp(value * value * -0.5) * 0.3989422804014327


def left_lanes(rows):
    return lax.broadcasted_iota(jnp.int32, (rows, LANES), 1) < HEAD_DIM


def two_heads(value):
    left = left_lanes(value.shape[0])
    zero = jnp.zeros_like(value)
    return jnp.concatenate([jnp.where(left, value, zero), jnp.where(left, zero, value)], axis=0)


def one_row(value):
    half = value.shape[0] // 2
    return jnp.where(left_lanes(half), value[:half], value[half:])


def bias_of(same):
    shape = same.shape
    order = lax.broadcasted_iota(jnp.int32, shape, 0) >= lax.broadcasted_iota(jnp.int32, shape, 1)
    return jnp.where(order & (same > 0.5), 0.0, MASKED).astype(F32)


def hot_rows(line, count):
    return (lax.broadcasted_iota(jnp.int32, (count, line.shape[1]), 0) == line).astype(BF)


def attend(groups, biases):
    size = groups[0][0].shape[0]
    scale = jnp.asarray(HEAD_DIM ** -0.5, BF)
    scores = [dot_t(two_heads(query) * scale, keyed) for query, keyed, _ in groups]
    found = []
    for value, bias in zip(scores, biases):
        value = (value.reshape(2, size, size) + bias[None]).reshape(2 * size, size)
        powers = jnp.exp(value - jnp.max(value, axis=-1, keepdims=True))
        found.append((powers * (1.0 / jnp.sum(powers, axis=-1, keepdims=True))).astype(BF))
    mixed = [one_row(dot(chances, valued)).astype(BF) for chances, (_, _, valued) in zip(found, groups)]
    return mixed, found


def attend_back(groups, mixed, chances, d_mixed):
    both = [two_heads(value) for value in d_mixed]
    d_chances = [dot_t(value, valued) for value, (_, _, valued) in zip(both, groups)]
    d_value = [t_dot(chance, value) for chance, value in zip(chances, both)]
    factor = HEAD_DIM ** -0.5
    d_scores = []
    for found, value, blend, chance in zip(d_chances, d_mixed, mixed, chances):
        overlap = jnp.sum(two_heads(value.astype(F32) * blend.astype(F32)), axis=-1, keepdims=True)
        d_scores.append((chance.astype(F32) * (found - overlap)).astype(BF))
    d_query = [one_row(dot(value, keyed)) * factor for value, (_, keyed, _) in zip(d_scores, groups)]
    d_key = [t_dot(value, two_heads(query)) * factor for value, (query, _, _) in zip(d_scores, groups)]
    return [[one.astype(BF) for one in some] for some in (d_query, d_key, d_value)]


def pairs_of(value):
    return [value[:, p:p + LANES] for p in range(0, value.shape[1], LANES)]


def lanes_of(p):
    return pl.ds(pl.multiple_of(p * LANES, LANES), LANES)


def routed_kernel(slot_count, batch, place, *refs):
    shards = refs[:slot_count]
    (tokens, spots, codes, router, gains,
     rows_o, gate_o, z_o, act_one_o, heads_o, chances_o, mixed_o, act_two_o, hidden_o, slope_o, branch_o, delta_o,
     w_first, w_up, w_down, sems) = refs[slot_count:]
    fetch_start(shards, (w_first, w_up, w_down), sems, place[0], (0, 1, 2))
    hot = hot_rows(spots[...], tokens.shape[0])
    rows = t_dot(hot, tokens[...])
    rows_o[...] = rows
    gate = jax.nn.sigmoid(jnp.sum(rows * router[...], axis=-1, keepdims=True))
    gate_o[...] = gate
    act = (rows * inverse_of(rows) * gains[0:1]).astype(BF)
    act_one_o[...] = act
    member = dot(hot_rows(codes[...], CODES * batch), hot).astype(BF)
    bias = bias_of(t_dot(member, member))
    ready(w_first, sems.at[0])
    heads = [dot(act, matrix(w_first, c)).astype(BF) for c in range(3)]
    for c in range(3):
        heads_o[c] = heads[c]
    groups = list(zip(*(pairs_of(value) for value in heads)))
    found, chances = attend(groups, [bias] * len(groups))
    for p, chance in enumerate(chances):
        chances_o[p] = chance.astype(F32)
    mixed = jnp.concatenate(found, axis=1)
    mixed_o[...] = mixed
    z = dot(mixed, matrix(w_first, 3))
    z_o[...] = z
    middle = rows + z
    act_two = (middle * inverse_of(middle) * gains[1:2]).astype(BF)
    act_two_o[...] = act_two
    ready(w_up, sems.at[1])
    ready(w_down, sems.at[2])
    width = rows.shape[1]
    for b in range(hidden_o.shape[1] // width):
        lanes = slice(b * width, (b + 1) * width)
        upped = dot(act_two, matrix(w_up, b))
        whole, dense = normal_parts(upped)
        hidden_o[:, lanes] = (upped * whole).astype(BF)
        slope_o[:, lanes] = whole + dense
    branch = z_o[...] + dot(hidden_o[...], w_down[...].reshape(hidden_o.shape[1], width))
    branch_o[...] = branch
    delta_o[...] = (gate * branch).astype(BF)


def deal_down(hidden, d_out, outs, core):
    width = d_out.shape[1]
    for b in range(hidden.shape[1] // width):
        deal_band(t_dot(hidden[:, b * width:(b + 1) * width], d_out), outs, core, b)


def routed_outer_kernel(out_count, place, hidden, d_delta, gate, branch, rows, *refs):
    outs, (d_logit_o, small_o) = refs[:out_count], refs[out_count:]
    gated = gate[...]
    upstream = d_delta[...].astype(F32)
    d_logit = jnp.sum(upstream * branch[...], axis=-1, keepdims=True) * gated * (1.0 - gated)
    d_logit_o[...] = d_logit
    deal_lines(split(jnp.sum(d_logit * rows[...], axis=0, keepdims=True)), outs, small_o)
    deal_down(hidden, (gated * upstream).astype(BF), outs, place[0] % 2)


def routed_back_kernel(slot_count, out_count, place, *refs):
    shards = refs[:slot_count]
    (d_delta, gate, rows, z, act_two, slope, d_logit, act_one, heads, chances, mixed, router, gains) = refs[
        slot_count:slot_count + 13]
    refs = refs[slot_count + 13:]
    ups_o, firsts_o = refs[:out_count], refs[out_count:2 * out_count]
    small_o, d_picked_o, w_first, w_up, w_down, sems = refs[2 * out_count:]
    core = place[0] % 2
    fetch_start(shards, (w_first, w_up, w_down), sems, place[0], (2, 1, 0))
    width = rows.shape[1]
    blocks = slope.shape[1] // width
    gradient = gate[...] * d_delta[...].astype(F32)
    d_out = gradient.astype(BF)
    ready(w_down, sems.at[2])
    d_upped = []
    for b in range(blocks):
        d_hidden = dot_t(d_out, band(w_down, b))
        d_upped.append((d_hidden * slope[:, b * width:(b + 1) * width]).astype(BF))
    ready(w_up, sems.at[1])
    d_act = jnp.zeros(rows.shape, F32)
    for b in range(blocks):
        d_act = d_act + dot_t(d_upped[b], matrix(w_up, b))
    held = rows[...]
    middle = held + z[...]
    inverse = inverse_of(middle)
    d_middle, g_two = norm_back(d_act, middle * inverse, inverse, gains[1:2])
    d_z = (gradient + d_middle).astype(BF)
    ready(w_first, sems.at[0])
    d_mixed = dot_t(d_z, matrix(w_first, 3)).astype(BF)
    for b in range(blocks):
        deal_matrix(t_dot(act_two[...], d_upped[b]), ups_o, core, b)
    blend = mixed[...]
    groups = list(zip(*(pairs_of(heads[c]) for c in range(3))))
    found = attend_back(
        groups, pairs_of(blend), [chances[p].astype(BF) for p in range(len(groups))], pairs_of(d_mixed))
    deal_matrix(t_dot(blend, d_z), firsts_o, core, 3)
    d_heads = [jnp.concatenate(one, axis=1) for one in found]
    d_act = jnp.zeros(rows.shape, F32)
    for c in range(3):
        d_act = d_act + dot_t(d_heads[c], matrix(w_first, c))
    for c in range(3):
        deal_matrix(t_dot(act_one[...], d_heads[c]), firsts_o, core, c)
    inverse = inverse_of(held)
    d_rows, g_one = norm_back(d_act, held * inverse, inverse, gains[0:1])
    d_picked_o[...] = d_rows + d_middle + d_logit[...] * router[...]
    deal_lines([g_one, g_two], firsts_o, small_o)


def dense_kernel(slot_count, place, *refs):
    shards = refs[:slot_count]
    (tokens, cotangent, delta, spots, segments, gains,
     result_o, back_o, picked_o, gain_o,
     act_one_o, d_heads_o, mixed_o, d_z_o, act_two_o, hidden_o, d_upped_o,
     w_first, w_up, w_down, rows, z, heads, chances, bias, fed, d_act, upped, d_hidden, d_mixed,
     act_one, d_heads, mixed, d_z, act_two, hidden, d_upped, sems, out_sems) = refs[slot_count:]
    holds = (w_first, w_up, w_down)
    fetch_start(shards, holds, sems, place[0], (0,))
    batch, length, _ = bias.shape
    width = tokens.shape[1]
    pairs = width // LANES
    blocks = hidden.shape[1] // width
    parts = [slice(s * length, (s + 1) * length) for s in range(batch)]
    copies = [
        pltpu.make_async_copy(held, out, out_sems.at[i])
        for i, (held, out) in enumerate((
            (act_one, act_one_o), (d_heads, d_heads_o), (mixed, mixed_o), (d_z, d_z_o),
            (act_two, act_two_o), (hidden, hidden_o), (d_upped, d_upped_o),
        ))
    ]

    hot = hot_rows(spots[...], tokens.shape[0])
    for s, part in enumerate(parts):
        held = tokens[part].astype(F32) + dot(hot[part], delta[...])
        rows[part] = held
        act_one[part] = (held * inverse_of(held) * gains[0:1]).astype(BF)
        member = hot_rows(segments[:, part], CODES)
        bias[s] = bias_of(t_dot(member, member))
    copies[0].start()
    ready(w_first, sems.at[0])
    for c in range(3):
        for part in parts:
            heads[c, part] = dot(act_one[part], matrix(w_first, c)).astype(BF)
    fetch_start(shards, holds, sems, place[0], (1, 2))

    def forward(p, carry):
        lanes = lanes_of(p)
        groups = [tuple(heads[c, part, lanes] for c in range(3)) for part in parts]
        blends, found = attend(groups, [bias[s] for s in range(batch)])
        for s, part in enumerate(parts):
            mixed[part, lanes] = blends[s]
            chances[s, p] = found[s]
        return carry

    lax.fori_loop(0, pairs, forward, 0)
    copies[2].start()
    for part in parts:
        attended = dot(mixed[part], matrix(w_first, 3))
        z[part] = attended
        middle = rows[part] + attended
        act_two[part] = (middle * inverse_of(middle) * gains[1:2]).astype(BF)
    copies[4].start()
    ready(w_up, sems.at[1])
    ready(w_down, sems.at[2])
    fed[...] = jnp.zeros(fed.shape, F32)
    d_act[...] = jnp.zeros(d_act.shape, F32)

    for b in range(blocks):
        lanes = slice(b * width, (b + 1) * width)
        for s, part in enumerate(parts):
            upped[...] = dot(act_two[part], matrix(w_up, b))
            d_hidden[...] = dot_t(cotangent[part], band(w_down, b))

            def strip(r, carry):
                spot = pl.ds(pl.multiple_of(r * STRIP, STRIP), STRIP)
                there = pl.ds(pl.multiple_of(s * length + r * STRIP, STRIP), STRIP)
                for half in range(2):
                    cut = slice(half * width // 2, (half + 1) * width // 2)
                    out = slice(b * width + half * width // 2, b * width + (half + 1) * width // 2)
                    value = upped[spot, cut]
                    whole, dense = normal_parts(value)
                    hidden[there, out] = (value * whole).astype(BF)
                    d_upped[there, out] = (d_hidden[spot, cut] * (whole + dense)).astype(BF)
                return carry

            lax.fori_loop(0, length // STRIP, strip, 0)
            fed[part] += dot(hidden[part, lanes], band(w_down, b))
            d_act[part] += dot_t(d_upped[part, lanes], matrix(w_up, b))
    copies[5].start()
    copies[6].start()
    gain = jnp.zeros((1, width), F32)
    for part in parts:
        result_o[part] = (rows[part] + z[part] + fed[part]).astype(BF)
        middle = rows[part] + z[part]
        inverse = inverse_of(middle)
        d_middle, more = norm_back(d_act[part], middle * inverse, inverse, gains[1:2])
        gain = gain + more
        held = cotangent[part].astype(F32) + d_middle
        d_act[part] = held
        d_z[part] = held.astype(BF)
        d_mixed[part] = dot_t(held.astype(BF), matrix(w_first, 3)).astype(BF)
    gain_o[1:2] = gain
    copies[3].start()

    def backward(p, carry):
        lanes = lanes_of(p)
        groups = [tuple(heads[c, part, lanes] for c in range(3)) for part in parts]
        found = attend_back(
            groups, [mixed[part, lanes] for part in parts], [chances[s, p] for s in range(batch)],
            [d_mixed[part, lanes] for part in parts])
        for c in range(3):
            for s, part in enumerate(parts):
                d_heads[c, part, lanes] = found[c][s]
        return carry

    lax.fori_loop(0, pairs, backward, 0)
    copies[1].start()
    gain = jnp.zeros((1, width), F32)
    for s, part in enumerate(parts):
        d_first = dot_t(d_heads[0, part], matrix(w_first, 0))
        d_first = d_first + dot_t(d_heads[1, part], matrix(w_first, 1))
        d_first = d_first + dot_t(d_heads[2, part], matrix(w_first, 2))
        held = rows[part]
        inverse = inverse_of(held)
        d_rows, more = norm_back(d_first, held * inverse, inverse, gains[0:1])
        gain = gain + more
        back_o[part] = (d_act[part] + d_rows).astype(BF)
    picked_o[...] = t_dot(hot, back_o[...]).astype(BF)
    gain_o[0:1] = gain
    for copy in copies:
        copy.wait()


def dense_outer_kernel(out_count, place, hidden, d_out, *refs):
    outs, (d_logit_o, small_o) = refs[:out_count], refs[out_count:]
    d_logit_o[...] = jnp.zeros(d_logit_o.shape, F32)
    deal_lines([jnp.zeros((1, d_out.shape[1]), F32)], outs, small_o)
    deal_down(hidden, d_out[...], outs, place[0] % 2)


def dense_back_kernel(out_count, place, act_two, d_upped, mixed, d_z, act_one, d_heads, gains, *refs):
    ups_o, firsts_o, small_o = refs[:out_count], refs[out_count:2 * out_count], refs[2 * out_count]
    core = place[0] % 2
    width = act_two.shape[1]
    for b in range(d_upped.shape[1] // width):
        deal_matrix(t_dot(act_two[...], d_upped[:, b * width:(b + 1) * width]), ups_o, core, b)
    deal_matrix(t_dot(mixed[...], d_z[...]), firsts_o, core, 3)
    for c in range(3):
        deal_matrix(t_dot(act_one[...], d_heads[c]), firsts_o, core, c)
    deal_lines([gains[0:1], gains[1:2]], firsts_o, small_o)


def call(kernel, inputs, anywhere, outs, scratch, flops, anywhere_outs=0):
    vmem = pl.BlockSpec(memory_space=pltpu.VMEM)
    hbm = pl.BlockSpec(memory_space=pltpu.HBM)
    specs = [pl.BlockSpec(memory_space=pltpu.SMEM)] + [hbm] * anywhere
    specs = specs + [vmem] * (len(inputs) - len(specs))
    moved = sum(v.size * v.dtype.itemsize for v in inputs) + sum(
        o.size * jnp.dtype(o.dtype).itemsize for o in outs)
    return tuple(pl.pallas_call(
        kernel,
        out_shape=outs,
        in_specs=specs,
        out_specs=[vmem] * (len(outs) - anywhere_outs) + [hbm] * anywhere_outs,
        scratch_shapes=scratch,
        compiler_params=pltpu.CompilerParams(vmem_limit_bytes=VMEM_BYTES),
        cost_estimate=pl.CostEstimate(flops=flops, bytes_accessed=moved, transcendentals=0),
    )(*inputs))


def body(
    tokens, cotangent, segments, chosen, router, norm_gains, attn_in, attn_out, ff_up, ff_down
):
    n = lax.axis_size("dp")
    routed = lax.axis_index("section") == 0
    place = lax.axis_index("dp").astype(jnp.int32).reshape(1)
    batch, length = segments.shape
    width = tokens.shape[1]
    kept = chosen.shape[1]
    rows_in, rows_down, ff = attn_in.shape[2], ff_down.shape[1], ff_up.shape[2]
    blocks, pairs = ff // width, width // LANES
    picked, count = batch * kept, batch * length
    gains = norm_gains[0]
    router_row = router[None]

    def shape(*dims, dtype=F32):
        return jax.ShapeDtypeStruct(dims, dtype)

    def hold(*dims, dtype=F32):
        return pltpu.VMEM(dims, dtype)

    first_part = jnp.concatenate([attn_in[0].reshape(-1, width), attn_out[0]])
    up_part = jnp.concatenate([ff_up[0][:, b * width:(b + 1) * width] for b in range(blocks)])
    parts = [first_part, up_part, ff_down[0]]
    part_rows = 4 * width // SHARDS
    order = lax.iota(jnp.int32, batch)[:, None]
    spots = (chosen + order * length).reshape(1, picked)
    lines = segments.reshape(1, count)
    codes = (segments + order * CODES).reshape(1, count)
    if sliced(n):
        half = part_rows // 2
        halves = [jnp.concatenate([first_part, up_part[:half]]), jnp.concatenate([up_part[half:], ff_down[0]])]
        shards = sum(gather_halves(halves, n, (spots, lines, codes)), [])
        outs = [shape(n // 2, part_rows, width, dtype=BF)] * 2
        wide_outs = [shape(n // 2, part_rows + EXTRA, width, dtype=BF)] * 2
    else:
        first, up, down = (lax.all_gather(part, "dp", axis=0) for part in parts)

        def dealt(value):
            value = value.reshape(n, 4, rows_in, width).transpose(1, 0, 2, 3)
            value = value.reshape(4, SHARDS, width // SHARDS, width).transpose(1, 0, 2, 3)
            return value.reshape(SHARDS, part_rows, width)

        shards = [dealt(first), dealt(up), down.reshape(SHARDS, part_rows, width)]
        outs = wide_outs = [shape(SHARDS, part_rows, width, dtype=BF)]
    number, out_number = len(shards), len(outs)
    w_first = w_up = w_down = hold(SHARDS, part_rows, width, dtype=BF)

    (rows, gate, z, act_one, heads, chances, mixed, act_two, hidden, slope, branch, delta) = call(
        functools.partial(routed_kernel, number, batch),
        [place, *shards, tokens, spots, codes, router_row, gains],
        number,
        [shape(picked, width), shape(picked, 1), shape(picked, width), shape(picked, width, dtype=BF),
         shape(3, picked, width, dtype=BF), shape(pairs, 2 * picked, picked),
         shape(picked, width, dtype=BF), shape(picked, width, dtype=BF), shape(picked, ff, dtype=BF),
         shape(picked, ff), shape(picked, width), shape(picked, width, dtype=BF)],
        [w_first, w_up, w_down, pltpu.SemaphoreType.DMA((3,))],
        4 * picked * width * (2 * width + ff),
    )
    arrived = lax.ppermute(delta, "section", [(0, 1)])

    (result, back, back_rows, dense_gains, *dense_kept) = call(
        functools.partial(dense_kernel, number),
        [place, *shards, tokens, cotangent, arrived, spots, lines, gains],
        number,
        [shape(count, width, dtype=BF), shape(count, width, dtype=BF), shape(picked, width, dtype=BF),
         shape(2, width),
         shape(count, width, dtype=BF), shape(3, count, width, dtype=BF), shape(count, width, dtype=BF),
         shape(count, width, dtype=BF), shape(count, width, dtype=BF), shape(count, ff, dtype=BF),
         shape(count, ff, dtype=BF)],
        [w_first, w_up, w_down, hold(count, width), hold(count, width), hold(3, count, width, dtype=BF),
         hold(batch, pairs, 2 * length, length, dtype=BF), hold(batch, length, length),
         hold(count, width), hold(count, width), hold(length, width), hold(length, width),
         hold(count, width, dtype=BF),
         hold(count, width, dtype=BF), hold(3, count, width, dtype=BF), hold(count, width, dtype=BF),
         hold(count, width, dtype=BF), hold(count, width, dtype=BF), hold(count, ff, dtype=BF),
         hold(count, ff, dtype=BF),
         pltpu.SemaphoreType.DMA((3,)), pltpu.SemaphoreType.DMA((7,))],
        4 * count * width * (4 * width + 2 * ff),
        anywhere_outs=7,
    )
    dense_act_one, dense_d_heads, dense_mixed, dense_d_z, dense_act_two, dense_hidden, dense_d_upped = dense_kept
    d_delta = lax.ppermute(back_rows, "section", [(1, 0)])
    returned = lax.ppermute(back, "section", [(1, 0)])

    outer_outs = [*wide_outs, shape(picked, 1), shape(EXTRA, width)]

    def routed_outer():
        return call(
            functools.partial(routed_outer_kernel, out_number),
            [place, hidden, d_delta, gate, branch, rows], 0, outer_outs, [], 2 * picked * width * ff)

    def dense_outer():
        return call(
            functools.partial(dense_outer_kernel, out_number),
            [place, dense_hidden, cotangent], 0, outer_outs, [], 2 * count * width * ff)

    (*down_pieces, d_logit, router_lines) = lax.cond(routed, routed_outer, dense_outer)
    if sliced(n):
        spot = spot_of(place[0], n // 4)
        down_sum = SumAndLines(*down_pieces, n, FAR[2], spot, place[0] % 2)

    def routed_back():
        return call(
            functools.partial(routed_back_kernel, number, out_number),
            [place, *shards, d_delta, gate, rows, z, act_two, slope, d_logit, act_one, heads, chances,
             mixed, router_row, gains],
            number,
            [*outs, *wide_outs, shape(EXTRA, width), shape(picked, width)],
            [w_first, w_up, w_down, pltpu.SemaphoreType.DMA((3,))],
            6 * picked * width * ff + 16 * picked * width * width,
        )

    def dense_back():
        found = call(
            functools.partial(dense_back_kernel, out_number),
            [place, dense_act_two, dense_d_upped, dense_mixed, dense_d_z, dense_act_one, dense_d_heads, dense_gains],
            0, [*outs, *wide_outs, shape(EXTRA, width)], [], 2 * count * width * ff + 8 * count * width * width,
        )
        return (*found, jnp.zeros((picked, width), F32))

    (*pieces, small, d_picked) = lax.cond(routed, routed_back, dense_back)
    up_pieces, first_pieces = pieces[:out_number], pieces[out_number:]
    picks = (chosen[:, :, None] == lax.iota(jnp.int32, length)[None, None, :]).astype(F32)

    def both_ends(returned, result):
        spread = jnp.einsum(
            "wgo,wgq->woq", picks, d_picked.reshape(batch, kept, width), precision=lax.Precision.HIGHEST)
        first_rows = (returned.astype(F32) + spread.reshape(count, width)).astype(BF)
        return jnp.where(routed, first_rows, result)[None]

    if sliced(n):
        pieces, returned = lax.optimization_barrier((pieces, returned))
        up_pieces, first_pieces = pieces[:out_number], pieces[out_number:]
        up_sum, first_sum = Sum(*up_pieces, n, FAR[1], spot), Sum(*first_pieces, n, FAR[0], spot)
        for s in range(n // 4):
            for one in (down_sum, up_sum, first_sum):
                one.step(s)
        ends = both_ends(returned, result)
        first_sum.came[0] = after(first_sum.came[0], ends)
        down_grad, up_grad, first_grad = (one.total() for one in (down_sum, up_sum, first_sum))
        down_grad, (first_grad, small) = down_grad[:part_rows], (first_grad[:part_rows], first_grad[part_rows:])
        router_grad = down_sum.all_lines()
    else:
        def plain(pieces, wide):
            whole = pieces[0]
            if wide:
                whole = whole.reshape(SHARDS, 4, -1, width).transpose(1, 0, 2, 3)
                whole = whole.reshape(4, n, -1, width).transpose(1, 0, 2, 3)
            return scatter_plain(whole.reshape(n, -1, width))

        down_grad = plain(down_pieces, False)
        up_grad, first_grad = plain(up_pieces, True), plain(first_pieces, True)
        small = lax.psum(small, "dp")
        ends = both_ends(returned, result)
        router_grad = jnp.sum(lax.psum(router_lines, "dp"), axis=0)
    first_grad = first_grad.reshape(4, rows_in, width)
    up_grad = up_grad.reshape(blocks, rows_in, width).transpose(1, 0, 2).reshape(rows_in, ff)
    gain_grad = lax.dynamic_slice_in_dim(small[:2], place[0] * (width // n), width // n, 1)
    router_grad = router_grad + lax.ppermute(router_grad, "section", [(0, 1), (1, 0)])

    return (
        ends, router_grad, gain_grad[None], first_grad[:3][None], first_grad[3][None],
        up_grad[None], down_grad[None],
    )


def solution(mesh):
    return jax.shard_map(
        body,
        mesh=mesh,
        in_specs=(
            P("dp", None),
            P("dp", None),
            P("dp", None),
            P("dp", None),
            P(),
            P("section", None, None),
            P("section", None, "dp", None),
            P("section", "dp", None),
            P("section", "dp", None),
            P("section", "dp", None),
        ),
        out_specs=(
            P("section", "dp", None),
            P(),
            P("section", None, "dp"),
            P("section", None, "dp", None),
            P("section", "dp", None),
            P("section", "dp", None),
            P("section", "dp", None),
        ),
        check_vma=False,
    )
```

```python
import functools

import jax
import jax.numpy as jnp
from jax import lax
from jax.experimental import pallas as pl
from jax.experimental.pallas import tpu as pltpu
from jax.sharding import PartitionSpec as P

HEAD_DIM = 64
LANES = 2 * HEAD_DIM
EPSILON = 1e-05
MASKED = -1e30
BF = jnp.bfloat16
F32 = jnp.float32
VMEM_BYTES = 60 * 1024 * 1024
STRIP = 16
CODES = 16
SHARDS = 16


def move(value, pairs):
    return lax.ppermute(value, "dp", pairs)


def device_at(spot, core, depth):
    return 4 * spot + core if spot < depth else 4 * (2 * depth - 1 - spot) + 2 + core


def routes(n):
    depth = n // 4
    ring = 2 * depth

    def turned(by):
        return [
            (device_at(r, c, depth), device_at((r + by) % ring, c, depth))
            for r in range(ring) for c in range(2)
        ]

    return turned(1), turned(-1), [(i, i ^ 1) for i in range(n)]


def hops(depth, far):
    return (depth, depth - 1) if far == 0 else (depth - 1, depth)


def after(value, token):
    return lax.optimization_barrier((value, token))[0]


def sliced(n):
    return n == 16


FAR = (0, 1, 0)


def first_ways(depth, far):
    return (depth, 1 - depth) if far == 0 else (-depth, depth - 1)


def lots(depth, far):
    ahead, behind = hops(depth, far)
    early = [0] + [sign * d for d in range(1, depth // 2 + 1) for sign in (1, -1)]
    late = [d for d in range(-behind, ahead + 1) if d not in early]
    return early, late


def gather_halves(halves, n, token):
    depth = n // 4
    forward, backward, beside = routes(n)
    held = [{0: half} for half in halves]
    for s in range(1, depth + 1):
        for far, mine in enumerate(held):
            ahead, behind = hops(depth, far)
            for sign, limit, way in ((1, ahead, forward), (-1, behind, backward)):
                if s <= limit:
                    source = mine[sign * (s - 1)]
                    mine[sign * s] = move(after(source, token) if s == 2 else source, way)
    found = []
    for far, mine in enumerate(held):
        early, late = lots(depth, far)
        found += [mine[d] for d in early + late]
        found += [move(jnp.stack([mine[d] for d in some]), beside) for some in (early, late)]
    return found


EXTRA = 16


class Sum:
    def __init__(self, own, other, n, far, spot, hurry):
        self.depth = n // 4
        forward, backward, beside = routes(n)
        self.ways = (forward, backward) if far == 0 else (backward, forward)
        self.far, self.spot = far, spot
        self.own, self.soon = own, None
        if hurry:
            first_two = jnp.stack([self.block(other, d) for d in first_ways(self.depth, far)])
            self.soon = move(first_two, beside)
            other = after(other, first_two)
        self.got = move(other, beside)
        self.came = [None, None]
        self.arrived = {}

    def block(self, held, distance):
        at = lax.rem(self.spot + (2 * self.depth + distance), 2 * self.depth)
        return lax.dynamic_index_in_dim(held, at, 0, keepdims=False)

    def term(self, distance, came, got=None):
        found = self.block(self.own, distance).astype(F32)
        found = found + (self.block(self.got, distance) if got is None else got).astype(F32)
        for value in came:
            if value is not None:
                found = found + value.astype(F32)
        return found

    def step(self, s):
        signs = [1 if self.far == i else -1 for i in range(2) if s + i < self.depth]
        values = [
            self.term(sign * (self.depth - s - i), [self.came[i]], self.soon[i] if s == 0 and self.soon is not None else None)
            for i, sign in enumerate(signs)]
        values = lax.optimization_barrier([value.astype(BF) for value in values])
        for i, (sign, value) in enumerate(zip(signs, values)):
            self.came[i] = self.arrived[-sign * (s + 1)] = move(value, self.ways[i])

    def total(self, token=None):
        last = self.came[0] if token is None else after(self.came[0], token)
        return lax.optimization_barrier(self.term(0, [self.came[1]])), last.astype(F32)


def scatter_plain(whole):
    return lax.psum_scatter(whole.astype(F32), "dp", scatter_dimension=0, tiled=False)


def dot(a, b):
    return jnp.dot(a, b, preferred_element_type=F32)


def dot_t(a, b):
    return lax.dot_general(a, b, (((1,), (1,)), ((), ())), preferred_element_type=F32)


def t_dot(a, b):
    return lax.dot_general(a, b, (((0,), (0,)), ((), ())), preferred_element_type=F32)


def spot_of(me, depth):
    return jnp.where((me // 2) % 2 == 0, me // 4, 2 * depth - 1 - me // 4)


def device_on(me, distance, core, depth):
    spot = lax.rem(spot_of(me, depth) + (2 * depth + distance), 2 * depth)
    base = jnp.where(spot < depth, 4 * spot, 4 * (2 * depth - 1 - spot) + 2)
    return base + ((me % 2) ^ core)


def fetch_start(refs, holds, sems, me, names):
    if len(refs) == 3:
        for i in names:
            pltpu.make_async_copy(refs[i], holds[i], sems.at[i]).start()
        return
    count = len(refs) // 2
    depth = (count - 2) // 2
    rows = holds[0].shape[1]
    cuts = ((0, 0, 0, 0, rows), (0, 1, rows, 0, rows // 2), (1, 1, 0, rows // 2, rows // 2), (1, 2, rows // 2, 0, rows))
    for i in names:
        for far, name, source, target, size in cuts:
            if name == i:
                mine = refs[far * count:(far + 1) * count]
                early, late = lots(depth, far)
                there = pl.ds(source, size)
                pieces = [(d, 0, ref.at[there]) for d, ref in zip(early + late, mine)]
                pieces += [(d, 1, mine[-2].at[k, there]) for k, d in enumerate(early)]
                pieces += [(d, 1, mine[-1].at[k, there]) for k, d in enumerate(late)]
                for distance, core, piece in pieces:
                    origin = device_on(me, -distance, core, depth)
                    pltpu.make_async_copy(piece, holds[i].at[origin, pl.ds(target, size)], sems.at[i]).start()


def ready(hold, sem):
    pltpu.make_async_copy(hold, hold, sem).wait()


def matrix(hold, q):
    shards, _, width = hold.shape
    count = width // shards
    return hold[:, q * count:(q + 1) * count, :].reshape(width, width)


def band(hold, b):
    shards, count, width = hold.shape
    some = width // count
    return hold[b * some:(b + 1) * some].reshape(width, width)


def deal(value, outs, me, first, piece):
    rows = piece.stop - piece.start
    number = value.shape[0] // rows
    if len(outs) == 1:
        outs[0][first:first + number, piece, :] = value.reshape(number, rows, value.shape[1]).astype(BF)
        return
    own, other = outs
    ring = own.shape[0]
    for t in range(number // 2):
        even, odd = value[2 * t * rows:(2 * t + 1) * rows], value[(2 * t + 1) * rows:(2 * t + 2) * rows]
        z, x = divmod(first // 2 + t, 2)
        spot = z if x == 0 else ring - 1 - z
        own[spot, piece, :] = jnp.where(me % 2 == 0, even, odd).astype(BF)
        other[spot, piece, :] = jnp.where(me % 2 == 0, odd, even).astype(BF)


def split(line):
    high = line.astype(BF).astype(F32)
    middle = (line - high).astype(BF).astype(F32)
    return [high, middle, line - high - middle]


def deal_lines(lines, outs, small):
    value = jnp.concatenate(lines + [jnp.zeros((EXTRA - len(lines), lines[0].shape[1]), F32)], axis=0)
    small[...] = value
    if len(outs) == 2:
        for out in outs:
            for spot in range(out.shape[0]):
                out[spot, out.shape[1] - EXTRA:, :] = value.astype(BF)


def deal_router(line, outs, small, me):
    three = split(line)
    none = jnp.zeros_like(line)
    mine, other = three + [none] * (EXTRA - 3), [none] * 3 + three + [none] * (EXTRA - 6)
    small[...] = jnp.concatenate(mine, axis=0)
    if len(outs) == 2:
        ring, row = outs[0].shape[0], outs[0].shape[1] - EXTRA
        for out, value in zip(outs, (mine, other)):
            value = jnp.concatenate(value, axis=0).astype(BF)
            for spot in range(ring):
                out[spot, row:, :] = jnp.zeros(value.shape, BF)
            for distance in first_ways(ring // 2, FAR[2]):
                out[lax.rem(spot_of(me, ring // 2) + ring + distance, ring), row:, :] = value


def router_kernel(count, place, *refs):
    own, got, arrived, (out, lines, sems) = refs[0], refs[1], refs[2:count + 2], refs[count + 2:]
    me = place[0]
    ring = count + 1
    depth = ring // 2
    spot = spot_of(me, depth)
    row = own.shape[1] - EXTRA
    away = lax.rem(spot + ring + first_ways(depth, FAR[2])[0], ring)
    copies = [pltpu.make_async_copy(own.at[away, pl.ds(row, EXTRA)], lines.at[0], sems.at[0]),
              pltpu.make_async_copy(got.at[0, pl.ds(row, EXTRA)], lines.at[1], sems.at[1])]
    ahead, behind = hops(depth, FAR[2])
    distances = list(range(-ahead, 0)) + list(range(1, behind + 1))
    for i, (distance, ref) in enumerate(zip(distances, arrived)):
        slot = 2 + lax.rem(spot + ring + distance, ring)
        copies.append(pltpu.make_async_copy(ref.at[pl.ds(row, EXTRA)], lines.at[slot], sems.at[2 + i]))
    for copy in copies:
        copy.start()
    for copy in copies:
        copy.wait()
    lines[2 + spot] = lines[0] + lines[1]
    total = jnp.zeros(out.shape, F32)
    for r in range(ring):
        value = lines[2 + r].astype(F32)
        low = (value[0:1] + value[1:2]) + value[2:3]
        high = (value[3:4] + value[4:5]) + value[5:6]
        total = total + jnp.where(me % 2 == 0, low, high)
        total = total + jnp.where(me % 2 == 0, high, low)
    out[...] = total


def deal_matrix(value, outs, me, q):
    count = value.shape[0] // SHARDS
    deal(value, outs, me, 0, slice(q * count, (q + 1) * count))


def deal_down(hidden, d_out, outs, me):
    width = d_out.shape[1]
    count = hidden.shape[1] // SHARDS
    for b in range(hidden.shape[1] // width):
        value = t_dot(hidden[:, b * width:(b + 1) * width], d_out)
        deal(value, outs, me, b * (width // count), slice(0, count))


def inverse_of(rows):
    return lax.rsqrt(jnp.mean(rows * rows, axis=-1, keepdims=True) + EPSILON)


def norm_back(upstream, normed, inverse, gain):
    scaled = upstream * gain
    d_gain = jnp.sum(upstream * normed, axis=0, keepdims=True)
    d_rows = inverse * (scaled - normed * jnp.mean(scaled * normed, axis=-1, keepdims=True))
    return d_rows, d_gain


def normal_parts(value):
    whole = 0.5 + 0.5 * lax.erf(value * 0.7071067811865476)
    return whole, value * jnp.exp(value * value * -0.5) * 0.3989422804014327


def left_lanes(rows):
    return lax.broadcasted_iota(jnp.int32, (rows, LANES), 1) < HEAD_DIM


def two_heads(value):
    left = left_lanes(value.shape[0])
    zero = jnp.zeros_like(value)
    return jnp.concatenate([jnp.where(left, value, zero), jnp.where(left, zero, value)], axis=0)


def one_row(value):
    half = value.shape[0] // 2
    return jnp.where(left_lanes(half), value[:half], value[half:])


def bias_of(same):
    shape = same.shape
    order = lax.broadcasted_iota(jnp.int32, shape, 0) >= lax.broadcasted_iota(jnp.int32, shape, 1)
    return jnp.where(order & (same > 0.5), 0.0, MASKED).astype(F32)


def hot_rows(line, count):
    return (lax.broadcasted_iota(jnp.int32, (count, line.shape[1]), 0) == line).astype(BF)


def attend(groups, biases):
    size = groups[0][0].shape[0]
    scale = jnp.asarray(HEAD_DIM ** -0.5, BF)
    scores = [dot_t(two_heads(query) * scale, keyed) for query, keyed, _ in groups]
    found = []
    for value, bias in zip(scores, biases):
        value = (value.reshape(2, size, size) + bias[None]).reshape(2 * size, size)
        powers = jnp.exp(value - jnp.max(value, axis=-1, keepdims=True))
        found.append((powers * (1.0 / jnp.sum(powers, axis=-1, keepdims=True))).astype(BF))
    mixed = [one_row(dot(chances, valued)).astype(BF) for chances, (_, _, valued) in zip(found, groups)]
    return mixed, found


def attend_back(groups, mixed, chances, d_mixed):
    both = [two_heads(value) for value in d_mixed]
    d_chances = [dot_t(value, valued) for value, (_, _, valued) in zip(both, groups)]
    d_value = [t_dot(chance, value) for chance, value in zip(chances, both)]
    factor = HEAD_DIM ** -0.5
    d_scores = []
    for found, value, blend, chance in zip(d_chances, d_mixed, mixed, chances):
        overlap = jnp.sum(two_heads(value.astype(F32) * blend.astype(F32)), axis=-1, keepdims=True)
        d_scores.append((chance.astype(F32) * (found - overlap)).astype(BF))
    d_query = [one_row(dot(value, keyed)) * factor for value, (_, keyed, _) in zip(d_scores, groups)]
    d_key = [t_dot(value, two_heads(query)) * factor for value, (query, _, _) in zip(d_scores, groups)]
    return [[one.astype(BF) for one in some] for some in (d_query, d_key, d_value)]


def pairs_of(value):
    return [value[:, p:p + LANES] for p in range(0, value.shape[1], LANES)]


def lanes_of(p):
    return pl.ds(pl.multiple_of(p * LANES, LANES), LANES)


def routed_kernel(slot_count, batch, place, *refs):
    shards = refs[:slot_count]
    (tokens, spots, codes, router, gains,
     rows_o, gate_o, z_o, act_one_o, heads_o, chances_o, mixed_o, act_two_o, hidden_o, slope_o, branch_o, delta_o,
     w_first, w_up, w_down, sems) = refs[slot_count:]
    fetch_start(shards, (w_first, w_up, w_down), sems, place[0], (0, 1, 2))
    hot = hot_rows(spots[...], tokens.shape[0])
    rows = t_dot(hot, tokens[...])
    rows_o[...] = rows
    gate = jax.nn.sigmoid(jnp.sum(rows * router[...], axis=-1, keepdims=True))
    gate_o[...] = gate
    act = (rows * inverse_of(rows) * gains[0:1]).astype(BF)
    act_one_o[...] = act
    member = dot(hot_rows(codes[...], CODES * batch), hot).astype(BF)
    bias = bias_of(t_dot(member, member))
    ready(w_first, sems.at[0])
    heads = [dot(act, matrix(w_first, c)).astype(BF) for c in range(3)]
    for c in range(3):
        heads_o[c] = heads[c]
    groups = list(zip(*(pairs_of(value) for value in heads)))
    found, chances = attend(groups, [bias] * len(groups))
    for p, chance in enumerate(chances):
        chances_o[p] = chance.astype(F32)
    mixed = jnp.concatenate(found, axis=1)
    mixed_o[...] = mixed
    z = dot(mixed, matrix(w_first, 3))
    z_o[...] = z
    middle = rows + z
    act_two = (middle * inverse_of(middle) * gains[1:2]).astype(BF)
    act_two_o[...] = act_two
    ready(w_up, sems.at[1])
    ready(w_down, sems.at[2])
    width = rows.shape[1]
    for b in range(hidden_o.shape[1] // width):
        lanes = slice(b * width, (b + 1) * width)
        upped = dot(act_two, matrix(w_up, b))
        whole, dense = normal_parts(upped)
        hidden_o[:, lanes] = (upped * whole).astype(BF)
        slope_o[:, lanes] = whole + dense
    branch = z_o[...] + dot(hidden_o[...], w_down[...].reshape(hidden_o.shape[1], width))
    branch_o[...] = branch
    delta_o[...] = (gate * branch).astype(BF)


def routed_back_kernel(slot_count, out_count, place, *refs):
    shards = refs[:slot_count]
    (d_delta, gate, branch, rows, z, hidden, act_two, slope, act_one, heads, chances, mixed, router, gains) = refs[
        slot_count:slot_count + 14]
    refs = refs[slot_count + 14:]
    downs_o, ups_o, firsts_o = (refs[i * out_count:(i + 1) * out_count] for i in range(3))
    router_o, small_o, d_picked_o, w_first, w_up, w_down, sems = refs[3 * out_count:]
    me = place[0]
    fetch_start(shards, (w_first, w_up, w_down), sems, me, (2, 1, 0))
    width = rows.shape[1]
    blocks = slope.shape[1] // width
    held = rows[...]
    gated = gate[...]
    upstream = d_delta[...].astype(F32)
    gradient = gated * upstream
    d_out = gradient.astype(BF)
    deal_down(hidden, d_out, downs_o, me)
    d_logit = jnp.sum(upstream * branch[...], axis=-1, keepdims=True) * gated * (1.0 - gated)
    deal_router(jnp.sum(d_logit * held, axis=0, keepdims=True), downs_o, router_o, me)
    ready(w_down, sems.at[2])
    d_upped = []
    for b in range(blocks):
        d_hidden = dot_t(d_out, band(w_down, b))
        d_upped.append((d_hidden * slope[:, b * width:(b + 1) * width]).astype(BF))
    ready(w_up, sems.at[1])
    d_act = jnp.zeros(rows.shape, F32)
    for b in range(blocks):
        d_act = d_act + dot_t(d_upped[b], matrix(w_up, b))
    middle = held + z[...]
    inverse = inverse_of(middle)
    d_middle, g_two = norm_back(d_act, middle * inverse, inverse, gains[1:2])
    d_z = (gradient + d_middle).astype(BF)
    ready(w_first, sems.at[0])
    d_mixed = dot_t(d_z, matrix(w_first, 3)).astype(BF)
    for b in range(blocks):
        deal_matrix(t_dot(act_two[...], d_upped[b]), ups_o, me, b)
    blend = mixed[...]
    groups = list(zip(*(pairs_of(heads[c]) for c in range(3))))
    found = attend_back(
        groups, pairs_of(blend), [chances[p].astype(BF) for p in range(len(groups))], pairs_of(d_mixed))
    deal_matrix(t_dot(blend, d_z), firsts_o, me, 3)
    d_heads = [jnp.concatenate(one, axis=1) for one in found]
    d_act = jnp.zeros(rows.shape, F32)
    for c in range(3):
        d_act = d_act + dot_t(d_heads[c], matrix(w_first, c))
    for c in range(3):
        deal_matrix(t_dot(act_one[...], d_heads[c]), firsts_o, me, c)
    inverse = inverse_of(held)
    d_rows, g_one = norm_back(d_act, held * inverse, inverse, gains[0:1])
    d_picked_o[...] = d_rows + d_middle + d_logit * router[...]
    deal_lines([g_one, g_two], ups_o, small_o)


def dense_kernel(slot_count, place, *refs):
    shards = refs[:slot_count]
    (tokens, cotangent, delta, spots, segments, gains,
     result_o, back_o, picked_o, gain_o,
     act_one_o, d_heads_o, mixed_o, d_z_o, act_two_o, hidden_o, d_upped_o,
     w_first, w_up, w_down, rows, z, heads, chances, bias, fed, d_act, upped, d_hidden, d_mixed,
     act_one, d_heads, mixed, d_z, act_two, hidden, d_upped, sems, out_sems) = refs[slot_count:]
    holds = (w_first, w_up, w_down)
    fetch_start(shards, holds, sems, place[0], (0,))
    batch, length, _ = bias.shape
    width = tokens.shape[1]
    pairs = width // LANES
    blocks = hidden.shape[1] // width
    parts = [slice(s * length, (s + 1) * length) for s in range(batch)]
    copies = [
        pltpu.make_async_copy(held, out, out_sems.at[i])
        for i, (held, out) in enumerate((
            (act_one, act_one_o), (d_heads, d_heads_o), (mixed, mixed_o), (d_z, d_z_o),
            (act_two, act_two_o), (hidden, hidden_o), (d_upped, d_upped_o),
        ))
    ]

    hot = hot_rows(spots[...], tokens.shape[0])
    for s, part in enumerate(parts):
        held = tokens[part].astype(F32) + dot(hot[part], delta[...])
        rows[part] = held
        act_one[part] = (held * inverse_of(held) * gains[0:1]).astype(BF)
        member = hot_rows(segments[:, part], CODES)
        bias[s] = bias_of(t_dot(member, member))
    copies[0].start()
    ready(w_first, sems.at[0])
    for c in range(3):
        for part in parts:
            heads[c, part] = dot(act_one[part], matrix(w_first, c)).astype(BF)
    fetch_start(shards, holds, sems, place[0], (1, 2))

    def forward(p, carry):
        lanes = lanes_of(p)
        groups = [tuple(heads[c, part, lanes] for c in range(3)) for part in parts]
        blends, found = attend(groups, [bias[s] for s in range(batch)])
        for s, part in enumerate(parts):
            mixed[part, lanes] = blends[s]
            chances[s, p] = found[s]
        return carry

    lax.fori_loop(0, pairs, forward, 0)
    copies[2].start()
    for part in parts:
        attended = dot(mixed[part], matrix(w_first, 3))
        z[part] = attended
        middle = rows[part] + attended
        act_two[part] = (middle * inverse_of(middle) * gains[1:2]).astype(BF)
    copies[4].start()
    ready(w_up, sems.at[1])
    ready(w_down, sems.at[2])
    fed[...] = jnp.zeros(fed.shape, F32)
    d_act[...] = jnp.zeros(d_act.shape, F32)

    for b in range(blocks):
        lanes = slice(b * width, (b + 1) * width)
        for s, part in enumerate(parts):
            upped[...] = dot(act_two[part], matrix(w_up, b))
            d_hidden[...] = dot_t(cotangent[part], band(w_down, b))

            def strip(r, carry):
                spot = pl.ds(pl.multiple_of(r * STRIP, STRIP), STRIP)
                there = pl.ds(pl.multiple_of(s * length + r * STRIP, STRIP), STRIP)
                for half in range(2):
                    cut = slice(half * width // 2, (half + 1) * width // 2)
                    out = slice(b * width + half * width // 2, b * width + (half + 1) * width // 2)
                    value = upped[spot, cut]
                    whole, dense = normal_parts(value)
                    hidden[there, out] = (value * whole).astype(BF)
                    d_upped[there, out] = (d_hidden[spot, cut] * (whole + dense)).astype(BF)
                return carry

            lax.fori_loop(0, length // STRIP, strip, 0)
            fed[part] += dot(hidden[part, lanes], band(w_down, b))
            d_act[part] += dot_t(d_upped[part, lanes], matrix(w_up, b))
    copies[5].start()
    copies[6].start()
    gain = jnp.zeros((1, width), F32)
    for part in parts:
        result_o[part] = (rows[part] + z[part] + fed[part]).astype(BF)
        middle = rows[part] + z[part]
        inverse = inverse_of(middle)
        d_middle, more = norm_back(d_act[part], middle * inverse, inverse, gains[1:2])
        gain = gain + more
        held = cotangent[part].astype(F32) + d_middle
        d_act[part] = held
        d_z[part] = held.astype(BF)
        d_mixed[part] = dot_t(held.astype(BF), matrix(w_first, 3)).astype(BF)
    gain_o[1:2] = gain
    copies[3].start()

    def backward(p, carry):
        lanes = lanes_of(p)
        groups = [tuple(heads[c, part, lanes] for c in range(3)) for part in parts]
        found = attend_back(
            groups, [mixed[part, lanes] for part in parts], [chances[s, p] for s in range(batch)],
            [d_mixed[part, lanes] for part in parts])
        for c in range(3):
            for s, part in enumerate(parts):
                d_heads[c, part, lanes] = found[c][s]
        return carry

    lax.fori_loop(0, pairs, backward, 0)
    copies[1].start()
    gain = jnp.zeros((1, width), F32)
    for s, part in enumerate(parts):
        d_first = dot_t(d_heads[0, part], matrix(w_first, 0))
        d_first = d_first + dot_t(d_heads[1, part], matrix(w_first, 1))
        d_first = d_first + dot_t(d_heads[2, part], matrix(w_first, 2))
        held = rows[part]
        inverse = inverse_of(held)
        d_rows, more = norm_back(d_first, held * inverse, inverse, gains[0:1])
        gain = gain + more
        back_o[part] = (d_act[part] + d_rows).astype(BF)
    picked_o[...] = t_dot(hot, back_o[...]).astype(BF)
    gain_o[0:1] = gain
    for copy in copies:
        copy.wait()


def dense_back_kernel(out_count, place, hidden, d_out, act_two, d_upped, mixed, d_z, act_one, d_heads, gains, *refs):
    downs_o, ups_o, firsts_o = (refs[i * out_count:(i + 1) * out_count] for i in range(3))
    router_o, small_o, d_picked_o = refs[3 * out_count:]
    me = place[0]
    deal_down(hidden, d_out[...], downs_o, me)
    deal_router(jnp.zeros((1, d_out.shape[1]), F32), downs_o, router_o, me)
    d_picked_o[...] = jnp.zeros(d_picked_o.shape, F32)
    width = act_two.shape[1]
    for b in range(d_upped.shape[1] // width):
        deal_matrix(t_dot(act_two[...], d_upped[:, b * width:(b + 1) * width]), ups_o, me, b)
    deal_matrix(t_dot(mixed[...], d_z[...]), firsts_o, me, 3)
    for c in range(3):
        deal_matrix(t_dot(act_one[...], d_heads[c]), firsts_o, me, c)
    deal_lines([gains[0:1], gains[1:2]], ups_o, small_o)


def call(kernel, inputs, anywhere, outs, scratch, flops, anywhere_outs=0):
    vmem = pl.BlockSpec(memory_space=pltpu.VMEM)
    hbm = pl.BlockSpec(memory_space=pltpu.HBM)
    specs = [pl.BlockSpec(memory_space=pltpu.SMEM)] + [hbm] * anywhere
    specs = specs + [vmem] * (len(inputs) - len(specs))
    moved = sum(v.size * v.dtype.itemsize for v in inputs) + sum(
        o.size * jnp.dtype(o.dtype).itemsize for o in outs)
    return tuple(pl.pallas_call(
        kernel,
        out_shape=outs,
        in_specs=specs,
        out_specs=[vmem] * (len(outs) - anywhere_outs) + [hbm] * anywhere_outs,
        scratch_shapes=scratch,
        compiler_params=pltpu.CompilerParams(vmem_limit_bytes=VMEM_BYTES),
        cost_estimate=pl.CostEstimate(flops=flops, bytes_accessed=moved, transcendentals=0),
    )(*inputs))


def body(
    tokens, cotangent, segments, chosen, router, norm_gains, attn_in, attn_out, ff_up, ff_down
):
    n = lax.axis_size("dp")
    routed = lax.axis_index("section") == 0
    place = lax.axis_index("dp").astype(jnp.int32).reshape(1)
    batch, length = segments.shape
    width = tokens.shape[1]
    kept = chosen.shape[1]
    rows_in, rows_down, ff = attn_in.shape[2], ff_down.shape[1], ff_up.shape[2]
    blocks, pairs = ff // width, width // LANES
    picked, count = batch * kept, batch * length
    gains = norm_gains[0]
    router_row = router[None]

    def shape(*dims, dtype=F32):
        return jax.ShapeDtypeStruct(dims, dtype)

    def hold(*dims, dtype=F32):
        return pltpu.VMEM(dims, dtype)

    first_part = jnp.concatenate([attn_in[0].reshape(-1, width), attn_out[0]])
    up_part = jnp.concatenate([ff_up[0][:, b * width:(b + 1) * width] for b in range(blocks)])
    parts = [first_part, up_part, ff_down[0]]
    part_rows = 4 * width // SHARDS
    order = lax.iota(jnp.int32, batch)[:, None]
    spots = (chosen + order * length).reshape(1, picked)
    lines = segments.reshape(1, count)
    codes = (segments + order * CODES).reshape(1, count)
    if sliced(n):
        half = part_rows // 2
        halves = [jnp.concatenate([first_part, up_part[:half]]), jnp.concatenate([up_part[half:], ff_down[0]])]
        shards = gather_halves(halves, n, (spots, lines, codes))
        outs, wide_outs = (
            [shape(n // 2, part_rows + more, width, dtype=BF)] * 2 for more in (0, EXTRA))
    else:
        first, up, down = (lax.all_gather(part, "dp", axis=0) for part in parts)

        def dealt(value):
            value = value.reshape(n, 4, rows_in, width).transpose(1, 0, 2, 3)
            value = value.reshape(4, SHARDS, width // SHARDS, width).transpose(1, 0, 2, 3)
            return value.reshape(SHARDS, part_rows, width)

        shards = [dealt(first), dealt(up), down.reshape(SHARDS, part_rows, width)]
        outs = wide_outs = [shape(SHARDS, part_rows, width, dtype=BF)]
    number, out_number = len(shards), len(outs)
    w_first = w_up = w_down = hold(SHARDS, part_rows, width, dtype=BF)

    (rows, gate, z, act_one, heads, chances, mixed, act_two, hidden, slope, branch, delta) = call(
        functools.partial(routed_kernel, number, batch),
        [place, *shards, tokens, spots, codes, router_row, gains],
        number,
        [shape(picked, width), shape(picked, 1), shape(picked, width), shape(picked, width, dtype=BF),
         shape(3, picked, width, dtype=BF), shape(pairs, 2 * picked, picked),
         shape(picked, width, dtype=BF), shape(picked, width, dtype=BF), shape(picked, ff, dtype=BF),
         shape(picked, ff), shape(picked, width), shape(picked, width, dtype=BF)],
        [w_first, w_up, w_down, pltpu.SemaphoreType.DMA((3,))],
        4 * picked * width * (2 * width + ff),
    )
    arrived = lax.ppermute(delta, "section", [(0, 1)])

    (result, back, back_rows, dense_gains, *dense_kept) = call(
        functools.partial(dense_kernel, number),
        [place, *shards, tokens, cotangent, arrived, spots, lines, gains],
        number,
        [shape(count, width, dtype=BF), shape(count, width, dtype=BF), shape(picked, width, dtype=BF),
         shape(2, width),
         shape(count, width, dtype=BF), shape(3, count, width, dtype=BF), shape(count, width, dtype=BF),
         shape(count, width, dtype=BF), shape(count, width, dtype=BF), shape(count, ff, dtype=BF),
         shape(count, ff, dtype=BF)],
        [w_first, w_up, w_down, hold(count, width), hold(count, width), hold(3, count, width, dtype=BF),
         hold(batch, pairs, 2 * length, length, dtype=BF), hold(batch, length, length),
         hold(count, width), hold(count, width), hold(length, width), hold(length, width),
         hold(count, width, dtype=BF),
         hold(count, width, dtype=BF), hold(3, count, width, dtype=BF), hold(count, width, dtype=BF),
         hold(count, width, dtype=BF), hold(count, width, dtype=BF), hold(count, ff, dtype=BF),
         hold(count, ff, dtype=BF),
         pltpu.SemaphoreType.DMA((3,)), pltpu.SemaphoreType.DMA((7,))],
        4 * count * width * (4 * width + 2 * ff),
        anywhere_outs=7,
    )
    dense_act_one, dense_d_heads, dense_mixed, dense_d_z, dense_act_two, dense_hidden, dense_d_upped = dense_kept
    d_delta = lax.ppermute(back_rows, "section", [(1, 0)])
    returned = lax.ppermute(after(back, d_delta), "section", [(1, 0)])

    back_outs = [
        *wide_outs, *wide_outs, *outs, shape(EXTRA, width), shape(EXTRA, width), shape(picked, width)]

    def routed_back():
        return call(
            functools.partial(routed_back_kernel, number, out_number),
            [place, *shards, d_delta, gate, branch, rows, z, hidden, act_two, slope, act_one, heads, chances,
             mixed, router_row, gains],
            number,
            back_outs,
            [w_first, w_up, w_down, pltpu.SemaphoreType.DMA((3,))],
            8 * picked * width * ff + 16 * picked * width * width,
        )

    def dense_back():
        return call(
            functools.partial(dense_back_kernel, out_number),
            [place, dense_hidden, cotangent, dense_act_two, dense_d_upped, dense_mixed, dense_d_z, dense_act_one,
             dense_d_heads, dense_gains],
            0, back_outs, [], 4 * count * width * ff + 8 * count * width * width,
        )

    (*pieces, router_lines, small, d_picked) = lax.cond(routed, routed_back, dense_back)
    up_pieces, first_pieces = pieces[:out_number], pieces[out_number:]
    picks = (chosen[:, :, None] == lax.iota(jnp.int32, length)[None, None, :]).astype(F32)

    def both_ends(returned, result):
        spread = jnp.einsum(
            "wgo,wgq->woq", picks, d_picked.reshape(batch, kept, width), precision=lax.Precision.HIGHEST)
        first_rows = (returned.astype(F32) + spread.reshape(count, width)).astype(BF)
        return jnp.where(routed, first_rows, result)[None]

    if sliced(n):
        pieces, returned = lax.optimization_barrier((pieces, returned))
        spot = spot_of(place[0], n // 4)
        down_sum, up_sum, first_sum = sums = [
            Sum(*pieces[i:i + 2], n, far, spot, i == 0) for i, far in zip((0, 2, 4), (FAR[2], FAR[1], FAR[0]))]
        for s in range(n // 4):
            for one in sums:
                one.step(s)
        arrived = [down_sum.arrived[d] for d in sorted(down_sum.arrived)]
        router_grad = call(
            functools.partial(router_kernel, len(arrived)),
            [place, down_sum.own, down_sum.soon, *arrived], len(arrived) + 2, [shape(1, width)],
            [hold(n // 2 + 2, EXTRA, width, dtype=BF), pltpu.SemaphoreType.DMA((n // 2 + 2,))], width,
        )[0][0]
        router_grad = router_grad + lax.ppermute(router_grad, "section", [(0, 1), (1, 0)])
        ends = both_ends(returned, result)
        down_grad, up_grad = (sum(one.total())[:part_rows] for one in (down_sum, up_sum))
        small = sum(up_sum.total())[part_rows:]
        due, last = first_sum.total((router_grad, ends, down_grad, up_grad))
        in_grad, out_grad = (due[rows] + last[rows] for rows in (slice(0, 3 * rows_in), slice(3 * rows_in, None)))
    else:
        def plain(pieces, wide):
            whole = pieces[0]
            if wide:
                whole = whole.reshape(SHARDS, 4, -1, width).transpose(1, 0, 2, 3)
                whole = whole.reshape(4, n, -1, width).transpose(1, 0, 2, 3)
            return scatter_plain(whole.reshape(n, -1, width))

        down_grad = plain(pieces[:1], False)
        up_grad, first_grad = plain(pieces[1:2], True), plain(pieces[2:], True)
        in_grad, out_grad = first_grad[:3 * rows_in], first_grad[3 * rows_in:]
        small = lax.psum(small, "dp")
        ends = both_ends(returned, result)
        router_grad = jnp.sum(lax.psum(router_lines, ("section", "dp")), axis=0)
    up_grad = up_grad.reshape(blocks, rows_in, width).transpose(1, 0, 2).reshape(rows_in, ff)
    gain_grad = lax.dynamic_slice_in_dim(small[:2], place[0] * (width // n), width // n, 1)
    return (
        ends, router_grad, gain_grad[None], in_grad.reshape(1, 3, rows_in, width), out_grad[None],
        up_grad[None], down_grad[None],
    )


def solution(mesh):
    return jax.shard_map(
        body,
        mesh=mesh,
        in_specs=(
            P("dp", None),
            P("dp", None),
            P("dp", None),
            P("dp", None),
            P(),
            P("section", None, None),
            P("section", None, "dp", None),
            P("section", "dp", None),
            P("section", "dp", None),
            P("section", "dp", None),
        ),
        out_specs=(
            P("section", "dp", None),
            P(),
            P("section", None, "dp"),
            P("section", None, "dp", None),
            P("section", "dp", None),
            P("section", "dp", None),
            P("section", "dp", None),
        ),
        check_vma=False,
    )
```

```python
import functools

import jax
import jax.numpy as jnp
from jax import lax
from jax.experimental import pallas as pl
from jax.experimental.pallas import tpu as pltpu
from jax.sharding import PartitionSpec as P

HEAD_DIM = 64
LANES = 2 * HEAD_DIM
EPSILON = 1e-05
MASKED = -1e30
BF = jnp.bfloat16
F32 = jnp.float32
VMEM_BYTES = 60 * 1024 * 1024
STRIP = 16
CODES = 16
SHARDS = 16


def move(value, pairs):
    return lax.ppermute(value, "dp", pairs)


def device_at(spot, core, depth):
    return 4 * spot + core if spot < depth else 4 * (2 * depth - 1 - spot) + 2 + core


def routes(n):
    depth = n // 4
    ring = 2 * depth

    def turned(by):
        return [
            (device_at(r, c, depth), device_at((r + by) % ring, c, depth))
            for r in range(ring) for c in range(2)
        ]

    return turned(1), turned(-1), [(i, i ^ 1) for i in range(n)]


def hops(depth, far):
    return (depth, depth - 1) if far == 0 else (depth - 1, depth)


def after(value, token):
    return lax.optimization_barrier((value, token))[0]


def sliced(n):
    return n == 16


FAR = (0, 1, 0)


def first_ways(depth, far):
    return (depth, 1 - depth) if far == 0 else (-depth, depth - 1)


def lots(depth, far):
    ahead, behind = hops(depth, far)
    early = [0] + [sign * d for d in range(1, depth // 2 + 1) for sign in (1, -1)]
    late = [d for d in range(-behind, ahead + 1) if d not in early]
    return early, late


def gather_halves(halves, n, token):
    depth = n // 4
    forward, backward, beside = routes(n)
    held = [{0: half} for half in halves]
    for s in range(1, depth + 1):
        for far, mine in enumerate(held):
            ahead, behind = hops(depth, far)
            for sign, limit, way in ((1, ahead, forward), (-1, behind, backward)):
                if s <= limit:
                    source = mine[sign * (s - 1)]
                    mine[sign * s] = move(after(source, token) if s == 2 else source, way)
    found = []
    for far, mine in enumerate(held):
        early, late = lots(depth, far)
        found += [mine[d] for d in early + late]
        found += [move(jnp.stack([mine[d] for d in some]), beside) for some in (early, late)]
    return found


EXTRA = 16


class Sum:
    def __init__(self, own, other, n, far, spot, hurry):
        self.depth = n // 4
        forward, backward, beside = routes(n)
        self.ways = (forward, backward) if far == 0 else (backward, forward)
        self.far, self.spot = far, spot
        self.own, self.soon = own, None
        if hurry:
            first_two = jnp.stack([self.block(other, d) for d in first_ways(self.depth, far)])
            self.soon = move(first_two, beside)
            other = after(other, first_two)
        self.got = move(other, beside)
        self.came = [None, None]
        self.arrived = {}

    def block(self, held, distance):
        at = lax.rem(self.spot + (2 * self.depth + distance), 2 * self.depth)
        return lax.dynamic_index_in_dim(held, at, 0, keepdims=False)

    def term(self, distance, came, got=None):
        found = self.block(self.own, distance).astype(F32)
        found = found + (self.block(self.got, distance) if got is None else got).astype(F32)
        for value in came:
            if value is not None:
                found = found + value.astype(F32)
        return found

    def step(self, s):
        signs = [1 if self.far == i else -1 for i in range(2) if s + i < self.depth]
        values = [
            self.term(sign * (self.depth - s - i), [self.came[i]], self.soon[i] if s == 0 and self.soon is not None else None)
            for i, sign in enumerate(signs)]
        values = lax.optimization_barrier([value.astype(BF) for value in values])
        for i, (sign, value) in enumerate(zip(signs, values)):
            self.came[i] = self.arrived[-sign * (s + 1)] = move(value, self.ways[i])

    def total(self, token=None):
        last = self.came[0] if token is None else after(self.came[0], token)
        return lax.optimization_barrier(self.term(0, [self.came[1]])), last.astype(F32)


def scatter_plain(whole):
    return lax.psum_scatter(whole.astype(F32), "dp", scatter_dimension=0, tiled=False)


def dot(a, b):
    return jnp.dot(a, b, preferred_element_type=F32)


def dot_t(a, b):
    return lax.dot_general(a, b, (((1,), (1,)), ((), ())), preferred_element_type=F32)


def t_dot(a, b):
    return lax.dot_general(a, b, (((0,), (0,)), ((), ())), preferred_element_type=F32)


def spot_of(me, depth):
    return jnp.where((me // 2) % 2 == 0, me // 4, 2 * depth - 1 - me // 4)


def device_on(me, distance, core, depth):
    spot = lax.rem(spot_of(me, depth) + (2 * depth + distance), 2 * depth)
    base = jnp.where(spot < depth, 4 * spot, 4 * (2 * depth - 1 - spot) + 2)
    return base + ((me % 2) ^ core)


def fetch_start(refs, holds, sems, me, names):
    if len(refs) == 3:
        for i in names:
            pltpu.make_async_copy(refs[i], holds[i], sems.at[i]).start()
        return
    count = len(refs) // 2
    depth = (count - 2) // 2
    rows = holds[0].shape[1]
    cuts = ((0, 0, 0, 0, rows), (0, 1, rows, 0, rows // 2), (1, 1, 0, rows // 2, rows // 2), (1, 2, rows // 2, 0, rows))
    for i in names:
        for far, name, source, target, size in cuts:
            if name == i:
                mine = refs[far * count:(far + 1) * count]
                early, late = lots(depth, far)
                there = pl.ds(source, size)
                pieces = [(d, 0, ref.at[there]) for d, ref in zip(early + late, mine)]
                pieces += [(d, 1, mine[-2].at[k, there]) for k, d in enumerate(early)]
                pieces += [(d, 1, mine[-1].at[k, there]) for k, d in enumerate(late)]
                for distance, core, piece in pieces:
                    origin = device_on(me, -distance, core, depth)
                    pltpu.make_async_copy(piece, holds[i].at[origin, pl.ds(target, size)], sems.at[i]).start()


def ready(hold, sem):
    pltpu.make_async_copy(hold, hold, sem).wait()


def matrix(hold, q):
    shards, _, width = hold.shape
    count = width // shards
    return hold[:, q * count:(q + 1) * count, :].reshape(width, width)


def band(hold, b):
    shards, count, width = hold.shape
    some = width // count
    return hold[b * some:(b + 1) * some].reshape(width, width)


def deal(value, outs, me, first, piece):
    rows = piece.stop - piece.start
    number = value.shape[0] // rows
    if len(outs) == 1:
        outs[0][first:first + number, piece, :] = value.reshape(number, rows, value.shape[1]).astype(BF)
        return
    own, other = outs
    ring = own.shape[0]
    for t in range(number // 2):
        even, odd = value[2 * t * rows:(2 * t + 1) * rows], value[(2 * t + 1) * rows:(2 * t + 2) * rows]
        z, x = divmod(first // 2 + t, 2)
        spot = z if x == 0 else ring - 1 - z
        own[spot, piece, :] = jnp.where(me % 2 == 0, even, odd).astype(BF)
        other[spot, piece, :] = jnp.where(me % 2 == 0, odd, even).astype(BF)


def split(line):
    high = line.astype(BF).astype(F32)
    middle = (line - high).astype(BF).astype(F32)
    return [high, middle, line - high - middle]


def deal_lines(lines, outs, small):
    value = jnp.concatenate(lines + [jnp.zeros((EXTRA - len(lines), lines[0].shape[1]), F32)], axis=0)
    small[...] = value
    if len(outs) == 2:
        for out in outs:
            for spot in range(out.shape[0]):
                out[spot, out.shape[1] - EXTRA:, :] = value.astype(BF)


def deal_router(line, outs, small, me):
    three = split(line)
    none = jnp.zeros_like(line)
    mine, other = three + [none] * (EXTRA - 3), [none] * 3 + three + [none] * (EXTRA - 6)
    small[...] = jnp.concatenate(mine, axis=0)
    if len(outs) == 2:
        ring, row = outs[0].shape[0], outs[0].shape[1] - EXTRA
        for out, value in zip(outs, (mine, other)):
            value = jnp.concatenate(value, axis=0).astype(BF)
            for spot in range(ring):
                out[spot, row:, :] = jnp.zeros(value.shape, BF)
            for distance in first_ways(ring // 2, FAR[2]):
                out[lax.rem(spot_of(me, ring // 2) + ring + distance, ring), row:, :] = value


def router_kernel(count, place, *refs):
    own, got, arrived, (out, lines, sems) = refs[0], refs[1], refs[2:count + 2], refs[count + 2:]
    me = place[0]
    ring = count + 1
    depth = ring // 2
    spot = spot_of(me, depth)
    row = own.shape[1] - EXTRA
    away = lax.rem(spot + ring + first_ways(depth, FAR[2])[0], ring)
    copies = [pltpu.make_async_copy(own.at[away, pl.ds(row, EXTRA)], lines.at[0], sems.at[0]),
              pltpu.make_async_copy(got.at[0, pl.ds(row, EXTRA)], lines.at[1], sems.at[1])]
    ahead, behind = hops(depth, FAR[2])
    distances = list(range(-ahead, 0)) + list(range(1, behind + 1))
    for i, (distance, ref) in enumerate(zip(distances, arrived)):
        slot = 2 + lax.rem(spot + ring + distance, ring)
        copies.append(pltpu.make_async_copy(ref.at[pl.ds(row, EXTRA)], lines.at[slot], sems.at[2 + i]))
    for copy in copies:
        copy.start()
    for copy in copies:
        copy.wait()
    lines[2 + spot] = lines[0] + lines[1]
    total = jnp.zeros(out.shape, F32)
    for r in range(ring):
        value = lines[2 + r].astype(F32)
        low = (value[0:1] + value[1:2]) + value[2:3]
        high = (value[3:4] + value[4:5]) + value[5:6]
        total = total + jnp.where(me % 2 == 0, low, high)
        total = total + jnp.where(me % 2 == 0, high, low)
    out[...] = total


def deal_matrix(value, outs, me, q):
    count = value.shape[0] // SHARDS
    deal(value, outs, me, 0, slice(q * count, (q + 1) * count))


def deal_down(hidden, d_out, outs, me):
    width = d_out.shape[1]
    count = hidden.shape[1] // SHARDS
    for b in range(hidden.shape[1] // width):
        value = t_dot(hidden[:, b * width:(b + 1) * width], d_out)
        deal(value, outs, me, b * (width // count), slice(0, count))


def inverse_of(rows):
    return lax.rsqrt(jnp.mean(rows * rows, axis=-1, keepdims=True) + EPSILON)


def norm_back(upstream, normed, inverse, gain):
    scaled = upstream * gain
    d_gain = jnp.sum(upstream * normed, axis=0, keepdims=True)
    d_rows = inverse * (scaled - normed * jnp.mean(scaled * normed, axis=-1, keepdims=True))
    return d_rows, d_gain


def normal_parts(value):
    whole = 0.5 + 0.5 * lax.erf(value * 0.7071067811865476)
    return whole, value * jnp.exp(value * value * -0.5) * 0.3989422804014327


def left_lanes(rows):
    return lax.broadcasted_iota(jnp.int32, (rows, LANES), 1) < HEAD_DIM


def two_heads(value):
    left = left_lanes(value.shape[0])
    zero = jnp.zeros_like(value)
    return jnp.concatenate([jnp.where(left, value, zero), jnp.where(left, zero, value)], axis=0)


def one_row(value):
    half = value.shape[0] // 2
    return jnp.where(left_lanes(half), value[:half], value[half:])


def bias_of(same):
    shape = same.shape
    order = lax.broadcasted_iota(jnp.int32, shape, 0) >= lax.broadcasted_iota(jnp.int32, shape, 1)
    return jnp.where(order & (same > 0.5), 0.0, MASKED).astype(F32)


def hot_rows(line, count):
    return (lax.broadcasted_iota(jnp.int32, (count, line.shape[1]), 0) == line).astype(BF)


def attend(groups, biases):
    size = groups[0][0].shape[0]
    scale = jnp.asarray(HEAD_DIM ** -0.5, BF)
    scores = [dot_t(two_heads(query) * scale, keyed) for query, keyed, _ in groups]
    found = []
    for value, bias in zip(scores, biases):
        value = (value.reshape(2, size, size) + bias[None]).reshape(2 * size, size)
        powers = jnp.exp(value - jnp.max(value, axis=-1, keepdims=True))
        found.append((powers * (1.0 / jnp.sum(powers, axis=-1, keepdims=True))).astype(BF))
    mixed = [one_row(dot(chances, valued)).astype(BF) for chances, (_, _, valued) in zip(found, groups)]
    return mixed, found


def attend_back(groups, mixed, chances, d_mixed):
    both = [two_heads(value) for value in d_mixed]
    d_chances = [dot_t(value, valued) for value, (_, _, valued) in zip(both, groups)]
    d_value = [t_dot(chance, value) for chance, value in zip(chances, both)]
    factor = HEAD_DIM ** -0.5
    d_scores = []
    for found, value, blend, chance in zip(d_chances, d_mixed, mixed, chances):
        overlap = jnp.sum(two_heads(value.astype(F32) * blend.astype(F32)), axis=-1, keepdims=True)
        d_scores.append((chance.astype(F32) * (found - overlap)).astype(BF))
    d_query = [one_row(dot(value, keyed)) * factor for value, (_, keyed, _) in zip(d_scores, groups)]
    d_key = [t_dot(value, two_heads(query)) * factor for value, (query, _, _) in zip(d_scores, groups)]
    return [[one.astype(BF) for one in some] for some in (d_query, d_key, d_value)]


def pairs_of(value):
    return [value[:, p:p + LANES] for p in range(0, value.shape[1], LANES)]


def lanes_of(p):
    return pl.ds(pl.multiple_of(p * LANES, LANES), LANES)


def routed_kernel(slot_count, batch, place, *refs):
    shards = refs[:slot_count]
    (tokens, spots, codes, router, gains,
     rows_o, gate_o, z_o, act_one_o, heads_o, chances_o, mixed_o, act_two_o, hidden_o, slope_o, branch_o, delta_o,
     w_first, w_up, w_down, sems) = refs[slot_count:]
    fetch_start(shards, (w_first, w_up, w_down), sems, place[0], (0, 1, 2))
    hot = hot_rows(spots[...], tokens.shape[0])
    rows = t_dot(hot, tokens[...])
    rows_o[...] = rows
    gate = jax.nn.sigmoid(jnp.sum(rows * router[...], axis=-1, keepdims=True))
    gate_o[...] = gate
    act = (rows * inverse_of(rows) * gains[0:1]).astype(BF)
    act_one_o[...] = act
    member = dot(hot_rows(codes[...], CODES * batch), hot).astype(BF)
    bias = bias_of(t_dot(member, member))
    ready(w_first, sems.at[0])
    heads = [dot(act, matrix(w_first, c)).astype(BF) for c in range(3)]
    for c in range(3):
        heads_o[c] = heads[c]
    groups = list(zip(*(pairs_of(value) for value in heads)))
    found, chances = attend(groups, [bias] * len(groups))
    for p, chance in enumerate(chances):
        chances_o[p] = chance.astype(F32)
    mixed = jnp.concatenate(found, axis=1)
    mixed_o[...] = mixed
    z = dot(mixed, matrix(w_first, 3))
    z_o[...] = z
    middle = rows + z
    act_two = (middle * inverse_of(middle) * gains[1:2]).astype(BF)
    act_two_o[...] = act_two
    ready(w_up, sems.at[1])
    ready(w_down, sems.at[2])
    width = rows.shape[1]
    for b in range(hidden_o.shape[1] // width):
        lanes = slice(b * width, (b + 1) * width)
        upped = dot(act_two, matrix(w_up, b))
        whole, dense = normal_parts(upped)
        hidden_o[:, lanes] = (upped * whole).astype(BF)
        slope_o[:, lanes] = whole + dense
    branch = z_o[...] + dot(hidden_o[...], w_down[...].reshape(hidden_o.shape[1], width))
    branch_o[...] = branch
    delta_o[...] = (gate * branch).astype(BF)


def routed_back_kernel(slot_count, out_count, place, *refs):
    shards = refs[:slot_count]
    (d_delta, gate, branch, rows, z, hidden, act_two, slope, act_one, heads, chances, mixed, router, gains) = refs[
        slot_count:slot_count + 14]
    refs = refs[slot_count + 14:]
    downs_o, ups_o, firsts_o = (refs[i * out_count:(i + 1) * out_count] for i in range(3))
    router_o, small_o, d_picked_o, w_first, w_up, w_down, sems = refs[3 * out_count:]
    me = place[0]
    fetch_start(shards, (w_first, w_up, w_down), sems, me, (2, 1, 0))
    width = rows.shape[1]
    blocks = slope.shape[1] // width
    held = rows[...]
    gated = gate[...]
    upstream = d_delta[...].astype(F32)
    gradient = gated * upstream
    d_out = gradient.astype(BF)
    deal_down(hidden, d_out, downs_o, me)
    d_logit = jnp.sum(upstream * branch[...], axis=-1, keepdims=True) * gated * (1.0 - gated)
    deal_router(jnp.sum(d_logit * held, axis=0, keepdims=True), downs_o, router_o, me)
    ready(w_down, sems.at[2])
    d_upped = []
    for b in range(blocks):
        d_hidden = dot_t(d_out, band(w_down, b))
        d_upped.append((d_hidden * slope[:, b * width:(b + 1) * width]).astype(BF))
    ready(w_up, sems.at[1])
    d_act = jnp.zeros(rows.shape, F32)
    for b in range(blocks):
        d_act = d_act + dot_t(d_upped[b], matrix(w_up, b))
    middle = held + z[...]
    inverse = inverse_of(middle)
    d_middle, g_two = norm_back(d_act, middle * inverse, inverse, gains[1:2])
    d_z = (gradient + d_middle).astype(BF)
    ready(w_first, sems.at[0])
    d_mixed = dot_t(d_z, matrix(w_first, 3)).astype(BF)
    for b in range(blocks):
        deal_matrix(t_dot(act_two[...], d_upped[b]), ups_o, me, b)
    blend = mixed[...]
    groups = list(zip(*(pairs_of(heads[c]) for c in range(3))))
    found = attend_back(
        groups, pairs_of(blend), [chances[p].astype(BF) for p in range(len(groups))], pairs_of(d_mixed))
    deal_matrix(t_dot(blend, d_z), firsts_o, me, 3)
    d_heads = [jnp.concatenate(one, axis=1) for one in found]
    d_act = jnp.zeros(rows.shape, F32)
    for c in range(3):
        d_act = d_act + dot_t(d_heads[c], matrix(w_first, c))
    for c in range(3):
        deal_matrix(t_dot(act_one[...], d_heads[c]), firsts_o, me, c)
    inverse = inverse_of(held)
    d_rows, g_one = norm_back(d_act, held * inverse, inverse, gains[0:1])
    d_picked_o[...] = d_rows + d_middle + d_logit * router[...]
    deal_lines([g_one, g_two], ups_o, small_o)


def dense_kernel(slot_count, place, *refs):
    shards = refs[:slot_count]
    (tokens, cotangent, delta, spots, segments, gains,
     result_o, back_o, picked_o, gain_o,
     act_one_o, d_heads_o, mixed_o, d_z_o, act_two_o, hidden_o, d_upped_o,
     w_first, w_up, w_down, rows, z, heads, chances, bias, fed, d_act, upped, d_hidden, d_mixed,
     act_one, d_heads, mixed, d_z, act_two, hidden, d_upped, sems, out_sems) = refs[slot_count:]
    holds = (w_first, w_up, w_down)
    fetch_start(shards, holds, sems, place[0], (0,))
    batch, length, _ = bias.shape
    width = tokens.shape[1]
    pairs = width // LANES
    blocks = hidden.shape[1] // width
    parts = [slice(s * length, (s + 1) * length) for s in range(batch)]
    copies = [
        pltpu.make_async_copy(held, out, out_sems.at[i])
        for i, (held, out) in enumerate((
            (act_one, act_one_o), (d_heads, d_heads_o), (mixed, mixed_o), (d_z, d_z_o),
            (act_two, act_two_o), (hidden, hidden_o), (d_upped, d_upped_o),
        ))
    ]

    hot = hot_rows(spots[...], tokens.shape[0])
    for s, part in enumerate(parts):
        held = tokens[part].astype(F32) + dot(hot[part], delta[...])
        rows[part] = held
        act_one[part] = (held * inverse_of(held) * gains[0:1]).astype(BF)
        member = hot_rows(segments[:, part], CODES)
        bias[s] = bias_of(t_dot(member, member))
    copies[0].start()
    ready(w_first, sems.at[0])
    for c in range(3):
        for part in parts:
            heads[c, part] = dot(act_one[part], matrix(w_first, c)).astype(BF)
    fetch_start(shards, holds, sems, place[0], (1, 2))

    def forward(p, carry):
        lanes = lanes_of(p)
        groups = [tuple(heads[c, part, lanes] for c in range(3)) for part in parts]
        blends, found = attend(groups, [bias[s] for s in range(batch)])
        for s, part in enumerate(parts):
            mixed[part, lanes] = blends[s]
            chances[s, p] = found[s]
        return carry

    lax.fori_loop(0, pairs, forward, 0)
    copies[2].start()
    for part in parts:
        attended = dot(mixed[part], matrix(w_first, 3))
        z[part] = attended
        middle = rows[part] + attended
        act_two[part] = (middle * inverse_of(middle) * gains[1:2]).astype(BF)
    copies[4].start()
    ready(w_up, sems.at[1])
    ready(w_down, sems.at[2])
    fed[...] = jnp.zeros(fed.shape, F32)
    d_act[...] = jnp.zeros(d_act.shape, F32)

    for b in range(blocks):
        lanes = slice(b * width, (b + 1) * width)
        for s, part in enumerate(parts):
            upped[...] = dot(act_two[part], matrix(w_up, b))
            d_hidden[...] = dot_t(cotangent[part], band(w_down, b))

            for r in range(length // STRIP):
                spot = slice(r * STRIP, (r + 1) * STRIP)
                there = slice(s * length + r * STRIP, s * length + (r + 1) * STRIP)
                for side in range(2):
                    cut = slice(side * width // 2, (side + 1) * width // 2)
                    out = slice(b * width + side * width // 2, b * width + (side + 1) * width // 2)
                    value = upped[spot, cut]
                    whole, dense = normal_parts(value)
                    hidden[there, out] = (value * whole).astype(BF)
                    d_upped[there, out] = (d_hidden[spot, cut] * (whole + dense)).astype(BF)
            fed[part] += dot(hidden[part, lanes], band(w_down, b))
            d_act[part] += dot_t(d_upped[part, lanes], matrix(w_up, b))
    copies[5].start()
    copies[6].start()
    gain = jnp.zeros((1, width), F32)
    for part in parts:
        result_o[part] = (rows[part] + z[part] + fed[part]).astype(BF)
        middle = rows[part] + z[part]
        inverse = inverse_of(middle)
        d_middle, more = norm_back(d_act[part], middle * inverse, inverse, gains[1:2])
        gain = gain + more
        held = cotangent[part].astype(F32) + d_middle
        d_act[part] = held
        d_z[part] = held.astype(BF)
        d_mixed[part] = dot_t(held.astype(BF), matrix(w_first, 3)).astype(BF)
    gain_o[1:2] = gain
    copies[3].start()

    def backward(p, carry):
        lanes = lanes_of(p)
        groups = [tuple(heads[c, part, lanes] for c in range(3)) for part in parts]
        found = attend_back(
            groups, [mixed[part, lanes] for part in parts], [chances[s, p] for s in range(batch)],
            [d_mixed[part, lanes] for part in parts])
        for c in range(3):
            for s, part in enumerate(parts):
                d_heads[c, part, lanes] = found[c][s]
        return carry

    lax.fori_loop(0, pairs, backward, 0)
    copies[1].start()
    gain = jnp.zeros((1, width), F32)
    for s, part in enumerate(parts):
        d_first = dot_t(d_heads[0, part], matrix(w_first, 0))
        d_first = d_first + dot_t(d_heads[1, part], matrix(w_first, 1))
        d_first = d_first + dot_t(d_heads[2, part], matrix(w_first, 2))
        held = rows[part]
        inverse = inverse_of(held)
        d_rows, more = norm_back(d_first, held * inverse, inverse, gains[0:1])
        gain = gain + more
        back_o[part] = (d_act[part] + d_rows).astype(BF)
    picked_o[...] = t_dot(hot, back_o[...]).astype(BF)
    gain_o[0:1] = gain
    for copy in copies:
        copy.wait()


def dense_back_kernel(out_count, place, hidden, d_out, act_two, d_upped, mixed, d_z, act_one, d_heads, gains, *refs):
    downs_o, ups_o, firsts_o = (refs[i * out_count:(i + 1) * out_count] for i in range(3))
    router_o, small_o, d_picked_o = refs[3 * out_count:]
    me = place[0]
    deal_down(hidden, d_out[...], downs_o, me)
    deal_router(jnp.zeros((1, d_out.shape[1]), F32), downs_o, router_o, me)
    d_picked_o[...] = jnp.zeros(d_picked_o.shape, F32)
    width = act_two.shape[1]
    for b in range(d_upped.shape[1] // width):
        deal_matrix(t_dot(act_two[...], d_upped[:, b * width:(b + 1) * width]), ups_o, me, b)
    deal_matrix(t_dot(mixed[...], d_z[...]), firsts_o, me, 3)
    for c in range(3):
        deal_matrix(t_dot(act_one[...], d_heads[c]), firsts_o, me, c)
    deal_lines([gains[0:1], gains[1:2]], ups_o, small_o)


def call(kernel, inputs, anywhere, outs, scratch, flops, anywhere_outs=0):
    vmem = pl.BlockSpec(memory_space=pltpu.VMEM)
    hbm = pl.BlockSpec(memory_space=pltpu.HBM)
    specs = [pl.BlockSpec(memory_space=pltpu.SMEM)] + [hbm] * anywhere
    specs = specs + [vmem] * (len(inputs) - len(specs))
    moved = sum(v.size * v.dtype.itemsize for v in inputs) + sum(
        o.size * jnp.dtype(o.dtype).itemsize for o in outs)
    return tuple(pl.pallas_call(
        kernel,
        out_shape=outs,
        in_specs=specs,
        out_specs=[vmem] * (len(outs) - anywhere_outs) + [hbm] * anywhere_outs,
        scratch_shapes=scratch,
        compiler_params=pltpu.CompilerParams(vmem_limit_bytes=VMEM_BYTES),
        cost_estimate=pl.CostEstimate(flops=flops, bytes_accessed=moved, transcendentals=0),
    )(*inputs))


def body(
    tokens, cotangent, segments, chosen, router, norm_gains, attn_in, attn_out, ff_up, ff_down
):
    n = lax.axis_size("dp")
    routed = lax.axis_index("section") == 0
    place = lax.axis_index("dp").astype(jnp.int32).reshape(1)
    batch, length = segments.shape
    width = tokens.shape[1]
    kept = chosen.shape[1]
    rows_in, rows_down, ff = attn_in.shape[2], ff_down.shape[1], ff_up.shape[2]
    blocks, pairs = ff // width, width // LANES
    picked, count = batch * kept, batch * length
    gains = norm_gains[0]
    router_row = router[None]

    def shape(*dims, dtype=F32):
        return jax.ShapeDtypeStruct(dims, dtype)

    def hold(*dims, dtype=F32):
        return pltpu.VMEM(dims, dtype)

    first_part = jnp.concatenate([attn_in[0].reshape(-1, width), attn_out[0]])
    up_part = jnp.concatenate([ff_up[0][:, b * width:(b + 1) * width] for b in range(blocks)])
    parts = [first_part, up_part, ff_down[0]]
    part_rows = 4 * width // SHARDS
    order = lax.iota(jnp.int32, batch)[:, None]
    spots = (chosen + order * length).reshape(1, picked)
    lines = segments.reshape(1, count)
    codes = (segments + order * CODES).reshape(1, count)
    if sliced(n):
        half = part_rows // 2
        halves = [jnp.concatenate([first_part, up_part[:half]]), jnp.concatenate([up_part[half:], ff_down[0]])]
        shards = gather_halves(halves, n, (spots, lines, codes))
        outs, wide_outs = (
            [shape(n // 2, part_rows + more, width, dtype=BF)] * 2 for more in (0, EXTRA))
    else:
        first, up, down = (lax.all_gather(part, "dp", axis=0) for part in parts)

        def dealt(value):
            value = value.reshape(n, 4, rows_in, width).transpose(1, 0, 2, 3)
            value = value.reshape(4, SHARDS, width // SHARDS, width).transpose(1, 0, 2, 3)
            return value.reshape(SHARDS, part_rows, width)

        shards = [dealt(first), dealt(up), down.reshape(SHARDS, part_rows, width)]
        outs = wide_outs = [shape(SHARDS, part_rows, width, dtype=BF)]
    number, out_number = len(shards), len(outs)
    w_first = w_up = w_down = hold(SHARDS, part_rows, width, dtype=BF)

    (rows, gate, z, act_one, heads, chances, mixed, act_two, hidden, slope, branch, delta) = call(
        functools.partial(routed_kernel, number, batch),
        [place, *shards, tokens, spots, codes, router_row, gains],
        number,
        [shape(picked, width), shape(picked, 1), shape(picked, width), shape(picked, width, dtype=BF),
         shape(3, picked, width, dtype=BF), shape(pairs, 2 * picked, picked),
         shape(picked, width, dtype=BF), shape(picked, width, dtype=BF), shape(picked, ff, dtype=BF),
         shape(picked, ff), shape(picked, width), shape(picked, width, dtype=BF)],
        [w_first, w_up, w_down, pltpu.SemaphoreType.DMA((3,))],
        4 * picked * width * (2 * width + ff),
    )
    arrived = lax.ppermute(delta, "section", [(0, 1)])

    (result, back, back_rows, dense_gains, *dense_kept) = call(
        functools.partial(dense_kernel, number),
        [place, *shards, tokens, cotangent, arrived, spots, lines, gains],
        number,
        [shape(count, width, dtype=BF), shape(count, width, dtype=BF), shape(picked, width, dtype=BF),
         shape(2, width),
         shape(count, width, dtype=BF), shape(3, count, width, dtype=BF), shape(count, width, dtype=BF),
         shape(count, width, dtype=BF), shape(count, width, dtype=BF), shape(count, ff, dtype=BF),
         shape(count, ff, dtype=BF)],
        [w_first, w_up, w_down, hold(count, width), hold(count, width), hold(3, count, width, dtype=BF),
         hold(batch, pairs, 2 * length, length, dtype=BF), hold(batch, length, length),
         hold(count, width), hold(count, width), hold(length, width), hold(length, width),
         hold(count, width, dtype=BF),
         hold(count, width, dtype=BF), hold(3, count, width, dtype=BF), hold(count, width, dtype=BF),
         hold(count, width, dtype=BF), hold(count, width, dtype=BF), hold(count, ff, dtype=BF),
         hold(count, ff, dtype=BF),
         pltpu.SemaphoreType.DMA((3,)), pltpu.SemaphoreType.DMA((7,))],
        4 * count * width * (4 * width + 2 * ff),
        anywhere_outs=7,
    )
    dense_act_one, dense_d_heads, dense_mixed, dense_d_z, dense_act_two, dense_hidden, dense_d_upped = dense_kept
    d_delta = lax.ppermute(back_rows, "section", [(1, 0)])
    returned = lax.ppermute(after(back, d_delta), "section", [(1, 0)])

    back_outs = [
        *wide_outs, *wide_outs, *outs, shape(EXTRA, width), shape(EXTRA, width), shape(picked, width)]

    def routed_back():
        return call(
            functools.partial(routed_back_kernel, number, out_number),
            [place, *shards, d_delta, gate, branch, rows, z, hidden, act_two, slope, act_one, heads, chances,
             mixed, router_row, gains],
            number,
            back_outs,
            [w_first, w_up, w_down, pltpu.SemaphoreType.DMA((3,))],
            8 * picked * width * ff + 16 * picked * width * width,
        )

    def dense_back():
        return call(
            functools.partial(dense_back_kernel, out_number),
            [place, dense_hidden, cotangent, dense_act_two, dense_d_upped, dense_mixed, dense_d_z, dense_act_one,
             dense_d_heads, dense_gains],
            0, back_outs, [], 4 * count * width * ff + 8 * count * width * width,
        )

    (*pieces, router_lines, small, d_picked) = lax.cond(routed, routed_back, dense_back)
    up_pieces, first_pieces = pieces[:out_number], pieces[out_number:]
    picks = (chosen[:, :, None] == lax.iota(jnp.int32, length)[None, None, :]).astype(F32)

    def both_ends(returned, result):
        spread = jnp.einsum(
            "wgo,wgq->woq", picks, d_picked.reshape(batch, kept, width), precision=lax.Precision.HIGHEST)
        first_rows = (returned.astype(F32) + spread.reshape(count, width)).astype(BF)
        return jnp.where(routed, first_rows, result)[None]

    if sliced(n):
        pieces, returned = lax.optimization_barrier((pieces, returned))
        spot = spot_of(place[0], n // 4)
        down_sum, up_sum, first_sum = sums = [
            Sum(*pieces[i:i + 2], n, far, spot, i == 0) for i, far in zip((0, 2, 4), (FAR[2], FAR[1], FAR[0]))]
        for s in range(n // 4):
            for one in sums:
                one.step(s)
        arrived = [down_sum.arrived[d] for d in sorted(down_sum.arrived)]
        router_grad = call(
            functools.partial(router_kernel, len(arrived)),
            [place, down_sum.own, down_sum.soon, *arrived], len(arrived) + 2, [shape(1, width)],
            [hold(n // 2 + 2, EXTRA, width, dtype=BF), pltpu.SemaphoreType.DMA((n // 2 + 2,))], width,
        )[0][0]
        router_grad = router_grad + lax.ppermute(router_grad, "section", [(0, 1), (1, 0)])
        ends = both_ends(returned, result)
        down_grad, up_grad = (sum(one.total())[:part_rows] for one in (down_sum, up_sum))
        small = sum(up_sum.total())[part_rows:]
        due, last = first_sum.total((router_grad, ends, down_grad, up_grad))
        in_grad, out_grad = (due[rows] + last[rows] for rows in (slice(0, 3 * rows_in), slice(3 * rows_in, None)))
    else:
        def plain(pieces, wide):
            whole = pieces[0]
            if wide:
                whole = whole.reshape(SHARDS, 4, -1, width).transpose(1, 0, 2, 3)
                whole = whole.reshape(4, n, -1, width).transpose(1, 0, 2, 3)
            return scatter_plain(whole.reshape(n, -1, width))

        down_grad = plain(pieces[:1], False)
        up_grad, first_grad = plain(pieces[1:2], True), plain(pieces[2:], True)
        in_grad, out_grad = first_grad[:3 * rows_in], first_grad[3 * rows_in:]
        small = lax.psum(small, "dp")
        ends = both_ends(returned, result)
        router_grad = jnp.sum(lax.psum(router_lines, ("section", "dp")), axis=0)
    up_grad = up_grad.reshape(blocks, rows_in, width).transpose(1, 0, 2).reshape(rows_in, ff)
    gain_grad = lax.dynamic_slice_in_dim(small[:2], place[0] * (width // n), width // n, 1)
    return (
        ends, router_grad, gain_grad[None], in_grad.reshape(1, 3, rows_in, width), out_grad[None],
        up_grad[None], down_grad[None],
    )


def solution(mesh):
    return jax.shard_map(
        body,
        mesh=mesh,
        in_specs=(
            P("dp", None),
            P("dp", None),
            P("dp", None),
            P("dp", None),
            P(),
            P("section", None, None),
            P("section", None, "dp", None),
            P("section", "dp", None),
            P("section", "dp", None),
            P("section", "dp", None),
        ),
        out_specs=(
            P("section", "dp", None),
            P(),
            P("section", None, "dp"),
            P("section", None, "dp", None),
            P("section", "dp", None),
            P("section", "dp", None),
            P("section", "dp", None),
        ),
        check_vma=False,
    )
```

```python
import functools

import jax
import jax.numpy as jnp
from jax import lax
from jax.experimental import pallas as pl
from jax.experimental.pallas import tpu as pltpu
from jax.sharding import PartitionSpec as P

HEAD_DIM = 64
LANES = 2 * HEAD_DIM
EPSILON = 1e-05
MASKED = -1e30
BF = jnp.bfloat16
F32 = jnp.float32
MIB = 1024 * 1024
DENSE_MIB = 60
STRIP = 16
CODES = 16
SHARDS = 16


def move(value, pairs):
    return lax.ppermute(value, "dp", pairs)


def device_at(spot, core, depth):
    return 4 * spot + core if spot < depth else 4 * (2 * depth - 1 - spot) + 2 + core


def routes(n):
    depth = n // 4
    ring = 2 * depth

    def turned(by):
        return [
            (device_at(r, c, depth), device_at((r + by) % ring, c, depth))
            for r in range(ring) for c in range(2)
        ]

    return turned(1), turned(-1), [(i, i ^ 1) for i in range(n)]


def hops(depth, far):
    return (depth, depth - 1) if far == 0 else (depth - 1, depth)


def after(value, token):
    return lax.optimization_barrier((value, token))[0]


def sliced(n):
    return n == 16


FAR = (0, 1, 0)


def first_ways(depth, far):
    return (depth, 1 - depth) if far == 0 else (-depth, depth - 1)


def lots(depth, far):
    ahead, behind = hops(depth, far)
    early = [0] + [sign * d for d in range(1, depth // 2 + 1) for sign in (1, -1)]
    late = [d for d in range(-behind, ahead + 1) if d not in early]
    return early, late


def gather_halves(halves, n, token):
    depth = n // 4
    forward, backward, beside = routes(n)
    held = [{0: half} for half in halves]
    for s in range(1, depth + 1):
        for far, mine in enumerate(held):
            ahead, behind = hops(depth, far)
            for sign, limit, way in ((1, ahead, forward), (-1, behind, backward)):
                if s <= limit:
                    source = mine[sign * (s - 1)]
                    mine[sign * s] = move(after(source, token) if s == 2 else source, way)
    found = []
    for far, mine in enumerate(held):
        early, late = lots(depth, far)
        found += [mine[d] for d in early + late]
        found += [move(jnp.stack([mine[d] for d in some]), beside) for some in (early, late)]
    return found


EXTRA = 16


class Sum:
    def __init__(self, own, other, n, far, spot, hurry):
        self.depth = n // 4
        forward, backward, beside = routes(n)
        self.ways = (forward, backward) if far == 0 else (backward, forward)
        self.far, self.spot = far, spot
        self.own, self.soon = own, None
        if hurry:
            first_two = jnp.stack([self.block(other, d) for d in first_ways(self.depth, far)])
            self.soon = move(first_two, beside)
            other = after(other, first_two)
        self.got = move(other, beside)
        self.came = [None, None]
        self.arrived = {}

    def block(self, held, distance):
        at = lax.rem(self.spot + (2 * self.depth + distance), 2 * self.depth)
        return lax.dynamic_index_in_dim(held, at, 0, keepdims=False)

    def term(self, distance, came, got=None):
        found = self.block(self.own, distance).astype(F32)
        found = found + (self.block(self.got, distance) if got is None else got).astype(F32)
        for value in came:
            if value is not None:
                found = found + value.astype(F32)
        return found

    def step(self, s):
        signs = [1 if self.far == i else -1 for i in range(2) if s + i < self.depth]
        values = [
            self.term(sign * (self.depth - s - i), [self.came[i]], self.soon[i] if s == 0 and self.soon is not None else None)
            for i, sign in enumerate(signs)]
        values = lax.optimization_barrier([value.astype(BF) for value in values])
        for i, (sign, value) in enumerate(zip(signs, values)):
            self.came[i] = self.arrived[-sign * (s + 1)] = move(value, self.ways[i])

    def total(self, token=None):
        last = self.came[0] if token is None else after(self.came[0], token)
        return lax.optimization_barrier(self.term(0, [self.came[1]])), last.astype(F32)


def scatter_plain(whole):
    return lax.psum_scatter(whole.astype(F32), "dp", scatter_dimension=0, tiled=False)


def dot(a, b):
    return jnp.dot(a, b, preferred_element_type=F32)


def dot_t(a, b):
    return lax.dot_general(a, b, (((1,), (1,)), ((), ())), preferred_element_type=F32)


def t_dot(a, b):
    return lax.dot_general(a, b, (((0,), (0,)), ((), ())), preferred_element_type=F32)


def spot_of(me, depth):
    return jnp.where((me // 2) % 2 == 0, me // 4, 2 * depth - 1 - me // 4)


def device_on(me, distance, core, depth):
    spot = lax.rem(spot_of(me, depth) + (2 * depth + distance), 2 * depth)
    base = jnp.where(spot < depth, 4 * spot, 4 * (2 * depth - 1 - spot) + 2)
    return base + ((me % 2) ^ core)


def fetch_start(refs, holds, sems, me, names):
    if len(refs) == 3:
        for i in names:
            pltpu.make_async_copy(refs[i], holds[i], sems.at[i]).start()
        return
    count = len(refs) // 2
    depth = (count - 2) // 2
    rows = holds[0].shape[1]
    cuts = ((0, 0, 0, 0, rows), (0, 1, rows, 0, rows // 2), (1, 1, 0, rows // 2, rows // 2), (1, 2, rows // 2, 0, rows))
    for i in names:
        for far, name, source, target, size in cuts:
            if name == i:
                mine = refs[far * count:(far + 1) * count]
                early, late = lots(depth, far)
                there = pl.ds(source, size)
                pieces = [(d, 0, ref.at[there]) for d, ref in zip(early + late, mine)]
                pieces += [(d, 1, mine[-2].at[k, there]) for k, d in enumerate(early)]
                pieces += [(d, 1, mine[-1].at[k, there]) for k, d in enumerate(late)]
                for distance, core, piece in pieces:
                    origin = device_on(me, -distance, core, depth)
                    pltpu.make_async_copy(piece, holds[i].at[origin, pl.ds(target, size)], sems.at[i]).start()


def ready(hold, sem):
    pltpu.make_async_copy(hold, hold, sem).wait()


def matrix(hold, q):
    shards, _, width = hold.shape
    count = width // shards
    return hold[:, q * count:(q + 1) * count, :].reshape(width, width)


def band(hold, b):
    shards, count, width = hold.shape
    some = width // count
    return hold[b * some:(b + 1) * some].reshape(width, width)


def deal(value, outs, me, first, piece):
    rows = piece.stop - piece.start
    number = value.shape[0] // rows
    if len(outs) == 1:
        outs[0][first:first + number, piece, :] = value.reshape(number, rows, value.shape[1]).astype(BF)
        return
    own, other = outs
    ring = own.shape[0]
    for t in range(number // 2):
        even, odd = value[2 * t * rows:(2 * t + 1) * rows], value[(2 * t + 1) * rows:(2 * t + 2) * rows]
        z, x = divmod(first // 2 + t, 2)
        spot = z if x == 0 else ring - 1 - z
        own[spot, piece, :] = jnp.where(me % 2 == 0, even, odd).astype(BF)
        other[spot, piece, :] = jnp.where(me % 2 == 0, odd, even).astype(BF)


def split(line):
    high = line.astype(BF).astype(F32)
    middle = (line - high).astype(BF).astype(F32)
    return [high, middle, line - high - middle]


def deal_lines(lines, outs, small):
    value = jnp.concatenate(lines + [jnp.zeros((EXTRA - len(lines), lines[0].shape[1]), F32)], axis=0)
    small[...] = value
    if len(outs) == 2:
        for out in outs:
            for spot in range(out.shape[0]):
                out[spot, out.shape[1] - EXTRA:, :] = value.astype(BF)


def deal_router(line, outs, small, me):
    three = split(line)
    none = jnp.zeros_like(line)
    mine, other = three + [none] * (EXTRA - 3), [none] * 3 + three + [none] * (EXTRA - 6)
    small[...] = jnp.concatenate(mine, axis=0)
    if len(outs) == 2:
        ring, row = outs[0].shape[0], outs[0].shape[1] - EXTRA
        for out, value in zip(outs, (mine, other)):
            value = jnp.concatenate(value, axis=0).astype(BF)
            for spot in range(ring):
                out[spot, row:, :] = jnp.zeros(value.shape, BF)
            for distance in first_ways(ring // 2, FAR[2]):
                out[lax.rem(spot_of(me, ring // 2) + ring + distance, ring), row:, :] = value


def router_kernel(count, place, *refs):
    own, got, arrived, (out, lines, sems) = refs[0], refs[1], refs[2:count + 2], refs[count + 2:]
    me = place[0]
    ring = count + 1
    depth = ring // 2
    spot = spot_of(me, depth)
    row = own.shape[1] - EXTRA
    away = lax.rem(spot + ring + first_ways(depth, FAR[2])[0], ring)
    copies = [pltpu.make_async_copy(own.at[away, pl.ds(row, EXTRA)], lines.at[0], sems.at[0]),
              pltpu.make_async_copy(got.at[0, pl.ds(row, EXTRA)], lines.at[1], sems.at[1])]
    ahead, behind = hops(depth, FAR[2])
    distances = list(range(-ahead, 0)) + list(range(1, behind + 1))
    for i, (distance, ref) in enumerate(zip(distances, arrived)):
        slot = 2 + lax.rem(spot + ring + distance, ring)
        copies.append(pltpu.make_async_copy(ref.at[pl.ds(row, EXTRA)], lines.at[slot], sems.at[2 + i]))
    for copy in copies:
        copy.start()
    for copy in copies:
        copy.wait()
    lines[2 + spot] = lines[0] + lines[1]
    total = jnp.zeros(out.shape, F32)
    for r in range(ring):
        value = lines[2 + r].astype(F32)
        low = (value[0:1] + value[1:2]) + value[2:3]
        high = (value[3:4] + value[4:5]) + value[5:6]
        total = total + jnp.where(me % 2 == 0, low, high)
        total = total + jnp.where(me % 2 == 0, high, low)
    out[...] = total


def deal_matrix(value, outs, me, q):
    count = value.shape[0] // SHARDS
    deal(value, outs, me, 0, slice(q * count, (q + 1) * count))


def deal_down(hidden, d_out, outs, me):
    width = d_out.shape[1]
    count = hidden.shape[1] // SHARDS
    for b in range(hidden.shape[1] // width):
        value = t_dot(hidden[:, b * width:(b + 1) * width], d_out)
        deal(value, outs, me, b * (width // count), slice(0, count))


def inverse_of(rows):
    return lax.rsqrt(jnp.mean(rows * rows, axis=-1, keepdims=True) + EPSILON)


def norm_back(upstream, normed, inverse, gain):
    scaled = upstream * gain
    d_gain = jnp.sum(upstream * normed, axis=0, keepdims=True)
    d_rows = inverse * (scaled - normed * jnp.mean(scaled * normed, axis=-1, keepdims=True))
    return d_rows, d_gain


def normal_parts(value):
    whole = 0.5 + 0.5 * lax.erf(value * 0.7071067811865476)
    return whole, value * jnp.exp(value * value * -0.5) * 0.3989422804014327


def left_lanes(rows):
    return lax.broadcasted_iota(jnp.int32, (rows, LANES), 1) < HEAD_DIM


def two_heads(value):
    left = left_lanes(value.shape[0])
    zero = jnp.zeros_like(value)
    return jnp.concatenate([jnp.where(left, value, zero), jnp.where(left, zero, value)], axis=0)


def one_row(value):
    half = value.shape[0] // 2
    return jnp.where(left_lanes(half), value[:half], value[half:])


def bias_of(same):
    shape = same.shape
    order = lax.broadcasted_iota(jnp.int32, shape, 0) >= lax.broadcasted_iota(jnp.int32, shape, 1)
    return jnp.where(order & (same > 0.5), 0.0, MASKED).astype(F32)


def hot_rows(line, count):
    return (lax.broadcasted_iota(jnp.int32, (count, line.shape[1]), 0) == line).astype(BF)


def attend(groups, biases):
    size = groups[0][0].shape[0]
    scale = jnp.asarray(HEAD_DIM ** -0.5, BF)
    scores = [dot_t(two_heads(query) * scale, keyed) for query, keyed, _ in groups]
    found = []
    for value, bias in zip(scores, biases):
        value = (value.reshape(2, size, size) + bias[None]).reshape(2 * size, size)
        powers = jnp.exp(value - jnp.max(value, axis=-1, keepdims=True))
        found.append((powers * (1.0 / jnp.sum(powers, axis=-1, keepdims=True))).astype(BF))
    mixed = [one_row(dot(chances, valued)).astype(BF) for chances, (_, _, valued) in zip(found, groups)]
    return mixed, found


def attend_back(groups, mixed, chances, d_mixed):
    both = [two_heads(value) for value in d_mixed]
    d_chances = [dot_t(value, valued) for value, (_, _, valued) in zip(both, groups)]
    d_value = [t_dot(chance, value) for chance, value in zip(chances, both)]
    factor = HEAD_DIM ** -0.5
    d_scores = []
    for found, value, blend, chance in zip(d_chances, d_mixed, mixed, chances):
        overlap = jnp.sum(two_heads(value.astype(F32) * blend.astype(F32)), axis=-1, keepdims=True)
        d_scores.append((chance.astype(F32) * (found - overlap)).astype(BF))
    d_query = [one_row(dot(value, keyed)) * factor for value, (_, keyed, _) in zip(d_scores, groups)]
    d_key = [t_dot(value, two_heads(query)) * factor for value, (query, _, _) in zip(d_scores, groups)]
    return [[one.astype(BF) for one in some] for some in (d_query, d_key, d_value)]


def pairs_of(value):
    return [value[:, p:p + LANES] for p in range(0, value.shape[1], LANES)]


def lanes_of(p):
    return pl.ds(pl.multiple_of(p * LANES, LANES), LANES)


def routed_kernel(slot_count, batch, place, *refs):
    shards = refs[:slot_count]
    (tokens, spots, codes, router, gains,
     rows_o, gate_o, z_o, act_one_o, heads_o, chances_o, mixed_o, act_two_o, hidden_o, slope_o, branch_o, delta_o,
     w_first, w_up, w_down, sems) = refs[slot_count:]
    fetch_start(shards, (w_first, w_up, w_down), sems, place[0], (0, 1, 2))
    hot = hot_rows(spots[...], tokens.shape[0])
    rows = t_dot(hot, tokens[...])
    rows_o[...] = rows
    gate = jax.nn.sigmoid(jnp.sum(rows * router[...], axis=-1, keepdims=True))
    gate_o[...] = gate
    act = (rows * inverse_of(rows) * gains[0:1]).astype(BF)
    act_one_o[...] = act
    member = dot(hot_rows(codes[...], CODES * batch), hot).astype(BF)
    bias = bias_of(t_dot(member, member))
    ready(w_first, sems.at[0])
    heads = [dot(act, matrix(w_first, c)).astype(BF) for c in range(3)]
    for c in range(3):
        heads_o[c] = heads[c]
    groups = list(zip(*(pairs_of(value) for value in heads)))
    found, chances = attend(groups, [bias] * len(groups))
    for p, chance in enumerate(chances):
        chances_o[p] = chance.astype(F32)
    mixed = jnp.concatenate(found, axis=1)
    mixed_o[...] = mixed
    z = dot(mixed, matrix(w_first, 3))
    z_o[...] = z
    middle = rows + z
    act_two = (middle * inverse_of(middle) * gains[1:2]).astype(BF)
    act_two_o[...] = act_two
    ready(w_up, sems.at[1])
    ready(w_down, sems.at[2])
    width = rows.shape[1]
    for b in range(hidden_o.shape[1] // width):
        lanes = slice(b * width, (b + 1) * width)
        upped = dot(act_two, matrix(w_up, b))
        whole, dense = normal_parts(upped)
        hidden_o[:, lanes] = (upped * whole).astype(BF)
        slope_o[:, lanes] = whole + dense
    branch = z_o[...] + dot(hidden_o[...], w_down[...].reshape(hidden_o.shape[1], width))
    branch_o[...] = branch
    delta_o[...] = (gate * branch).astype(BF)


def routed_back_kernel(slot_count, out_count, place, *refs):
    shards = refs[:slot_count]
    (d_delta, gate, branch, rows, z, hidden, act_two, slope, act_one, heads, chances, mixed, router, gains) = refs[
        slot_count:slot_count + 14]
    refs = refs[slot_count + 14:]
    downs_o, ups_o, firsts_o = (refs[i * out_count:(i + 1) * out_count] for i in range(3))
    router_o, small_o, d_picked_o, w_first, w_up, w_down, sems = refs[3 * out_count:]
    me = place[0]
    fetch_start(shards, (w_first, w_up, w_down), sems, me, (2, 1, 0))
    width = rows.shape[1]
    blocks = slope.shape[1] // width
    held = rows[...]
    gated = gate[...]
    upstream = d_delta[...].astype(F32)
    gradient = gated * upstream
    d_out = gradient.astype(BF)
    deal_down(hidden, d_out, downs_o, me)
    d_logit = jnp.sum(upstream * branch[...], axis=-1, keepdims=True) * gated * (1.0 - gated)
    deal_router(jnp.sum(d_logit * held, axis=0, keepdims=True), downs_o, router_o, me)
    ready(w_down, sems.at[2])
    d_upped = []
    for b in range(blocks):
        d_hidden = dot_t(d_out, band(w_down, b))
        d_upped.append((d_hidden * slope[:, b * width:(b + 1) * width]).astype(BF))
    ready(w_up, sems.at[1])
    d_act = jnp.zeros(rows.shape, F32)
    for b in range(blocks):
        d_act = d_act + dot_t(d_upped[b], matrix(w_up, b))
    middle = held + z[...]
    inverse = inverse_of(middle)
    d_middle, g_two = norm_back(d_act, middle * inverse, inverse, gains[1:2])
    d_z = (gradient + d_middle).astype(BF)
    ready(w_first, sems.at[0])
    d_mixed = dot_t(d_z, matrix(w_first, 3)).astype(BF)
    for b in range(blocks):
        deal_matrix(t_dot(act_two[...], d_upped[b]), ups_o, me, b)
    blend = mixed[...]
    groups = list(zip(*(pairs_of(heads[c]) for c in range(3))))
    found = attend_back(
        groups, pairs_of(blend), [chances[p].astype(BF) for p in range(len(groups))], pairs_of(d_mixed))
    deal_matrix(t_dot(blend, d_z), firsts_o, me, 3)
    d_heads = [jnp.concatenate(one, axis=1) for one in found]
    d_act = jnp.zeros(rows.shape, F32)
    for c in range(3):
        d_act = d_act + dot_t(d_heads[c], matrix(w_first, c))
    for c in range(3):
        deal_matrix(t_dot(act_one[...], d_heads[c]), firsts_o, me, c)
    inverse = inverse_of(held)
    d_rows, g_one = norm_back(d_act, held * inverse, inverse, gains[0:1])
    d_picked_o[...] = d_rows + d_middle + d_logit * router[...]
    deal_lines([g_one, g_two], ups_o, small_o)


def dense_kernel(slot_count, place, *refs):
    shards = refs[:slot_count]
    (tokens, cotangent, delta, spots, segments, gains,
     result_o, back_o, picked_o, gain_o,
     act_one_o, d_heads_o, mixed_o, d_z_o, act_two_o, hidden_o, d_upped_o,
     w_first, w_up, w_down, rows, z, heads, chances, bias, fed, d_act, upped, d_hidden, d_mixed,
     act_one, d_heads, mixed, d_z, act_two, hidden, d_upped, sems, out_sems) = refs[slot_count:]
    holds = (w_first, w_up, w_down)
    fetch_start(shards, holds, sems, place[0], (0,))
    batch, length, _ = bias.shape
    width = tokens.shape[1]
    pairs = width // LANES
    blocks = hidden.shape[1] // width
    parts = [slice(s * length, (s + 1) * length) for s in range(batch)]
    copies = [
        pltpu.make_async_copy(held, out, out_sems.at[i])
        for i, (held, out) in enumerate((
            (act_one, act_one_o), (d_heads, d_heads_o), (mixed, mixed_o), (d_z, d_z_o),
            (act_two, act_two_o), (hidden, hidden_o), (d_upped, d_upped_o),
        ))
    ]

    hot = hot_rows(spots[...], tokens.shape[0])
    for s, part in enumerate(parts):
        held = tokens[part].astype(F32) + dot(hot[part], delta[...])
        rows[part] = held
        act_one[part] = (held * inverse_of(held) * gains[0:1]).astype(BF)
        member = hot_rows(segments[:, part], CODES)
        bias[s] = bias_of(t_dot(member, member))
    copies[0].start()
    ready(w_first, sems.at[0])
    for c in range(3):
        for part in parts:
            heads[c, part] = dot(act_one[part], matrix(w_first, c)).astype(BF)
    fetch_start(shards, holds, sems, place[0], (1, 2))

    def forward(p, carry):
        lanes = lanes_of(p)
        groups = [tuple(heads[c, part, lanes] for c in range(3)) for part in parts]
        blends, found = attend(groups, [bias[s] for s in range(batch)])
        for s, part in enumerate(parts):
            mixed[part, lanes] = blends[s]
            chances[s, p] = found[s]
        return carry

    lax.fori_loop(0, pairs, forward, 0)
    copies[2].start()
    for part in parts:
        attended = dot(mixed[part], matrix(w_first, 3))
        z[part] = attended
        middle = rows[part] + attended
        act_two[part] = (middle * inverse_of(middle) * gains[1:2]).astype(BF)
    copies[4].start()
    ready(w_up, sems.at[1])
    ready(w_down, sems.at[2])
    fed[...] = jnp.zeros(fed.shape, F32)
    d_act[...] = jnp.zeros(d_act.shape, F32)

    for b in range(blocks):
        lanes = slice(b * width, (b + 1) * width)
        for s, part in enumerate(parts):
            upped[...] = dot(act_two[part], matrix(w_up, b))
            d_hidden[...] = dot_t(cotangent[part], band(w_down, b))

            for r in range(length // STRIP):
                spot = slice(r * STRIP, (r + 1) * STRIP)
                there = slice(s * length + r * STRIP, s * length + (r + 1) * STRIP)
                for side in range(2):
                    cut = slice(side * width // 2, (side + 1) * width // 2)
                    out = slice(b * width + side * width // 2, b * width + (side + 1) * width // 2)
                    value = upped[spot, cut]
                    whole, dense = normal_parts(value)
                    hidden[there, out] = (value * whole).astype(BF)
                    d_upped[there, out] = (d_hidden[spot, cut] * (whole + dense)).astype(BF)
            fed[part] += dot(hidden[part, lanes], band(w_down, b))
            d_act[part] += dot_t(d_upped[part, lanes], matrix(w_up, b))
    copies[5].start()
    copies[6].start()
    gain = jnp.zeros((1, width), F32)
    for part in parts:
        result_o[part] = (rows[part] + z[part] + fed[part]).astype(BF)
        middle = rows[part] + z[part]
        inverse = inverse_of(middle)
        d_middle, more = norm_back(d_act[part], middle * inverse, inverse, gains[1:2])
        gain = gain + more
        held = cotangent[part].astype(F32) + d_middle
        d_act[part] = held
        d_z[part] = held.astype(BF)
        d_mixed[part] = dot_t(held.astype(BF), matrix(w_first, 3)).astype(BF)
    gain_o[1:2] = gain
    copies[3].start()

    def backward(p, carry):
        lanes = lanes_of(p)
        groups = [tuple(heads[c, part, lanes] for c in range(3)) for part in parts]
        found = attend_back(
            groups, [mixed[part, lanes] for part in parts], [chances[s, p] for s in range(batch)],
            [d_mixed[part, lanes] for part in parts])
        for c in range(3):
            for s, part in enumerate(parts):
                d_heads[c, part, lanes] = found[c][s]
        return carry

    lax.fori_loop(0, pairs, backward, 0)
    copies[1].start()
    gain = jnp.zeros((1, width), F32)
    for s, part in enumerate(parts):
        d_first = dot_t(d_heads[0, part], matrix(w_first, 0))
        d_first = d_first + dot_t(d_heads[1, part], matrix(w_first, 1))
        d_first = d_first + dot_t(d_heads[2, part], matrix(w_first, 2))
        held = rows[part]
        inverse = inverse_of(held)
        d_rows, more = norm_back(d_first, held * inverse, inverse, gains[0:1])
        gain = gain + more
        back_o[part] = (d_act[part] + d_rows).astype(BF)
    picked_o[...] = t_dot(hot, back_o[...]).astype(BF)
    gain_o[0:1] = gain
    for copy in copies:
        copy.wait()


def dense_back_kernel(out_count, place, hidden, d_out, act_two, d_upped, mixed, d_z, act_one, d_heads, gains, *refs):
    downs_o, ups_o, firsts_o = (refs[i * out_count:(i + 1) * out_count] for i in range(3))
    router_o, small_o, d_picked_o = refs[3 * out_count:]
    me = place[0]
    deal_down(hidden, d_out[...], downs_o, me)
    deal_router(jnp.zeros((1, d_out.shape[1]), F32), downs_o, router_o, me)
    d_picked_o[...] = jnp.zeros(d_picked_o.shape, F32)
    width = act_two.shape[1]
    for b in range(d_upped.shape[1] // width):
        deal_matrix(t_dot(act_two[...], d_upped[:, b * width:(b + 1) * width]), ups_o, me, b)
    deal_matrix(t_dot(mixed[...], d_z[...]), firsts_o, me, 3)
    for c in range(3):
        deal_matrix(t_dot(act_one[...], d_heads[c]), firsts_o, me, c)
    deal_lines([gains[0:1], gains[1:2]], ups_o, small_o)


def call(kernel, inputs, anywhere, outs, scratch, flops, mib, anywhere_outs=0):
    vmem = pl.BlockSpec(memory_space=pltpu.VMEM)
    hbm = pl.BlockSpec(memory_space=pltpu.HBM)
    specs = [pl.BlockSpec(memory_space=pltpu.SMEM)] + [hbm] * anywhere
    specs = specs + [vmem] * (len(inputs) - len(specs))
    moved = sum(v.size * v.dtype.itemsize for v in inputs) + sum(
        o.size * jnp.dtype(o.dtype).itemsize for o in outs)
    return tuple(pl.pallas_call(
        kernel,
        out_shape=outs,
        in_specs=specs,
        out_specs=[vmem] * (len(outs) - anywhere_outs) + [hbm] * anywhere_outs,
        scratch_shapes=scratch,
        compiler_params=pltpu.CompilerParams(vmem_limit_bytes=mib * MIB),
        cost_estimate=pl.CostEstimate(flops=flops, bytes_accessed=moved, transcendentals=0),
    )(*inputs))


def body(
    tokens, cotangent, segments, chosen, router, norm_gains, attn_in, attn_out, ff_up, ff_down
):
    n = lax.axis_size("dp")
    routed = lax.axis_index("section") == 0
    place = lax.axis_index("dp").astype(jnp.int32).reshape(1)
    batch, length = segments.shape
    width = tokens.shape[1]
    kept = chosen.shape[1]
    rows_in, rows_down, ff = attn_in.shape[2], ff_down.shape[1], ff_up.shape[2]
    blocks, pairs = ff // width, width // LANES
    picked, count = batch * kept, batch * length
    gains = norm_gains[0]
    router_row = router[None]

    def shape(*dims, dtype=F32):
        return jax.ShapeDtypeStruct(dims, dtype)

    def hold(*dims, dtype=F32):
        return pltpu.VMEM(dims, dtype)

    first_part = jnp.concatenate([attn_in[0].reshape(-1, width), attn_out[0]])
    up_part = jnp.concatenate([ff_up[0][:, b * width:(b + 1) * width] for b in range(blocks)])
    parts = [first_part, up_part, ff_down[0]]
    part_rows = 4 * width // SHARDS
    order = lax.iota(jnp.int32, batch)[:, None]
    spots = (chosen + order * length).reshape(1, picked)
    lines = segments.reshape(1, count)
    codes = (segments + order * CODES).reshape(1, count)
    if sliced(n):
        half = part_rows // 2
        halves = [jnp.concatenate([first_part, up_part[:half]]), jnp.concatenate([up_part[half:], ff_down[0]])]
        shards = gather_halves(halves, n, (spots, lines, codes))
        outs, wide_outs = (
            [shape(n // 2, part_rows + more, width, dtype=BF)] * 2 for more in (0, EXTRA))
    else:
        first, up, down = (lax.all_gather(part, "dp", axis=0) for part in parts)

        def dealt(value):
            value = value.reshape(n, 4, rows_in, width).transpose(1, 0, 2, 3)
            value = value.reshape(4, SHARDS, width // SHARDS, width).transpose(1, 0, 2, 3)
            return value.reshape(SHARDS, part_rows, width)

        shards = [dealt(first), dealt(up), down.reshape(SHARDS, part_rows, width)]
        outs = wide_outs = [shape(SHARDS, part_rows, width, dtype=BF)]
    number, out_number = len(shards), len(outs)
    w_first = w_up = w_down = hold(SHARDS, part_rows, width, dtype=BF)

    (rows, gate, z, act_one, heads, chances, mixed, act_two, hidden, slope, branch, delta) = call(
        functools.partial(routed_kernel, number, batch),
        [place, *shards, tokens, spots, codes, router_row, gains],
        number,
        [shape(picked, width), shape(picked, 1), shape(picked, width), shape(picked, width, dtype=BF),
         shape(3, picked, width, dtype=BF), shape(pairs, 2 * picked, picked),
         shape(picked, width, dtype=BF), shape(picked, width, dtype=BF), shape(picked, ff, dtype=BF),
         shape(picked, ff), shape(picked, width), shape(picked, width, dtype=BF)],
        [w_first, w_up, w_down, pltpu.SemaphoreType.DMA((3,))],
        4 * picked * width * (2 * width + ff),
        28,
    )
    arrived = lax.ppermute(delta, "section", [(0, 1)])

    (result, back, back_rows, dense_gains, *dense_kept) = call(
        functools.partial(dense_kernel, number),
        [place, *shards, tokens, cotangent, arrived, spots, lines, gains],
        number,
        [shape(count, width, dtype=BF), shape(count, width, dtype=BF), shape(picked, width, dtype=BF),
         shape(2, width),
         shape(count, width, dtype=BF), shape(3, count, width, dtype=BF), shape(count, width, dtype=BF),
         shape(count, width, dtype=BF), shape(count, width, dtype=BF), shape(count, ff, dtype=BF),
         shape(count, ff, dtype=BF)],
        [w_first, w_up, w_down, hold(count, width), hold(count, width), hold(3, count, width, dtype=BF),
         hold(batch, pairs, 2 * length, length, dtype=BF), hold(batch, length, length),
         hold(count, width), hold(count, width), hold(length, width), hold(length, width),
         hold(count, width, dtype=BF),
         hold(count, width, dtype=BF), hold(3, count, width, dtype=BF), hold(count, width, dtype=BF),
         hold(count, width, dtype=BF), hold(count, width, dtype=BF), hold(count, ff, dtype=BF),
         hold(count, ff, dtype=BF),
         pltpu.SemaphoreType.DMA((3,)), pltpu.SemaphoreType.DMA((7,))],
        4 * count * width * (4 * width + 2 * ff),
        DENSE_MIB,
        anywhere_outs=7,
    )
    dense_act_one, dense_d_heads, dense_mixed, dense_d_z, dense_act_two, dense_hidden, dense_d_upped = dense_kept
    d_delta = lax.ppermute(back_rows, "section", [(1, 0)])
    returned = lax.ppermute(after(back, d_delta), "section", [(1, 0)])

    back_outs = [
        *wide_outs, *wide_outs, *outs, shape(EXTRA, width), shape(EXTRA, width), shape(picked, width)]

    def routed_back():
        return call(
            functools.partial(routed_back_kernel, number, out_number),
            [place, *shards, d_delta, gate, branch, rows, z, hidden, act_two, slope, act_one, heads, chances,
             mixed, router_row, gains],
            number,
            back_outs,
            [w_first, w_up, w_down, pltpu.SemaphoreType.DMA((3,))],
            8 * picked * width * ff + 16 * picked * width * width,
            44,
        )

    def dense_back():
        return call(
            functools.partial(dense_back_kernel, out_number),
            [place, dense_hidden, cotangent, dense_act_two, dense_d_upped, dense_mixed, dense_d_z, dense_act_one,
             dense_d_heads, dense_gains],
            0, back_outs, [], 4 * count * width * ff + 8 * count * width * width, 44,
        )

    (*pieces, router_lines, small, d_picked) = lax.cond(routed, routed_back, dense_back)
    up_pieces, first_pieces = pieces[:out_number], pieces[out_number:]
    picks = (chosen[:, :, None] == lax.iota(jnp.int32, length)[None, None, :]).astype(F32)

    def both_ends(returned, result):
        spread = jnp.einsum(
            "wgo,wgq->woq", picks, d_picked.reshape(batch, kept, width), precision=lax.Precision.HIGHEST)
        first_rows = (returned.astype(F32) + spread.reshape(count, width)).astype(BF)
        return jnp.where(routed, first_rows, result)[None]

    if sliced(n):
        pieces, returned = lax.optimization_barrier((pieces, returned))
        spot = spot_of(place[0], n // 4)
        down_sum, up_sum, first_sum = sums = [
            Sum(*pieces[i:i + 2], n, far, spot, i == 0) for i, far in zip((0, 2, 4), (FAR[2], FAR[1], FAR[0]))]
        for s in range(n // 4):
            for one in sums:
                one.step(s)
        arrived = [down_sum.arrived[d] for d in sorted(down_sum.arrived)]
        router_grad = call(
            functools.partial(router_kernel, len(arrived)),
            [place, down_sum.own, down_sum.soon, *arrived], len(arrived) + 2, [shape(1, width)],
            [hold(n // 2 + 2, EXTRA, width, dtype=BF), pltpu.SemaphoreType.DMA((n // 2 + 2,))], width, 2,
        )[0][0]
        router_grad = router_grad + lax.ppermute(router_grad, "section", [(0, 1), (1, 0)])
        ends = both_ends(returned, result)
        down_grad, up_grad = (sum(one.total())[:part_rows] for one in (down_sum, up_sum))
        small = sum(up_sum.total())[part_rows:]
        due, last = first_sum.total((router_grad, ends, down_grad, up_grad))
        in_grad, out_grad = (due[rows] + last[rows] for rows in (slice(0, 3 * rows_in), slice(3 * rows_in, None)))
    else:
        def plain(pieces, wide):
            whole = pieces[0]
            if wide:
                whole = whole.reshape(SHARDS, 4, -1, width).transpose(1, 0, 2, 3)
                whole = whole.reshape(4, n, -1, width).transpose(1, 0, 2, 3)
            return scatter_plain(whole.reshape(n, -1, width))

        down_grad = plain(pieces[:1], False)
        up_grad, first_grad = plain(pieces[1:2], True), plain(pieces[2:], True)
        in_grad, out_grad = first_grad[:3 * rows_in], first_grad[3 * rows_in:]
        small = lax.psum(small, "dp")
        ends = both_ends(returned, result)
        router_grad = jnp.sum(lax.psum(router_lines, ("section", "dp")), axis=0)
    up_grad = up_grad.reshape(blocks, rows_in, width).transpose(1, 0, 2).reshape(rows_in, ff)
    gain_grad = lax.dynamic_slice_in_dim(small[:2], place[0] * (width // n), width // n, 1)
    return (
        ends, router_grad, gain_grad[None], in_grad.reshape(1, 3, rows_in, width), out_grad[None],
        up_grad[None], down_grad[None],
    )


def solution(mesh):
    return jax.shard_map(
        body,
        mesh=mesh,
        in_specs=(
            P("dp", None),
            P("dp", None),
            P("dp", None),
            P("dp", None),
            P(),
            P("section", None, None),
            P("section", None, "dp", None),
            P("section", "dp", None),
            P("section", "dp", None),
            P("section", "dp", None),
        ),
        out_specs=(
            P("section", "dp", None),
            P(),
            P("section", None, "dp"),
            P("section", None, "dp", None),
            P("section", "dp", None),
            P("section", "dp", None),
            P("section", "dp", None),
        ),
        check_vma=False,
    )
```

```python
import functools

import jax
import jax.numpy as jnp
from jax import lax
from jax.experimental import pallas as pl
from jax.experimental.pallas import tpu as pltpu
from jax.sharding import PartitionSpec as P

HEAD_DIM = 64
LANES = 2 * HEAD_DIM
EPSILON = 1e-05
MASKED = -1e30
BF = jnp.bfloat16
F32 = jnp.float32
MIB = 1024 * 1024
DENSE_MIB = 60
STRIP = 16
CODES = 16
SHARDS = 16


def move(value, pairs):
    return lax.ppermute(value, "dp", pairs)


def device_at(spot, core, depth):
    return 4 * spot + core if spot < depth else 4 * (2 * depth - 1 - spot) + 2 + core


def routes(n):
    depth = n // 4
    ring = 2 * depth

    def turned(by):
        return [
            (device_at(r, c, depth), device_at((r + by) % ring, c, depth))
            for r in range(ring) for c in range(2)
        ]

    return turned(1), turned(-1), [(i, i ^ 1) for i in range(n)]


def hops(depth, far):
    return (depth, depth - 1) if far == 0 else (depth - 1, depth)


def after(value, token):
    return lax.optimization_barrier((value, token))[0]


def sliced(n):
    return n == 16


FAR = (0, 1, 0)


def first_ways(depth, far):
    return (depth, 1 - depth) if far == 0 else (-depth, depth - 1)


def lots(depth, far):
    ahead, behind = hops(depth, far)
    early = [0] + [sign * d for d in range(1, depth // 2 + 1) for sign in (1, -1)]
    late = [d for d in range(-behind, ahead + 1) if d not in early]
    return early, late


def gather_halves(halves, n, token):
    depth = n // 4
    forward, backward, beside = routes(n)
    held = [{0: half} for half in halves]
    for s in range(1, depth + 1):
        for far, mine in enumerate(held):
            ahead, behind = hops(depth, far)
            for sign, limit, way in ((1, ahead, forward), (-1, behind, backward)):
                if s <= limit:
                    source = mine[sign * (s - 1)]
                    mine[sign * s] = move(after(source, token) if s == 2 else source, way)
    found = []
    for far, mine in enumerate(held):
        early, late = lots(depth, far)
        found += [mine[d] for d in early + late]
        found += [move(jnp.stack([mine[d] for d in some]), beside) for some in (early, late)]
    return found


EXTRA = 16


class Sum:
    def __init__(self, own, other, n, far, spot, soon):
        self.depth = n // 4
        forward, backward, beside = routes(n)
        self.ways = (forward, backward) if far == 0 else (backward, forward)
        self.far, self.spot = far, spot
        self.own, self.soon = own, soon
        self.got = move(other, beside)
        self.came = [None, None]
        self.arrived = {}

    def block(self, held, distance):
        at = lax.rem(self.spot + (2 * self.depth + distance), 2 * self.depth)
        return lax.dynamic_index_in_dim(held, at, 0, keepdims=False)

    def term(self, distance, came, got=None):
        found = self.block(self.own, distance).astype(F32)
        found = found + (self.block(self.got, distance) if got is None else got).astype(F32)
        for value in came:
            if value is not None:
                found = found + value.astype(F32)
        return found

    def step(self, s):
        signs = [1 if self.far == i else -1 for i in range(2) if s + i < self.depth]
        values = [
            self.term(sign * (self.depth - s - i), [self.came[i]], self.soon[i] if s == 0 and self.soon is not None else None)
            for i, sign in enumerate(signs)]
        values = lax.optimization_barrier([value.astype(BF) for value in values])
        for i, (sign, value) in enumerate(zip(signs, values)):
            self.came[i] = self.arrived[-sign * (s + 1)] = move(value, self.ways[i])

    def total(self, token=None):
        last = self.came[0] if token is None else after(self.came[0], token)
        return lax.optimization_barrier(self.term(0, [self.came[1]])), last.astype(F32)


def scatter_plain(whole):
    return lax.psum_scatter(whole.astype(F32), "dp", scatter_dimension=0, tiled=False)


def dot(a, b):
    return jnp.dot(a, b, preferred_element_type=F32)


def dot_t(a, b):
    return lax.dot_general(a, b, (((1,), (1,)), ((), ())), preferred_element_type=F32)


def t_dot(a, b):
    return lax.dot_general(a, b, (((0,), (0,)), ((), ())), preferred_element_type=F32)


def spot_of(me, depth):
    return jnp.where((me // 2) % 2 == 0, me // 4, 2 * depth - 1 - me // 4)


def device_on(me, distance, core, depth):
    spot = lax.rem(spot_of(me, depth) + (2 * depth + distance), 2 * depth)
    base = jnp.where(spot < depth, 4 * spot, 4 * (2 * depth - 1 - spot) + 2)
    return base + ((me % 2) ^ core)


def fetch_start(refs, holds, sems, me, names):
    if len(refs) == 3:
        for i in names:
            pltpu.make_async_copy(refs[i], holds[i], sems.at[i]).start()
        return
    count = len(refs) // 2
    depth = (count - 2) // 2
    rows = holds[0].shape[1]
    cuts = ((0, 0, 0, 0, rows), (0, 1, rows, 0, rows // 2), (1, 1, 0, rows // 2, rows // 2), (1, 2, rows // 2, 0, rows))
    for i in names:
        for far, name, source, target, size in cuts:
            if name == i:
                mine = refs[far * count:(far + 1) * count]
                early, late = lots(depth, far)
                there = pl.ds(source, size)
                pieces = [(d, 0, ref.at[there]) for d, ref in zip(early + late, mine)]
                pieces += [(d, 1, mine[-2].at[k, there]) for k, d in enumerate(early)]
                pieces += [(d, 1, mine[-1].at[k, there]) for k, d in enumerate(late)]
                for distance, core, piece in pieces:
                    origin = device_on(me, -distance, core, depth)
                    pltpu.make_async_copy(piece, holds[i].at[origin, pl.ds(target, size)], sems.at[i]).start()


def ready(hold, sem):
    pltpu.make_async_copy(hold, hold, sem).wait()


def matrix(hold, q):
    shards, _, width = hold.shape
    count = width // shards
    return hold[:, q * count:(q + 1) * count, :].reshape(width, width)


def band(hold, b):
    shards, count, width = hold.shape
    some = width // count
    return hold[b * some:(b + 1) * some].reshape(width, width)


def deal(value, outs, me, first, piece):
    rows = piece.stop - piece.start
    number = value.shape[0] // rows
    if len(outs) == 1:
        outs[0][first:first + number, piece, :] = value.reshape(number, rows, value.shape[1]).astype(BF)
        return
    own, other = outs
    ring = own.shape[0]
    for t in range(number // 2):
        even, odd = value[2 * t * rows:(2 * t + 1) * rows], value[(2 * t + 1) * rows:(2 * t + 2) * rows]
        z, x = divmod(first // 2 + t, 2)
        spot = z if x == 0 else ring - 1 - z
        own[spot, piece, :] = jnp.where(me % 2 == 0, even, odd).astype(BF)
        other[spot, piece, :] = jnp.where(me % 2 == 0, odd, even).astype(BF)


def split(line):
    high = line.astype(BF).astype(F32)
    middle = (line - high).astype(BF).astype(F32)
    return [high, middle, line - high - middle]


def deal_lines(lines, outs, small):
    value = jnp.concatenate(lines + [jnp.zeros((EXTRA - len(lines), lines[0].shape[1]), F32)], axis=0)
    small[...] = value
    if len(outs) == 2:
        for out in outs:
            for spot in range(out.shape[0]):
                out[spot, out.shape[1] - EXTRA:, :] = value.astype(BF)


def deal_router(line, outs, small, me):
    three = split(line)
    none = jnp.zeros_like(line)
    mine, other = three + [none] * (EXTRA - 3), [none] * 3 + three + [none] * (EXTRA - 6)
    small[...] = jnp.concatenate(mine, axis=0)
    if len(outs) == 2:
        ring, row = outs[0].shape[0], outs[0].shape[1] - EXTRA
        for out, value in zip(outs, (mine, other)):
            value = jnp.concatenate(value, axis=0).astype(BF)
            for spot in range(ring):
                out[spot, row:, :] = jnp.zeros(value.shape, BF)
            for distance in first_ways(ring // 2, FAR[2]):
                out[lax.rem(spot_of(me, ring // 2) + ring + distance, ring), row:, :] = value


def router_kernel(count, place, *refs):
    own, got, arrived, (out, lines, sems) = refs[0], refs[1], refs[2:count + 2], refs[count + 2:]
    me = place[0]
    ring = count + 1
    depth = ring // 2
    spot = spot_of(me, depth)
    row = own.shape[1] - EXTRA
    away = lax.rem(spot + ring + first_ways(depth, FAR[2])[0], ring)
    copies = [pltpu.make_async_copy(own.at[away, pl.ds(row, EXTRA)], lines.at[0], sems.at[0]),
              pltpu.make_async_copy(got.at[0, pl.ds(row, EXTRA)], lines.at[1], sems.at[1])]
    ahead, behind = hops(depth, FAR[2])
    distances = list(range(-ahead, 0)) + list(range(1, behind + 1))
    for i, (distance, ref) in enumerate(zip(distances, arrived)):
        slot = 2 + lax.rem(spot + ring + distance, ring)
        copies.append(pltpu.make_async_copy(ref.at[pl.ds(row, EXTRA)], lines.at[slot], sems.at[2 + i]))
    for copy in copies:
        copy.start()
    for copy in copies:
        copy.wait()
    lines[2 + spot] = lines[0] + lines[1]
    total = jnp.zeros(out.shape, F32)
    for r in range(ring):
        value = lines[2 + r].astype(F32)
        low = (value[0:1] + value[1:2]) + value[2:3]
        high = (value[3:4] + value[4:5]) + value[5:6]
        total = total + jnp.where(me % 2 == 0, low, high)
        total = total + jnp.where(me % 2 == 0, high, low)
    out[...] = total


def copy_soon(outs, soon, me):
    if len(outs) == 2:
        ring = outs[1].shape[0]
        for i, distance in enumerate(first_ways(ring // 2, FAR[2])):
            soon[i] = outs[1][lax.rem(spot_of(me, ring // 2) + ring + distance, ring)]


def deal_matrix(value, outs, me, q):
    count = value.shape[0] // SHARDS
    deal(value, outs, me, 0, slice(q * count, (q + 1) * count))


def deal_down(hidden, d_out, outs, me):
    width = d_out.shape[1]
    count = hidden.shape[1] // SHARDS
    for b in range(hidden.shape[1] // width):
        value = t_dot(hidden[:, b * width:(b + 1) * width], d_out)
        deal(value, outs, me, b * (width // count), slice(0, count))


def inverse_of(rows):
    return lax.rsqrt(jnp.mean(rows * rows, axis=-1, keepdims=True) + EPSILON)


def norm_back(upstream, normed, inverse, gain):
    scaled = upstream * gain
    d_gain = jnp.sum(upstream * normed, axis=0, keepdims=True)
    d_rows = inverse * (scaled - normed * jnp.mean(scaled * normed, axis=-1, keepdims=True))
    return d_rows, d_gain


def normal_parts(value):
    whole = 0.5 + 0.5 * lax.erf(value * 0.7071067811865476)
    return whole, value * jnp.exp(value * value * -0.5) * 0.3989422804014327


def left_lanes(rows):
    return lax.broadcasted_iota(jnp.int32, (rows, LANES), 1) < HEAD_DIM


def two_heads(value):
    left = left_lanes(value.shape[0])
    zero = jnp.zeros_like(value)
    return jnp.concatenate([jnp.where(left, value, zero), jnp.where(left, zero, value)], axis=0)


def one_row(value):
    half = value.shape[0] // 2
    return jnp.where(left_lanes(half), value[:half], value[half:])


def bias_of(same):
    shape = same.shape
    order = lax.broadcasted_iota(jnp.int32, shape, 0) >= lax.broadcasted_iota(jnp.int32, shape, 1)
    return jnp.where(order & (same > 0.5), 0.0, MASKED).astype(F32)


def hot_rows(line, count):
    return (lax.broadcasted_iota(jnp.int32, (count, line.shape[1]), 0) == line).astype(BF)


def attend(groups, biases):
    size = groups[0][0].shape[0]
    scale = jnp.asarray(HEAD_DIM ** -0.5, BF)
    scores = [dot_t(two_heads(query) * scale, keyed) for query, keyed, _ in groups]
    found = []
    for value, bias in zip(scores, biases):
        value = (value.reshape(2, size, size) + bias[None]).reshape(2 * size, size)
        powers = jnp.exp(value - jnp.max(value, axis=-1, keepdims=True))
        found.append((powers * (1.0 / jnp.sum(powers, axis=-1, keepdims=True))).astype(BF))
    mixed = [one_row(dot(chances, valued)).astype(BF) for chances, (_, _, valued) in zip(found, groups)]
    return mixed, found


def attend_back(groups, mixed, chances, d_mixed):
    both = [two_heads(value) for value in d_mixed]
    d_chances = [dot_t(value, valued) for value, (_, _, valued) in zip(both, groups)]
    d_value = [t_dot(chance, value) for chance, value in zip(chances, both)]
    factor = HEAD_DIM ** -0.5
    d_scores = []
    for found, value, blend, chance in zip(d_chances, d_mixed, mixed, chances):
        overlap = jnp.sum(two_heads(value.astype(F32) * blend.astype(F32)), axis=-1, keepdims=True)
        d_scores.append((chance.astype(F32) * (found - overlap)).astype(BF))
    d_query = [one_row(dot(value, keyed)) * factor for value, (_, keyed, _) in zip(d_scores, groups)]
    d_key = [t_dot(value, two_heads(query)) * factor for value, (query, _, _) in zip(d_scores, groups)]
    return [[one.astype(BF) for one in some] for some in (d_query, d_key, d_value)]


def pairs_of(value):
    return [value[:, p:p + LANES] for p in range(0, value.shape[1], LANES)]


def lanes_of(p):
    return pl.ds(pl.multiple_of(p * LANES, LANES), LANES)


def routed_kernel(slot_count, batch, place, *refs):
    shards = refs[:slot_count]
    (tokens, spots, codes, router, gains,
     rows_o, gate_o, z_o, act_one_o, heads_o, chances_o, mixed_o, act_two_o, hidden_o, slope_o, branch_o, delta_o,
     w_first, w_up, w_down, sems) = refs[slot_count:]
    fetch_start(shards, (w_first, w_up, w_down), sems, place[0], (0, 1, 2))
    hot = hot_rows(spots[...], tokens.shape[0])
    rows = t_dot(hot, tokens[...])
    rows_o[...] = rows
    gate = jax.nn.sigmoid(jnp.sum(rows * router[...], axis=-1, keepdims=True))
    gate_o[...] = gate
    act = (rows * inverse_of(rows) * gains[0:1]).astype(BF)
    act_one_o[...] = act
    member = dot(hot_rows(codes[...], CODES * batch), hot).astype(BF)
    bias = bias_of(t_dot(member, member))
    ready(w_first, sems.at[0])
    heads = [dot(act, matrix(w_first, c)).astype(BF) for c in range(3)]
    for c in range(3):
        heads_o[c] = heads[c]
    groups = list(zip(*(pairs_of(value) for value in heads)))
    found, chances = attend(groups, [bias] * len(groups))
    for p, chance in enumerate(chances):
        chances_o[p] = chance.astype(F32)
    mixed = jnp.concatenate(found, axis=1)
    mixed_o[...] = mixed
    z = dot(mixed, matrix(w_first, 3))
    z_o[...] = z
    middle = rows + z
    act_two = (middle * inverse_of(middle) * gains[1:2]).astype(BF)
    act_two_o[...] = act_two
    ready(w_up, sems.at[1])
    ready(w_down, sems.at[2])
    width = rows.shape[1]
    for b in range(hidden_o.shape[1] // width):
        lanes = slice(b * width, (b + 1) * width)
        upped = dot(act_two, matrix(w_up, b))
        whole, dense = normal_parts(upped)
        hidden_o[:, lanes] = (upped * whole).astype(BF)
        slope_o[:, lanes] = whole + dense
    branch = z_o[...] + dot(hidden_o[...], w_down[...].reshape(hidden_o.shape[1], width))
    branch_o[...] = branch
    delta_o[...] = (gate * branch).astype(BF)


def routed_back_kernel(slot_count, out_count, place, *refs):
    shards = refs[:slot_count]
    (d_delta, gate, branch, rows, z, hidden, act_two, slope, act_one, heads, chances, mixed, router, gains) = refs[
        slot_count:slot_count + 14]
    refs = refs[slot_count + 14:]
    downs_o, ups_o, firsts_o = (refs[i * out_count:(i + 1) * out_count] for i in range(3))
    soon_o, router_o, small_o, d_picked_o, w_first, w_up, w_down, sems = refs[3 * out_count:]
    me = place[0]
    fetch_start(shards, (w_first, w_up, w_down), sems, me, (2, 1, 0))
    width = rows.shape[1]
    blocks = slope.shape[1] // width
    held = rows[...]
    gated = gate[...]
    upstream = d_delta[...].astype(F32)
    gradient = gated * upstream
    d_out = gradient.astype(BF)
    deal_down(hidden, d_out, downs_o, me)
    d_logit = jnp.sum(upstream * branch[...], axis=-1, keepdims=True) * gated * (1.0 - gated)
    deal_router(jnp.sum(d_logit * held, axis=0, keepdims=True), downs_o, router_o, me)
    copy_soon(downs_o, soon_o, me)
    ready(w_down, sems.at[2])
    d_upped = []
    for b in range(blocks):
        d_hidden = dot_t(d_out, band(w_down, b))
        d_upped.append((d_hidden * slope[:, b * width:(b + 1) * width]).astype(BF))
    ready(w_up, sems.at[1])
    d_act = jnp.zeros(rows.shape, F32)
    for b in range(blocks):
        d_act = d_act + dot_t(d_upped[b], matrix(w_up, b))
    middle = held + z[...]
    inverse = inverse_of(middle)
    d_middle, g_two = norm_back(d_act, middle * inverse, inverse, gains[1:2])
    d_z = (gradient + d_middle).astype(BF)
    ready(w_first, sems.at[0])
    d_mixed = dot_t(d_z, matrix(w_first, 3)).astype(BF)
    for b in range(blocks):
        deal_matrix(t_dot(act_two[...], d_upped[b]), ups_o, me, b)
    blend = mixed[...]
    groups = list(zip(*(pairs_of(heads[c]) for c in range(3))))
    found = attend_back(
        groups, pairs_of(blend), [chances[p].astype(BF) for p in range(len(groups))], pairs_of(d_mixed))
    deal_matrix(t_dot(blend, d_z), firsts_o, me, 3)
    d_heads = [jnp.concatenate(one, axis=1) for one in found]
    d_act = jnp.zeros(rows.shape, F32)
    for c in range(3):
        d_act = d_act + dot_t(d_heads[c], matrix(w_first, c))
    for c in range(3):
        deal_matrix(t_dot(act_one[...], d_heads[c]), firsts_o, me, c)
    inverse = inverse_of(held)
    d_rows, g_one = norm_back(d_act, held * inverse, inverse, gains[0:1])
    d_picked_o[...] = d_rows + d_middle + d_logit * router[...]
    deal_lines([g_one, g_two], ups_o, small_o)


def dense_kernel(slot_count, place, *refs):
    shards = refs[:slot_count]
    (tokens, cotangent, delta, spots, segments, gains,
     result_o, back_o, picked_o, gain_o,
     act_one_o, d_heads_o, mixed_o, d_z_o, act_two_o, hidden_o, d_upped_o,
     w_first, w_up, w_down, rows, z, heads, chances, bias, fed, d_act, upped, d_hidden, d_mixed,
     act_one, d_heads, mixed, d_z, act_two, hidden, d_upped, sems, out_sems) = refs[slot_count:]
    holds = (w_first, w_up, w_down)
    fetch_start(shards, holds, sems, place[0], (0,))
    batch, length, _ = bias.shape
    width = tokens.shape[1]
    pairs = width // LANES
    blocks = hidden.shape[1] // width
    parts = [slice(s * length, (s + 1) * length) for s in range(batch)]
    copies = [
        pltpu.make_async_copy(held, out, out_sems.at[i])
        for i, (held, out) in enumerate((
            (act_one, act_one_o), (d_heads, d_heads_o), (mixed, mixed_o), (d_z, d_z_o),
            (act_two, act_two_o), (hidden, hidden_o), (d_upped, d_upped_o),
        ))
    ]

    hot = hot_rows(spots[...], tokens.shape[0])
    for s, part in enumerate(parts):
        held = tokens[part].astype(F32) + dot(hot[part], delta[...])
        rows[part] = held
        act_one[part] = (held * inverse_of(held) * gains[0:1]).astype(BF)
        member = hot_rows(segments[:, part], CODES)
        bias[s] = bias_of(t_dot(member, member))
    copies[0].start()
    ready(w_first, sems.at[0])
    for c in range(3):
        for part in parts:
            heads[c, part] = dot(act_one[part], matrix(w_first, c)).astype(BF)
    fetch_start(shards, holds, sems, place[0], (1, 2))

    def forward(p, carry):
        lanes = lanes_of(p)
        groups = [tuple(heads[c, part, lanes] for c in range(3)) for part in parts]
        blends, found = attend(groups, [bias[s] for s in range(batch)])
        for s, part in enumerate(parts):
            mixed[part, lanes] = blends[s]
            chances[s, p] = found[s]
        return carry

    lax.fori_loop(0, pairs, forward, 0)
    copies[2].start()
    for part in parts:
        attended = dot(mixed[part], matrix(w_first, 3))
        z[part] = attended
        middle = rows[part] + attended
        act_two[part] = (middle * inverse_of(middle) * gains[1:2]).astype(BF)
    copies[4].start()
    ready(w_up, sems.at[1])
    ready(w_down, sems.at[2])
    fed[...] = jnp.zeros(fed.shape, F32)
    d_act[...] = jnp.zeros(d_act.shape, F32)

    for b in range(blocks):
        lanes = slice(b * width, (b + 1) * width)
        for s, part in enumerate(parts):
            upped[...] = dot(act_two[part], matrix(w_up, b))
            d_hidden[...] = dot_t(cotangent[part], band(w_down, b))

            for r in range(length // STRIP):
                spot = slice(r * STRIP, (r + 1) * STRIP)
                there = slice(s * length + r * STRIP, s * length + (r + 1) * STRIP)
                for side in range(2):
                    cut = slice(side * width // 2, (side + 1) * width // 2)
                    out = slice(b * width + side * width // 2, b * width + (side + 1) * width // 2)
                    value = upped[spot, cut]
                    whole, dense = normal_parts(value)
                    hidden[there, out] = (value * whole).astype(BF)
                    d_upped[there, out] = (d_hidden[spot, cut] * (whole + dense)).astype(BF)
            fed[part] += dot(hidden[part, lanes], band(w_down, b))
            d_act[part] += dot_t(d_upped[part, lanes], matrix(w_up, b))
    copies[5].start()
    copies[6].start()
    gain = jnp.zeros((1, width), F32)
    for part in parts:
        result_o[part] = (rows[part] + z[part] + fed[part]).astype(BF)
        middle = rows[part] + z[part]
        inverse = inverse_of(middle)
        d_middle, more = norm_back(d_act[part], middle * inverse, inverse, gains[1:2])
        gain = gain + more
        held = cotangent[part].astype(F32) + d_middle
        d_act[part] = held
        d_z[part] = held.astype(BF)
        d_mixed[part] = dot_t(held.astype(BF), matrix(w_first, 3)).astype(BF)
    gain_o[1:2] = gain
    copies[3].start()

    def backward(p, carry):
        lanes = lanes_of(p)
        groups = [tuple(heads[c, part, lanes] for c in range(3)) for part in parts]
        found = attend_back(
            groups, [mixed[part, lanes] for part in parts], [chances[s, p] for s in range(batch)],
            [d_mixed[part, lanes] for part in parts])
        for c in range(3):
            for s, part in enumerate(parts):
                d_heads[c, part, lanes] = found[c][s]
        return carry

    lax.fori_loop(0, pairs, backward, 0)
    copies[1].start()
    gain = jnp.zeros((1, width), F32)
    for s, part in enumerate(parts):
        d_first = dot_t(d_heads[0, part], matrix(w_first, 0))
        d_first = d_first + dot_t(d_heads[1, part], matrix(w_first, 1))
        d_first = d_first + dot_t(d_heads[2, part], matrix(w_first, 2))
        held = rows[part]
        inverse = inverse_of(held)
        d_rows, more = norm_back(d_first, held * inverse, inverse, gains[0:1])
        gain = gain + more
        back_o[part] = (d_act[part] + d_rows).astype(BF)
    picked_o[...] = t_dot(hot, back_o[...]).astype(BF)
    gain_o[0:1] = gain
    for copy in copies:
        copy.wait()


def dense_back_kernel(out_count, place, hidden, d_out, act_two, d_upped, mixed, d_z, act_one, d_heads, gains, *refs):
    downs_o, ups_o, firsts_o = (refs[i * out_count:(i + 1) * out_count] for i in range(3))
    soon_o, router_o, small_o, d_picked_o = refs[3 * out_count:]
    me = place[0]
    deal_down(hidden, d_out[...], downs_o, me)
    deal_router(jnp.zeros((1, d_out.shape[1]), F32), downs_o, router_o, me)
    copy_soon(downs_o, soon_o, me)
    d_picked_o[...] = jnp.zeros(d_picked_o.shape, F32)
    width = act_two.shape[1]
    for b in range(d_upped.shape[1] // width):
        deal_matrix(t_dot(act_two[...], d_upped[:, b * width:(b + 1) * width]), ups_o, me, b)
    deal_matrix(t_dot(mixed[...], d_z[...]), firsts_o, me, 3)
    for c in range(3):
        deal_matrix(t_dot(act_one[...], d_heads[c]), firsts_o, me, c)
    deal_lines([gains[0:1], gains[1:2]], ups_o, small_o)


def call(kernel, inputs, anywhere, outs, scratch, flops, mib, anywhere_outs=0):
    vmem = pl.BlockSpec(memory_space=pltpu.VMEM)
    hbm = pl.BlockSpec(memory_space=pltpu.HBM)
    specs = [pl.BlockSpec(memory_space=pltpu.SMEM)] + [hbm] * anywhere
    specs = specs + [vmem] * (len(inputs) - len(specs))
    moved = sum(v.size * v.dtype.itemsize for v in inputs) + sum(
        o.size * jnp.dtype(o.dtype).itemsize for o in outs)
    return tuple(pl.pallas_call(
        kernel,
        out_shape=outs,
        in_specs=specs,
        out_specs=[vmem] * (len(outs) - anywhere_outs) + [hbm] * anywhere_outs,
        scratch_shapes=scratch,
        compiler_params=pltpu.CompilerParams(vmem_limit_bytes=mib * MIB),
        cost_estimate=pl.CostEstimate(flops=flops, bytes_accessed=moved, transcendentals=0),
    )(*inputs))


def body(
    tokens, cotangent, segments, chosen, router, norm_gains, attn_in, attn_out, ff_up, ff_down
):
    n = lax.axis_size("dp")
    routed = lax.axis_index("section") == 0
    place = lax.axis_index("dp").astype(jnp.int32).reshape(1)
    batch, length = segments.shape
    width = tokens.shape[1]
    kept = chosen.shape[1]
    rows_in, rows_down, ff = attn_in.shape[2], ff_down.shape[1], ff_up.shape[2]
    blocks, pairs = ff // width, width // LANES
    picked, count = batch * kept, batch * length
    gains = norm_gains[0]
    router_row = router[None]

    def shape(*dims, dtype=F32):
        return jax.ShapeDtypeStruct(dims, dtype)

    def hold(*dims, dtype=F32):
        return pltpu.VMEM(dims, dtype)

    first_part = jnp.concatenate([attn_in[0].reshape(-1, width), attn_out[0]])
    up_part = jnp.concatenate([ff_up[0][:, b * width:(b + 1) * width] for b in range(blocks)])
    parts = [first_part, up_part, ff_down[0]]
    part_rows = 4 * width // SHARDS
    order = lax.iota(jnp.int32, batch)[:, None]
    spots = (chosen + order * length).reshape(1, picked)
    lines = segments.reshape(1, count)
    codes = (segments + order * CODES).reshape(1, count)
    if sliced(n):
        half = part_rows // 2
        halves = [jnp.concatenate([first_part, up_part[:half]]), jnp.concatenate([up_part[half:], ff_down[0]])]
        shards = gather_halves(halves, n, (spots, lines, codes))
        outs, wide_outs = (
            [shape(n // 2, part_rows + more, width, dtype=BF)] * 2 for more in (0, EXTRA))
    else:
        first, up, down = (lax.all_gather(part, "dp", axis=0) for part in parts)

        def dealt(value):
            value = value.reshape(n, 4, rows_in, width).transpose(1, 0, 2, 3)
            value = value.reshape(4, SHARDS, width // SHARDS, width).transpose(1, 0, 2, 3)
            return value.reshape(SHARDS, part_rows, width)

        shards = [dealt(first), dealt(up), down.reshape(SHARDS, part_rows, width)]
        outs = wide_outs = [shape(SHARDS, part_rows, width, dtype=BF)]
    number, out_number = len(shards), len(outs)
    w_first = w_up = w_down = hold(SHARDS, part_rows, width, dtype=BF)

    (rows, gate, z, act_one, heads, chances, mixed, act_two, hidden, slope, branch, delta) = call(
        functools.partial(routed_kernel, number, batch),
        [place, *shards, tokens, spots, codes, router_row, gains],
        number,
        [shape(picked, width), shape(picked, 1), shape(picked, width), shape(picked, width, dtype=BF),
         shape(3, picked, width, dtype=BF), shape(pairs, 2 * picked, picked),
         shape(picked, width, dtype=BF), shape(picked, width, dtype=BF), shape(picked, ff, dtype=BF),
         shape(picked, ff), shape(picked, width), shape(picked, width, dtype=BF)],
        [w_first, w_up, w_down, pltpu.SemaphoreType.DMA((3,))],
        4 * picked * width * (2 * width + ff),
        28,
    )
    arrived = lax.ppermute(delta, "section", [(0, 1)])

    (result, back, back_rows, dense_gains, *dense_kept) = call(
        functools.partial(dense_kernel, number),
        [place, *shards, tokens, cotangent, arrived, spots, lines, gains],
        number,
        [shape(count, width, dtype=BF), shape(count, width, dtype=BF), shape(picked, width, dtype=BF),
         shape(2, width),
         shape(count, width, dtype=BF), shape(3, count, width, dtype=BF), shape(count, width, dtype=BF),
         shape(count, width, dtype=BF), shape(count, width, dtype=BF), shape(count, ff, dtype=BF),
         shape(count, ff, dtype=BF)],
        [w_first, w_up, w_down, hold(count, width), hold(count, width), hold(3, count, width, dtype=BF),
         hold(batch, pairs, 2 * length, length, dtype=BF), hold(batch, length, length),
         hold(count, width), hold(count, width), hold(length, width), hold(length, width),
         hold(count, width, dtype=BF),
         hold(count, width, dtype=BF), hold(3, count, width, dtype=BF), hold(count, width, dtype=BF),
         hold(count, width, dtype=BF), hold(count, width, dtype=BF), hold(count, ff, dtype=BF),
         hold(count, ff, dtype=BF),
         pltpu.SemaphoreType.DMA((3,)), pltpu.SemaphoreType.DMA((7,))],
        4 * count * width * (4 * width + 2 * ff),
        DENSE_MIB,
        anywhere_outs=7,
    )
    dense_act_one, dense_d_heads, dense_mixed, dense_d_z, dense_act_two, dense_hidden, dense_d_upped = dense_kept
    d_delta = lax.ppermute(back_rows, "section", [(1, 0)])
    returned = lax.ppermute(after(back, d_delta), "section", [(1, 0)])

    back_outs = [
        *wide_outs, *wide_outs, *outs, shape(2, part_rows + EXTRA, width, dtype=BF), shape(EXTRA, width),
        shape(EXTRA, width), shape(picked, width)]

    def routed_back():
        return call(
            functools.partial(routed_back_kernel, number, out_number),
            [place, *shards, d_delta, gate, branch, rows, z, hidden, act_two, slope, act_one, heads, chances,
             mixed, router_row, gains],
            number,
            back_outs,
            [w_first, w_up, w_down, pltpu.SemaphoreType.DMA((3,))],
            8 * picked * width * ff + 16 * picked * width * width,
            44,
        )

    def dense_back():
        return call(
            functools.partial(dense_back_kernel, out_number),
            [place, dense_hidden, cotangent, dense_act_two, dense_d_upped, dense_mixed, dense_d_z, dense_act_one,
             dense_d_heads, dense_gains],
            0, back_outs, [], 4 * count * width * ff + 8 * count * width * width, 44,
        )

    (*pieces, router_lines, small, d_picked) = lax.cond(routed, routed_back, dense_back)
    up_pieces, first_pieces = pieces[:out_number], pieces[out_number:]
    picks = (chosen[:, :, None] == lax.iota(jnp.int32, length)[None, None, :]).astype(F32)

    def both_ends(returned, result):
        spread = jnp.einsum(
            "wgo,wgq->woq", picks, d_picked.reshape(batch, kept, width), precision=lax.Precision.HIGHEST)
        first_rows = (returned.astype(F32) + spread.reshape(count, width)).astype(BF)
        return jnp.where(routed, first_rows, result)[None]

    if sliced(n):
        pieces, returned = lax.optimization_barrier((pieces, returned))
        spot = spot_of(place[0], n // 4)
        soon = move(pieces[6], routes(n)[2])
        pieces = after(pieces[:6], soon)
        down_sum, up_sum, first_sum = sums = [
            Sum(*pieces[i:i + 2], n, far, spot, early) for i, far, early in (
                (0, FAR[2], soon), (2, FAR[1], None), (4, FAR[0], None))]
        for s in range(n // 4):
            for one in sums:
                one.step(s)
            if s == 0:
                d_picked = after(d_picked, first_sum.came[0])
        arrived = [down_sum.arrived[d] for d in sorted(down_sum.arrived)]
        router_grad = call(
            functools.partial(router_kernel, len(arrived)),
            [place, down_sum.own, down_sum.soon, *arrived], len(arrived) + 2, [shape(1, width)],
            [hold(n // 2 + 2, EXTRA, width, dtype=BF), pltpu.SemaphoreType.DMA((n // 2 + 2,))], width, 2,
        )[0][0]
        router_grad = router_grad + lax.ppermute(router_grad, "section", [(0, 1), (1, 0)])
        ends = both_ends(returned, result)
        down_grad, up_grad = (sum(one.total())[:part_rows] for one in (down_sum, up_sum))
        small = sum(up_sum.total())[part_rows:]
        due, last = first_sum.total((router_grad, ends, down_grad, up_grad))
        in_grad, out_grad = (due[rows] + last[rows] for rows in (slice(0, 3 * rows_in), slice(3 * rows_in, None)))
    else:
        def plain(pieces, wide):
            whole = pieces[0]
            if wide:
                whole = whole.reshape(SHARDS, 4, -1, width).transpose(1, 0, 2, 3)
                whole = whole.reshape(4, n, -1, width).transpose(1, 0, 2, 3)
            return scatter_plain(whole.reshape(n, -1, width))

        down_grad = plain(pieces[:1], False)
        up_grad, first_grad = plain(pieces[1:2], True), plain(pieces[2:3], True)
        in_grad, out_grad = first_grad[:3 * rows_in], first_grad[3 * rows_in:]
        small = lax.psum(small, "dp")
        ends = both_ends(returned, result)
        router_grad = jnp.sum(lax.psum(router_lines, ("section", "dp")), axis=0)
    up_grad = up_grad.reshape(blocks, rows_in, width).transpose(1, 0, 2).reshape(rows_in, ff)
    gain_grad = lax.dynamic_slice_in_dim(small[:2], place[0] * (width // n), width // n, 1)
    return (
        ends, router_grad, gain_grad[None], in_grad.reshape(1, 3, rows_in, width), out_grad[None],
        up_grad[None], down_grad[None],
    )


def solution(mesh):
    return jax.shard_map(
        body,
        mesh=mesh,
        in_specs=(
            P("dp", None),
            P("dp", None),
            P("dp", None),
            P("dp", None),
            P(),
            P("section", None, None),
            P("section", None, "dp", None),
            P("section", "dp", None),
            P("section", "dp", None),
            P("section", "dp", None),
        ),
        out_specs=(
            P("section", "dp", None),
            P(),
            P("section", None, "dp"),
            P("section", None, "dp", None),
            P("section", "dp", None),
            P("section", "dp", None),
            P("section", "dp", None),
        ),
        check_vma=False,
    )
```

```python
import functools

import jax
import jax.numpy as jnp
from jax import lax
from jax.experimental import pallas as pl
from jax.experimental.pallas import tpu as pltpu
from jax.sharding import PartitionSpec as P

HEAD_DIM = 64
LANES = 2 * HEAD_DIM
EPSILON = 1e-05
MASKED = -1e30
BF = jnp.bfloat16
F32 = jnp.float32
MIB = 1024 * 1024
DENSE_MIB = 60
STRIP = 16
CODES = 16
SHARDS = 16


def move(value, pairs):
    return lax.ppermute(value, "dp", pairs)


def device_at(spot, core, depth):
    return 4 * spot + core if spot < depth else 4 * (2 * depth - 1 - spot) + 2 + core


def routes(n):
    depth = n // 4
    ring = 2 * depth

    def turned(by):
        return [
            (device_at(r, c, depth), device_at((r + by) % ring, c, depth))
            for r in range(ring) for c in range(2)
        ]

    return turned(1), turned(-1), [(i, i ^ 1) for i in range(n)]


def hops(depth, far):
    return (depth, depth - 1) if far == 0 else (depth - 1, depth)


def after(value, token):
    return lax.optimization_barrier((value, token))[0]


def sliced(n):
    return n == 16


FAR = (0, 1, 0)


def first_ways(depth, far):
    return (depth, 1 - depth) if far == 0 else (-depth, depth - 1)


def lots(depth, far):
    ahead, behind = hops(depth, far)
    early = [0] + [sign * d for d in range(1, depth // 2 + 1) for sign in (1, -1)]
    late = [d for d in range(-behind, ahead + 1) if d not in early]
    return early, late


def gather_halves(halves, n, token):
    depth = n // 4
    forward, backward, beside = routes(n)
    held = [{0: half} for half in halves]
    for s in range(1, depth + 1):
        for far, mine in enumerate(held):
            ahead, behind = hops(depth, far)
            for sign, limit, way in ((1, ahead, forward), (-1, behind, backward)):
                if s <= limit:
                    source = mine[sign * (s - 1)]
                    mine[sign * s] = move(after(source, token) if s == 2 else source, way)
    found = []
    for far, mine in enumerate(held):
        early, late = lots(depth, far)
        found += [mine[d] for d in early + late]
        found += [move(jnp.stack([mine[d] for d in some]), beside) for some in (early, late)]
    return found


EXTRA = 16


class Sum:
    def __init__(self, own, other, n, far, spot, soon):
        self.depth = n // 4
        forward, backward, beside = routes(n)
        self.ways = (forward, backward) if far == 0 else (backward, forward)
        self.far, self.spot = far, spot
        self.own, self.soon = own, soon
        self.got = move(other, beside)
        self.came = [None, None]
        self.arrived = {}

    def block(self, held, distance):
        at = lax.rem(self.spot + (2 * self.depth + distance), 2 * self.depth)
        return lax.dynamic_index_in_dim(held, at, 0, keepdims=False)

    def term(self, distance, came, got=None):
        found = self.block(self.own, distance).astype(F32)
        found = found + (self.block(self.got, distance) if got is None else got).astype(F32)
        for value in came:
            if value is not None:
                found = found + value.astype(F32)
        return found

    def step(self, s):
        signs = [1 if self.far == i else -1 for i in range(2) if s + i < self.depth]
        values = [
            self.term(sign * (self.depth - s - i), [self.came[i]], self.soon[i] if s == 0 and self.soon is not None else None)
            for i, sign in enumerate(signs)]
        values = lax.optimization_barrier([value.astype(BF) for value in values])
        for i, (sign, value) in enumerate(zip(signs, values)):
            self.came[i] = self.arrived[-sign * (s + 1)] = move(value, self.ways[i])

    def total(self, token=None):
        last = self.came[0] if token is None else after(self.came[0], token)
        return lax.optimization_barrier(self.term(0, [self.came[1]])), last.astype(F32)


def scatter_plain(whole):
    return lax.psum_scatter(whole.astype(F32), "dp", scatter_dimension=0, tiled=False)


def dot(a, b):
    return jnp.dot(a, b, preferred_element_type=F32)


def dot_t(a, b):
    return lax.dot_general(a, b, (((1,), (1,)), ((), ())), preferred_element_type=F32)


def t_dot(a, b):
    return lax.dot_general(a, b, (((0,), (0,)), ((), ())), preferred_element_type=F32)


def spot_of(me, depth):
    return jnp.where((me // 2) % 2 == 0, me // 4, 2 * depth - 1 - me // 4)


def device_on(me, distance, core, depth):
    spot = lax.rem(spot_of(me, depth) + (2 * depth + distance), 2 * depth)
    base = jnp.where(spot < depth, 4 * spot, 4 * (2 * depth - 1 - spot) + 2)
    return base + ((me % 2) ^ core)


def fetch_start(refs, holds, sems, me, names):
    if len(refs) == 3:
        for i in names:
            pltpu.make_async_copy(refs[i], holds[i], sems.at[i]).start()
        return
    count = len(refs) // 2
    depth = (count - 2) // 2
    rows = holds[0].shape[1]
    cuts = ((0, 0, 0, 0, rows), (0, 1, rows, 0, rows // 2), (1, 1, 0, rows // 2, rows // 2), (1, 2, rows // 2, 0, rows))
    for i in names:
        for far, name, source, target, size in cuts:
            if name == i:
                mine = refs[far * count:(far + 1) * count]
                early, late = lots(depth, far)
                there = pl.ds(source, size)
                pieces = [(d, 0, ref.at[there]) for d, ref in zip(early + late, mine)]
                pieces += [(d, 1, mine[-2].at[k, there]) for k, d in enumerate(early)]
                pieces += [(d, 1, mine[-1].at[k, there]) for k, d in enumerate(late)]
                for distance, core, piece in pieces:
                    origin = device_on(me, -distance, core, depth)
                    pltpu.make_async_copy(piece, holds[i].at[origin, pl.ds(target, size)], sems.at[i]).start()


def ready(hold, sem):
    pltpu.make_async_copy(hold, hold, sem).wait()


def matrix(hold, q):
    shards, _, width = hold.shape
    count = width // shards
    return hold[:, q * count:(q + 1) * count, :].reshape(width, width)


def band(hold, b):
    shards, count, width = hold.shape
    some = width // count
    return hold[b * some:(b + 1) * some].reshape(width, width)


def deal(value, outs, me, first, piece):
    rows = piece.stop - piece.start
    number = value.shape[0] // rows
    if len(outs) == 1:
        outs[0][first:first + number, piece, :] = value.reshape(number, rows, value.shape[1]).astype(BF)
        return
    own, other = outs
    ring = own.shape[0]
    for t in range(number // 2):
        even, odd = value[2 * t * rows:(2 * t + 1) * rows], value[(2 * t + 1) * rows:(2 * t + 2) * rows]
        z, x = divmod(first // 2 + t, 2)
        spot = z if x == 0 else ring - 1 - z
        own[spot, piece, :] = jnp.where(me % 2 == 0, even, odd).astype(BF)
        other[spot, piece, :] = jnp.where(me % 2 == 0, odd, even).astype(BF)


def split(line):
    high = line.astype(BF).astype(F32)
    middle = (line - high).astype(BF).astype(F32)
    return [high, middle, line - high - middle]


def deal_lines(lines, outs, small):
    value = jnp.concatenate(lines + [jnp.zeros((EXTRA - len(lines), lines[0].shape[1]), F32)], axis=0)
    small[...] = value
    if len(outs) == 2:
        for out in outs:
            for spot in range(out.shape[0]):
                out[spot, out.shape[1] - EXTRA:, :] = value.astype(BF)


def deal_router(line, outs, small, me):
    three = split(line)
    none = jnp.zeros_like(line)
    mine, other = three + [none] * (EXTRA - 3), [none] * 3 + three + [none] * (EXTRA - 6)
    small[...] = jnp.concatenate(mine, axis=0)
    if len(outs) == 2:
        ring, row = outs[0].shape[0], outs[0].shape[1] - EXTRA
        for out, value in zip(outs, (mine, other)):
            value = jnp.concatenate(value, axis=0).astype(BF)
            for spot in range(ring):
                out[spot, row:, :] = jnp.zeros(value.shape, BF)
            for distance in first_ways(ring // 2, FAR[2]):
                out[lax.rem(spot_of(me, ring // 2) + ring + distance, ring), row:, :] = value


def router_kernel(count, place, *refs):
    own, got, arrived, (out, lines, sems) = refs[0], refs[1], refs[2:count + 2], refs[count + 2:]
    me = place[0]
    ring = count + 1
    depth = ring // 2
    spot = spot_of(me, depth)
    row = own.shape[1] - EXTRA
    away = lax.rem(spot + ring + first_ways(depth, FAR[2])[0], ring)
    copies = [pltpu.make_async_copy(own.at[away, pl.ds(row, EXTRA)], lines.at[0], sems.at[0]),
              pltpu.make_async_copy(got.at[0, pl.ds(row, EXTRA)], lines.at[1], sems.at[1])]
    ahead, behind = hops(depth, FAR[2])
    distances = list(range(-ahead, 0)) + list(range(1, behind + 1))
    for i, (distance, ref) in enumerate(zip(distances, arrived)):
        slot = 2 + lax.rem(spot + ring + distance, ring)
        copies.append(pltpu.make_async_copy(ref.at[pl.ds(row, EXTRA)], lines.at[slot], sems.at[2 + i]))
    for copy in copies:
        copy.start()
    for copy in copies:
        copy.wait()
    lines[2 + spot] = lines[0] + lines[1]
    total = jnp.zeros(out.shape, F32)
    for r in range(ring):
        value = lines[2 + r].astype(F32)
        low = (value[0:1] + value[1:2]) + value[2:3]
        high = (value[3:4] + value[4:5]) + value[5:6]
        total = total + jnp.where(me % 2 == 0, low, high)
        total = total + jnp.where(me % 2 == 0, high, low)
    out[...] = total


def copy_soon(outs, soon, me):
    if len(outs) == 2:
        ring = outs[1].shape[0]
        for i, distance in enumerate(first_ways(ring // 2, FAR[2])):
            soon[i] = outs[1][lax.rem(spot_of(me, ring // 2) + ring + distance, ring)]


def deal_matrix(value, outs, me, q):
    count = value.shape[0] // SHARDS
    deal(value, outs, me, 0, slice(q * count, (q + 1) * count))


def deal_down(hidden, d_out, outs, me):
    width = d_out.shape[1]
    count = hidden.shape[1] // SHARDS
    for b in range(hidden.shape[1] // width):
        value = t_dot(hidden[:, b * width:(b + 1) * width], d_out)
        deal(value, outs, me, b * (width // count), slice(0, count))


def inverse_of(rows):
    return lax.rsqrt(jnp.mean(rows * rows, axis=-1, keepdims=True) + EPSILON)


def norm_back(upstream, normed, inverse, gain):
    scaled = upstream * gain
    d_gain = jnp.sum(upstream * normed, axis=0, keepdims=True)
    d_rows = inverse * (scaled - normed * jnp.mean(scaled * normed, axis=-1, keepdims=True))
    return d_rows, d_gain


def normal_parts(value):
    whole = 0.5 + 0.5 * lax.erf(value * 0.7071067811865476)
    return whole, value * jnp.exp(value * value * -0.5) * 0.3989422804014327


def left_lanes(rows):
    return lax.broadcasted_iota(jnp.int32, (rows, LANES), 1) < HEAD_DIM


def two_heads(value):
    left = left_lanes(value.shape[0])
    zero = jnp.zeros_like(value)
    return jnp.concatenate([jnp.where(left, value, zero), jnp.where(left, zero, value)], axis=0)


def one_row(value):
    half = value.shape[0] // 2
    return jnp.where(left_lanes(half), value[:half], value[half:])


def bias_of(same):
    shape = same.shape
    order = lax.broadcasted_iota(jnp.int32, shape, 0) >= lax.broadcasted_iota(jnp.int32, shape, 1)
    return jnp.where(order & (same > 0.5), 0.0, MASKED).astype(F32)


def hot_rows(line, count):
    return (lax.broadcasted_iota(jnp.int32, (count, line.shape[1]), 0) == line).astype(BF)


def attend(groups, biases):
    size = groups[0][0].shape[0]
    scale = jnp.asarray(HEAD_DIM ** -0.5, BF)
    scores = [dot_t(two_heads(query) * scale, keyed) for query, keyed, _ in groups]
    found = []
    for value, bias in zip(scores, biases):
        value = (value.reshape(2, size, size) + bias[None]).reshape(2 * size, size)
        powers = jnp.exp(value - jnp.max(value, axis=-1, keepdims=True))
        found.append((powers * (1.0 / jnp.sum(powers, axis=-1, keepdims=True))).astype(BF))
    mixed = [one_row(dot(chances, valued)).astype(BF) for chances, (_, _, valued) in zip(found, groups)]
    return mixed, found


def attend_back(groups, mixed, chances, d_mixed):
    both = [two_heads(value) for value in d_mixed]
    d_chances = [dot_t(value, valued) for value, (_, _, valued) in zip(both, groups)]
    d_value = [t_dot(chance, value) for chance, value in zip(chances, both)]
    factor = HEAD_DIM ** -0.5
    d_scores = []
    for found, value, blend, chance in zip(d_chances, d_mixed, mixed, chances):
        overlap = jnp.sum(two_heads(value.astype(F32) * blend.astype(F32)), axis=-1, keepdims=True)
        d_scores.append((chance.astype(F32) * (found - overlap)).astype(BF))
    d_query = [one_row(dot(value, keyed)) * factor for value, (_, keyed, _) in zip(d_scores, groups)]
    d_key = [t_dot(value, two_heads(query)) * factor for value, (query, _, _) in zip(d_scores, groups)]
    return [[one.astype(BF) for one in some] for some in (d_query, d_key, d_value)]


def pairs_of(value):
    return [value[:, p:p + LANES] for p in range(0, value.shape[1], LANES)]


def lanes_of(p):
    return pl.ds(pl.multiple_of(p * LANES, LANES), LANES)


def routed_kernel(slot_count, batch, place, *refs):
    shards = refs[:slot_count]
    (tokens, spots, codes, router, gains,
     rows_o, gate_o, z_o, act_one_o, heads_o, chances_o, mixed_o, act_two_o, hidden_o, slope_o, branch_o, delta_o,
     w_first, w_up, w_down, sems) = refs[slot_count:]
    fetch_start(shards, (w_first, w_up, w_down), sems, place[0], (0, 1, 2))
    hot = hot_rows(spots[...], tokens.shape[0])
    rows = t_dot(hot, tokens[...])
    rows_o[...] = rows
    gate = jax.nn.sigmoid(jnp.sum(rows * router[...], axis=-1, keepdims=True))
    gate_o[...] = gate
    act = (rows * inverse_of(rows) * gains[0:1]).astype(BF)
    act_one_o[...] = act
    member = dot(hot_rows(codes[...], CODES * batch), hot).astype(BF)
    bias = bias_of(t_dot(member, member))
    ready(w_first, sems.at[0])
    heads = [dot(act, matrix(w_first, c)).astype(BF) for c in range(3)]
    for c in range(3):
        heads_o[c] = heads[c]
    groups = list(zip(*(pairs_of(value) for value in heads)))
    found, chances = attend(groups, [bias] * len(groups))
    for p, chance in enumerate(chances):
        chances_o[p] = chance.astype(F32)
    mixed = jnp.concatenate(found, axis=1)
    mixed_o[...] = mixed
    z = dot(mixed, matrix(w_first, 3))
    z_o[...] = z
    middle = rows + z
    act_two = (middle * inverse_of(middle) * gains[1:2]).astype(BF)
    act_two_o[...] = act_two
    ready(w_up, sems.at[1])
    ready(w_down, sems.at[2])
    width = rows.shape[1]
    for b in range(hidden_o.shape[1] // width):
        lanes = slice(b * width, (b + 1) * width)
        upped = dot(act_two, matrix(w_up, b))
        whole, dense = normal_parts(upped)
        hidden_o[:, lanes] = (upped * whole).astype(BF)
        slope_o[:, lanes] = whole + dense
    branch = z_o[...] + dot(hidden_o[...], w_down[...].reshape(hidden_o.shape[1], width))
    branch_o[...] = branch
    delta_o[...] = (gate * branch).astype(BF)


def routed_back_kernel(slot_count, out_count, place, *refs):
    shards = refs[:slot_count]
    (d_delta, gate, branch, rows, z, hidden, act_two, slope, act_one, heads, chances, mixed, router, gains) = refs[
        slot_count:slot_count + 14]
    refs = refs[slot_count + 14:]
    downs_o, ups_o, firsts_o = (refs[i * out_count:(i + 1) * out_count] for i in range(3))
    soon_o, router_o, small_o, d_picked_o, w_first, w_up, w_down, sems = refs[3 * out_count:]
    me = place[0]
    fetch_start(shards, (w_first, w_up, w_down), sems, me, (2, 1, 0))
    width = rows.shape[1]
    blocks = slope.shape[1] // width
    held = rows[...]
    gated = gate[...]
    upstream = d_delta[...].astype(F32)
    gradient = gated * upstream
    d_out = gradient.astype(BF)
    deal_down(hidden, d_out, downs_o, me)
    d_logit = jnp.sum(upstream * branch[...], axis=-1, keepdims=True) * gated * (1.0 - gated)
    deal_router(jnp.sum(d_logit * held, axis=0, keepdims=True), downs_o, router_o, me)
    copy_soon(downs_o, soon_o, me)
    ready(w_down, sems.at[2])
    d_upped = []
    for b in range(blocks):
        d_hidden = dot_t(d_out, band(w_down, b))
        d_upped.append((d_hidden * slope[:, b * width:(b + 1) * width]).astype(BF))
    ready(w_up, sems.at[1])
    d_act = jnp.zeros(rows.shape, F32)
    for b in range(blocks):
        d_act = d_act + dot_t(d_upped[b], matrix(w_up, b))
    middle = held + z[...]
    inverse = inverse_of(middle)
    d_middle, g_two = norm_back(d_act, middle * inverse, inverse, gains[1:2])
    d_z = (gradient + d_middle).astype(BF)
    ready(w_first, sems.at[0])
    d_mixed = dot_t(d_z, matrix(w_first, 3)).astype(BF)
    for b in range(blocks):
        deal_matrix(t_dot(act_two[...], d_upped[b]), ups_o, me, b)
    blend = mixed[...]
    groups = list(zip(*(pairs_of(heads[c]) for c in range(3))))
    found = attend_back(
        groups, pairs_of(blend), [chances[p].astype(BF) for p in range(len(groups))], pairs_of(d_mixed))
    deal_matrix(t_dot(blend, d_z), firsts_o, me, 3)
    d_heads = [jnp.concatenate(one, axis=1) for one in found]
    d_act = jnp.zeros(rows.shape, F32)
    for c in range(3):
        d_act = d_act + dot_t(d_heads[c], matrix(w_first, c))
    for c in range(3):
        deal_matrix(t_dot(act_one[...], d_heads[c]), firsts_o, me, c)
    inverse = inverse_of(held)
    d_rows, g_one = norm_back(d_act, held * inverse, inverse, gains[0:1])
    d_picked_o[...] = d_rows + d_middle + d_logit * router[...]
    deal_lines([g_one, g_two], ups_o, small_o)


def dense_kernel(slot_count, place, *refs):
    shards = refs[:slot_count]
    (tokens, cotangent, delta, spots, segments, gains,
     result_o, back_o, picked_o, gain_o,
     act_one_o, d_heads_o, mixed_o, d_z_o, act_two_o, hidden_o, d_upped_o,
     w_first, w_up, w_down, rows, z, heads, chances, bias, fed, d_act, upped, d_hidden, d_mixed,
     act_one, d_heads, mixed, d_z, act_two, hidden, d_upped, sems, out_sems) = refs[slot_count:]
    holds = (w_first, w_up, w_down)
    fetch_start(shards, holds, sems, place[0], (0,))
    batch, length, _ = bias.shape
    width = tokens.shape[1]
    pairs = width // LANES
    blocks = hidden.shape[1] // width
    parts = [slice(s * length, (s + 1) * length) for s in range(batch)]
    copies = [
        pltpu.make_async_copy(held, out, out_sems.at[i])
        for i, (held, out) in enumerate((
            (act_one, act_one_o), (d_heads, d_heads_o), (mixed, mixed_o), (d_z, d_z_o),
            (act_two, act_two_o), (hidden, hidden_o), (d_upped, d_upped_o),
        ))
    ]

    hot = hot_rows(spots[...], tokens.shape[0])
    for s, part in enumerate(parts):
        held = tokens[part].astype(F32) + dot(hot[part], delta[...])
        rows[part] = held
        act_one[part] = (held * inverse_of(held) * gains[0:1]).astype(BF)
        member = hot_rows(segments[:, part], CODES)
        bias[s] = bias_of(t_dot(member, member))
    copies[0].start()
    ready(w_first, sems.at[0])
    for c in range(3):
        for part in parts:
            heads[c, part] = dot(act_one[part], matrix(w_first, c)).astype(BF)
    fetch_start(shards, holds, sems, place[0], (1, 2))

    def forward(p, carry):
        lanes = lanes_of(p)
        groups = [tuple(heads[c, part, lanes] for c in range(3)) for part in parts]
        blends, found = attend(groups, [bias[s] for s in range(batch)])
        for s, part in enumerate(parts):
            mixed[part, lanes] = blends[s]
            chances[s, p] = found[s]
        return carry

    lax.fori_loop(0, pairs, forward, 0)
    copies[2].start()
    for part in parts:
        attended = dot(mixed[part], matrix(w_first, 3))
        z[part] = attended
        middle = rows[part] + attended
        act_two[part] = (middle * inverse_of(middle) * gains[1:2]).astype(BF)
    copies[4].start()
    ready(w_up, sems.at[1])
    ready(w_down, sems.at[2])
    fed[...] = jnp.zeros(fed.shape, F32)
    d_act[...] = jnp.zeros(d_act.shape, F32)

    for b in range(blocks):
        lanes = slice(b * width, (b + 1) * width)
        for s, part in enumerate(parts):
            upped[...] = dot(act_two[part], matrix(w_up, b))
            d_hidden[...] = dot_t(cotangent[part], band(w_down, b))

            for r in range(length // STRIP):
                spot = slice(r * STRIP, (r + 1) * STRIP)
                there = slice(s * length + r * STRIP, s * length + (r + 1) * STRIP)
                for side in range(2):
                    cut = slice(side * width // 2, (side + 1) * width // 2)
                    out = slice(b * width + side * width // 2, b * width + (side + 1) * width // 2)
                    value = upped[spot, cut]
                    whole, dense = normal_parts(value)
                    hidden[there, out] = (value * whole).astype(BF)
                    d_upped[there, out] = (d_hidden[spot, cut] * (whole + dense)).astype(BF)
            fed[part] += dot(hidden[part, lanes], band(w_down, b))
            d_act[part] += dot_t(d_upped[part, lanes], matrix(w_up, b))
    copies[5].start()
    copies[6].start()
    gain = jnp.zeros((1, width), F32)
    for part in parts:
        result_o[part] = (rows[part] + z[part] + fed[part]).astype(BF)
        middle = rows[part] + z[part]
        inverse = inverse_of(middle)
        d_middle, more = norm_back(d_act[part], middle * inverse, inverse, gains[1:2])
        gain = gain + more
        held = cotangent[part].astype(F32) + d_middle
        d_act[part] = held
        d_z[part] = held.astype(BF)
        d_mixed[part] = dot_t(held.astype(BF), matrix(w_first, 3)).astype(BF)
    gain_o[1:2] = gain
    copies[3].start()

    def backward(p, carry):
        lanes = lanes_of(p)
        groups = [tuple(heads[c, part, lanes] for c in range(3)) for part in parts]
        found = attend_back(
            groups, [mixed[part, lanes] for part in parts], [chances[s, p] for s in range(batch)],
            [d_mixed[part, lanes] for part in parts])
        for c in range(3):
            for s, part in enumerate(parts):
                d_heads[c, part, lanes] = found[c][s]
        return carry

    lax.fori_loop(0, pairs, backward, 0)
    copies[1].start()
    gain = jnp.zeros((1, width), F32)
    for s, part in enumerate(parts):
        d_first = dot_t(d_heads[0, part], matrix(w_first, 0))
        d_first = d_first + dot_t(d_heads[1, part], matrix(w_first, 1))
        d_first = d_first + dot_t(d_heads[2, part], matrix(w_first, 2))
        held = rows[part]
        inverse = inverse_of(held)
        d_rows, more = norm_back(d_first, held * inverse, inverse, gains[0:1])
        gain = gain + more
        back_o[part] = (d_act[part] + d_rows).astype(BF)
    picked_o[...] = t_dot(hot, back_o[...]).astype(BF)
    gain_o[0:1] = gain
    for copy in copies:
        copy.wait()


def dense_back_kernel(out_count, place, hidden, d_out, act_two, d_upped, mixed, d_z, act_one, d_heads, gains, *refs):
    downs_o, ups_o, firsts_o = (refs[i * out_count:(i + 1) * out_count] for i in range(3))
    soon_o, router_o, small_o, d_picked_o = refs[3 * out_count:]
    me = place[0]
    deal_down(hidden, d_out[...], downs_o, me)
    deal_router(jnp.zeros((1, d_out.shape[1]), F32), downs_o, router_o, me)
    copy_soon(downs_o, soon_o, me)
    d_picked_o[...] = jnp.zeros(d_picked_o.shape, F32)
    width = act_two.shape[1]
    for b in range(d_upped.shape[1] // width):
        deal_matrix(t_dot(act_two[...], d_upped[:, b * width:(b + 1) * width]), ups_o, me, b)
    deal_matrix(t_dot(mixed[...], d_z[...]), firsts_o, me, 3)
    for c in range(3):
        deal_matrix(t_dot(act_one[...], d_heads[c]), firsts_o, me, c)
    deal_lines([gains[0:1], gains[1:2]], ups_o, small_o)


def call(kernel, inputs, anywhere, outs, scratch, flops, mib, anywhere_outs=0):
    vmem = pl.BlockSpec(memory_space=pltpu.VMEM)
    hbm = pl.BlockSpec(memory_space=pltpu.HBM)
    specs = [pl.BlockSpec(memory_space=pltpu.SMEM)] + [hbm] * anywhere
    specs = specs + [vmem] * (len(inputs) - len(specs))
    moved = sum(v.size * v.dtype.itemsize for v in inputs) + sum(
        o.size * jnp.dtype(o.dtype).itemsize for o in outs)
    return tuple(pl.pallas_call(
        kernel,
        out_shape=outs,
        in_specs=specs,
        out_specs=[vmem] * (len(outs) - anywhere_outs) + [hbm] * anywhere_outs,
        scratch_shapes=scratch,
        compiler_params=pltpu.CompilerParams(vmem_limit_bytes=mib * MIB),
        cost_estimate=pl.CostEstimate(flops=flops, bytes_accessed=moved, transcendentals=0),
    )(*inputs))


def body(
    tokens, cotangent, segments, chosen, router, norm_gains, attn_in, attn_out, ff_up, ff_down
):
    n = lax.axis_size("dp")
    routed = lax.axis_index("section") == 0
    place = lax.axis_index("dp").astype(jnp.int32).reshape(1)
    batch, length = segments.shape
    width = tokens.shape[1]
    kept = chosen.shape[1]
    rows_in, rows_down, ff = attn_in.shape[2], ff_down.shape[1], ff_up.shape[2]
    blocks, pairs = ff // width, width // LANES
    picked, count = batch * kept, batch * length
    gains = norm_gains[0]
    router_row = router[None]

    def shape(*dims, dtype=F32):
        return jax.ShapeDtypeStruct(dims, dtype)

    def hold(*dims, dtype=F32):
        return pltpu.VMEM(dims, dtype)

    first_part = jnp.concatenate([attn_in[0].reshape(-1, width), attn_out[0]])
    up_part = jnp.concatenate([ff_up[0][:, b * width:(b + 1) * width] for b in range(blocks)])
    parts = [first_part, up_part, ff_down[0]]
    part_rows = 4 * width // SHARDS
    order = lax.iota(jnp.int32, batch)[:, None]
    spots = (chosen + order * length).reshape(1, picked)
    lines = segments.reshape(1, count)
    codes = (segments + order * CODES).reshape(1, count)
    if sliced(n):
        half = part_rows // 2
        halves = [jnp.concatenate([first_part, up_part[:half]]), jnp.concatenate([up_part[half:], ff_down[0]])]
        shards = gather_halves(halves, n, (spots, lines, codes))
        outs, wide_outs = (
            [shape(n // 2, part_rows + more, width, dtype=BF)] * 2 for more in (0, EXTRA))
    else:
        first, up, down = (lax.all_gather(part, "dp", axis=0) for part in parts)

        def dealt(value):
            value = value.reshape(n, 4, rows_in, width).transpose(1, 0, 2, 3)
            value = value.reshape(4, SHARDS, width // SHARDS, width).transpose(1, 0, 2, 3)
            return value.reshape(SHARDS, part_rows, width)

        shards = [dealt(first), dealt(up), down.reshape(SHARDS, part_rows, width)]
        outs = wide_outs = [shape(SHARDS, part_rows, width, dtype=BF)]
    number, out_number = len(shards), len(outs)
    w_first = w_up = w_down = hold(SHARDS, part_rows, width, dtype=BF)

    (rows, gate, z, act_one, heads, chances, mixed, act_two, hidden, slope, branch, delta) = call(
        functools.partial(routed_kernel, number, batch),
        [place, *shards, tokens, spots, codes, router_row, gains],
        number,
        [shape(picked, width), shape(picked, 1), shape(picked, width), shape(picked, width, dtype=BF),
         shape(3, picked, width, dtype=BF), shape(pairs, 2 * picked, picked),
         shape(picked, width, dtype=BF), shape(picked, width, dtype=BF), shape(picked, ff, dtype=BF),
         shape(picked, ff), shape(picked, width), shape(picked, width, dtype=BF)],
        [w_first, w_up, w_down, pltpu.SemaphoreType.DMA((3,))],
        4 * picked * width * (2 * width + ff),
        28,
    )
    arrived = lax.ppermute(delta, "section", [(0, 1)])

    (result, back, back_rows, dense_gains, *dense_kept) = call(
        functools.partial(dense_kernel, number),
        [place, *shards, tokens, cotangent, arrived, spots, lines, gains],
        number,
        [shape(count, width, dtype=BF), shape(count, width, dtype=BF), shape(picked, width, dtype=BF),
         shape(2, width),
         shape(count, width, dtype=BF), shape(3, count, width, dtype=BF), shape(count, width, dtype=BF),
         shape(count, width, dtype=BF), shape(count, width, dtype=BF), shape(count, ff, dtype=BF),
         shape(count, ff, dtype=BF)],
        [w_first, w_up, w_down, hold(count, width), hold(count, width), hold(3, count, width, dtype=BF),
         hold(batch, pairs, 2 * length, length, dtype=BF), hold(batch, length, length),
         hold(count, width), hold(count, width), hold(length, width), hold(length, width),
         hold(count, width, dtype=BF),
         hold(count, width, dtype=BF), hold(3, count, width, dtype=BF), hold(count, width, dtype=BF),
         hold(count, width, dtype=BF), hold(count, width, dtype=BF), hold(count, ff, dtype=BF),
         hold(count, ff, dtype=BF),
         pltpu.SemaphoreType.DMA((3,)), pltpu.SemaphoreType.DMA((7,))],
        4 * count * width * (4 * width + 2 * ff),
        DENSE_MIB,
        anywhere_outs=7,
    )
    dense_act_one, dense_d_heads, dense_mixed, dense_d_z, dense_act_two, dense_hidden, dense_d_upped = dense_kept
    d_delta = lax.ppermute(back_rows, "section", [(1, 0)])
    returned = lax.ppermute(after(back, d_delta), "section", [(1, 0)])

    back_outs = [
        *wide_outs, *wide_outs, *outs, shape(2, part_rows + EXTRA, width, dtype=BF), shape(EXTRA, width),
        shape(EXTRA, width), shape(picked, width)]

    def routed_back():
        return call(
            functools.partial(routed_back_kernel, number, out_number),
            [place, *shards, d_delta, gate, branch, rows, z, hidden, act_two, slope, act_one, heads, chances,
             mixed, router_row, gains],
            number,
            back_outs,
            [w_first, w_up, w_down, pltpu.SemaphoreType.DMA((3,))],
            8 * picked * width * ff + 16 * picked * width * width,
            44,
        )

    def dense_back():
        return call(
            functools.partial(dense_back_kernel, out_number),
            [place, dense_hidden, cotangent, dense_act_two, dense_d_upped, dense_mixed, dense_d_z, dense_act_one,
             dense_d_heads, dense_gains],
            0, back_outs, [], 4 * count * width * ff + 8 * count * width * width, 44,
        )

    (*pieces, router_lines, small, d_picked) = lax.cond(routed, routed_back, dense_back)
    up_pieces, first_pieces = pieces[:out_number], pieces[out_number:]
    picks = (chosen[:, :, None] == lax.iota(jnp.int32, length)[None, None, :]).astype(F32)

    def both_ends(returned, result):
        spread = jnp.einsum(
            "wgo,wgq->woq", picks, d_picked.reshape(batch, kept, width), precision=lax.Precision.HIGHEST)
        first_rows = (returned.astype(F32) + spread.reshape(count, width)).astype(BF)
        return jnp.where(routed, first_rows, result)[None]

    if sliced(n):
        pieces, returned = lax.optimization_barrier((pieces, returned))
        spot = spot_of(place[0], n // 4)
        soon = move(pieces[6], routes(n)[2])
        pieces = after(pieces[:6], soon)
        down_sum, up_sum, first_sum = sums = [
            Sum(*pieces[i:i + 2], n, far, spot, early) for i, far, early in (
                (0, FAR[2], soon), (2, FAR[1], None), (4, FAR[0], None))]
        for s in range(n // 4):
            for one in sums:
                one.step(s)
            if s == 0:
                d_picked = after(d_picked, first_sum.came[0])
        arrived = [down_sum.arrived[d] for d in sorted(down_sum.arrived)]
        router_grad = call(
            functools.partial(router_kernel, len(arrived)),
            [place, down_sum.own, down_sum.soon, *arrived], len(arrived) + 2, [shape(1, width)],
            [hold(n // 2 + 2, EXTRA, width, dtype=BF), pltpu.SemaphoreType.DMA((n // 2 + 2,))], width, 2,
        )[0][0]
        router_grad = router_grad + lax.ppermute(router_grad, "section", [(0, 1), (1, 0)])
        ends = both_ends(returned, result)
        down_grad = sum(down_sum.total())[:part_rows]
        up_due, up_last = up_sum.total()
        up_grad = jnp.concatenate([
            up_due[b * rows_in:(b + 1) * rows_in] + up_last[b * rows_in:(b + 1) * rows_in] for b in range(blocks)
        ], axis=1)
        small = up_due[part_rows:] + up_last[part_rows:]
        due, last = first_sum.total((router_grad, ends, down_grad, up_grad))
        in_grad, out_grad = (due[rows] + last[rows] for rows in (slice(0, 3 * rows_in), slice(3 * rows_in, None)))
    else:
        def plain(pieces, wide):
            whole = pieces[0]
            if wide:
                whole = whole.reshape(SHARDS, 4, -1, width).transpose(1, 0, 2, 3)
                whole = whole.reshape(4, n, -1, width).transpose(1, 0, 2, 3)
            return scatter_plain(whole.reshape(n, -1, width))

        down_grad = plain(pieces[:1], False)
        up_grad, first_grad = plain(pieces[1:2], True), plain(pieces[2:3], True)
        up_grad = up_grad.reshape(blocks, rows_in, width).transpose(1, 0, 2).reshape(rows_in, ff)
        in_grad, out_grad = first_grad[:3 * rows_in], first_grad[3 * rows_in:]
        small = lax.psum(small, "dp")
        ends = both_ends(returned, result)
        router_grad = jnp.sum(lax.psum(router_lines, ("section", "dp")), axis=0)
    gain_grad = lax.dynamic_slice_in_dim(small[:2], place[0] * (width // n), width // n, 1)
    return (
        ends, router_grad, gain_grad[None], in_grad.reshape(1, 3, rows_in, width), out_grad[None],
        up_grad[None], down_grad[None],
    )


def solution(mesh):
    return jax.shard_map(
        body,
        mesh=mesh,
        in_specs=(
            P("dp", None),
            P("dp", None),
            P("dp", None),
            P("dp", None),
            P(),
            P("section", None, None),
            P("section", None, "dp", None),
            P("section", "dp", None),
            P("section", "dp", None),
            P("section", "dp", None),
        ),
        out_specs=(
            P("section", "dp", None),
            P(),
            P("section", None, "dp"),
            P("section", None, "dp", None),
            P("section", "dp", None),
            P("section", "dp", None),
            P("section", "dp", None),
        ),
        check_vma=False,
    )
```
